128 devices in a mesh: gx: 16 (over x, z), gy: 8 (over y, core).
Axes of the slice: x: 4, y: 4, z: 4, core: 2. Of those that a mesh axis runs over, the one named last changes fastest.
Arguments:
- layer_slowness: float32 [8], replicated, may hold values from 0.5 to 2
- layer_rigidity: float32 [8], replicated, may hold values from 0.5 to 4
- layer_damping: float32 [8], replicated, may hold values from 0.02 to 0.2
- layer_of_level: int32 [32], replicated, may hold values from 0 to 7
- slot_offset: int32 [32768], replicated, may hold values from 0 to 2047
- slot_level: int32 [32768], replicated, may hold values from 0 to 31
- slot_target: int32 [32768], P(('gx', 'gy')), may hold values from 0 to 786431
- live_count: int32 [128], P(('gx', 'gy')), may hold values from 1 to 256, 16384 in all
- moduli: float32 [2, 512, 256, 256], P(None, 'gx', 'gy'), may hold values from 0.02 to 0.06
- field_old: float32 [3, 512, 256, 256], P(None, 'gx', 'gy'), may hold values from -0.3 to 0.3
- field_now: float32 [3, 512, 256, 256], P(None, 'gx', 'gy'), may hold values from -0.3 to 0.3
Outputs:
- final_field: float32 [3, 512, 256, 256], P(None, 'gx', 'gy')
- prior_field: float32 [3, 512, 256, 256], P(None, 'gx', 'gy')
The draws below stay inside these ranges and needn't reach their ends.
Inputs may be any that keep to these rules, and one draw needn't show every extreme that they name: live_count sums to 32768 // 2 over all owners, and some owner uses all 256 slots.
All inputs are finite; a program needn't handle non-finite values. No bound on the sum of `live_count` on one device may be relied on, other than what follows from the above.
Results may differ from the reference program's by a relative error of at most 0.0036.
Values may be sent and summed in bfloat16 or wider, within the bound.
A program may use at most 128 MiB of HBM per device.

```python
import math
import jax
import jax.numpy as jnp
import numpy as np
from jax import lax

F = 128
NK = 1024
NR = 2048
ND = 32
NL = 8
STEPS = 4
TSTART = 32
Q_DEV = 256
CX = 32
CY = 32
NZ = 256
SLOTS = 32768
NX = 512
NY = 256
N_GX = 16
N_GY = 8


def plant(drawn, rng, least, high):
    place = [jax.random.randint(jax.random.fold_in(rng, axis), (), 0, length) for axis, length in enumerate(drawn.shape)]
    main_axis = drawn.shape.index(max(drawn.shape))
    beside = place[:main_axis] + [(place[main_axis] + 1) % drawn.shape[main_axis]] + place[main_axis + 1:]
    return drawn.at[tuple(place)].set(least).at[tuple(beside)].set(high)


def steps_of(own_key, extent, shards, least, high):
    level = 1.0
    for position, parts in shards:
        draws = jax.random.uniform(jax.random.fold_in(jax.random.fold_in(own_key, 6), position), (parts,), jnp.float32, least / len(shards), high / len(shards))
        level = level * jnp.repeat(jnp.exp(draws), extent[position] // parts).reshape((-1,) + (1,) * (len(extent) - 1 - position))
    return level


def split_up(count, total, bound, lean):
    portions = [(1 << 20) // math.isqrt(rank ** lean) + 1 for rank in range(2, count + 1)]
    rest, holding = total - bound - (count - 1), [1] * (count - 1)
    while rest > 0:
        free = [i for i in range(count - 1) if holding[i] < bound]
        whole, budget = sum([portions[i] for i in free]), rest
        for i in free:
            extra = min(bound - holding[i], max(1, budget * portions[i] // whole), rest)
            holding[i] = holding[i] + extra
            rest = rest - extra
    return np.array([bound] + holding)


def ragged_sizes(rng, count, total, bound, lean):
    if count == 2:
        one = jax.random.randint(rng, (), max(1, total - bound), min(bound, total - 1) + 1)
        return jnp.stack([one, total - one])
    lengths = jnp.asarray(split_up(count, total, bound, lean), jnp.int32)
    couples = (count - 1) // 2
    source_of, taker = lengths[1:1 + 2 * couples:2], lengths[2:2 + 2 * couples:2]
    room = jnp.minimum(source_of - 1, bound - taker)
    moved = jax.random.randint(jax.random.fold_in(rng, 1), (couples,), 0, 1 << 20) % (room + 1)
    lengths = lengths.at[1:1 + 2 * couples:2].set(source_of - moved).at[2:2 + 2 * couples:2].set(taker + moved)
    return lengths[jax.random.permutation(jax.random.fold_in(rng, 2), count)]


def noise(stream_key, dims, scale, most, split=(), held_as=jnp.bfloat16):
    entries = jax.random.normal(stream_key, dims, jnp.float32) * scale
    if len(split) > 0:
        entries = steps_of(stream_key, dims, split, -0.22, 0.18) * entries
    return jnp.clip(entries, min=-most, max=most).astype(held_as)


def setup_inputs(seed: int = 0) -> dict:
    arg_keys = jax.random.split(jax.random.key(seed), 12)
    layer_slowness = jnp.clip(jnp.exp(jax.random.uniform(arg_keys[0], (NL,), jnp.float32, math.log(0.5), math.log(2.0))), 0.5, 2.0)
    layer_rigidity = jnp.clip(jnp.exp(jax.random.uniform(arg_keys[1], (NL,), jnp.float32, math.log(0.5), math.log(4.0))), 0.5, 4.0)
    layer_damping = jnp.clip(jnp.exp(jax.random.uniform(arg_keys[2], (NL,), jnp.float32, math.log(0.02), math.log(0.2))), 0.02, 0.2)
    layer_of_level = plant(jax.random.randint(arg_keys[3], (ND,), 0, NL), jax.random.fold_in(arg_keys[3], 1), 0, NL - 1).astype(jnp.int32)
    slot_offset = plant(jax.random.randint(arg_keys[4], (SLOTS,), 0, NR), jax.random.fold_in(arg_keys[4], 1), 0, NR - 1).astype(jnp.int32)
    slot_level = plant(jax.random.randint(arg_keys[5], (SLOTS,), 0, ND), jax.random.fold_in(arg_keys[5], 1), 0, ND - 1).astype(jnp.int32)
    slot_target = plant(jax.random.randint(arg_keys[6], (SLOTS,), 0, 3 * CX * CY * NZ), jax.random.fold_in(arg_keys[6], 1), 0, (3 * CX * CY * NZ) - 1).astype(jnp.int32)
    live_count = ragged_sizes(arg_keys[7], N_GX * N_GY, SLOTS // 2, Q_DEV, 2).astype(jnp.int32)
    moduli = jnp.clip(0.02 + 0.04 * jax.random.uniform(arg_keys[8], (2, NX, NY, NZ), jnp.float32) ** steps_of(arg_keys[8], (2, NX, NY, NZ), ((1, 16), (2, 8)), -0.2, 0.2), 0.02, 0.06)
    field_old = noise(arg_keys[9], (3, NX, NY, NZ), 0.05, 0.3, ((1, 16), (2, 8)), jnp.float32)
    field_now = noise(arg_keys[10], (3, NX, NY, NZ), 0.05, 0.3, ((1, 16), (2, 8)), jnp.float32)
    return dict(layer_slowness=layer_slowness, layer_rigidity=layer_rigidity, layer_damping=layer_damping, layer_of_level=layer_of_level, slot_offset=slot_offset, slot_level=slot_level, slot_target=slot_target, live_count=live_count, moduli=moduli, field_old=field_old, field_now=field_now)


step_depth = 0.25

def level_table(values, layer_of_level):
    one_hot = (layer_of_level[:, None] == jnp.arange(values.shape[0], dtype=jnp.int32)[None, :]).astype(jnp.float32)
    return lax.optimization_barrier(jnp.sum(one_hot * values[None, :], axis=1))

def wave_kernel(angular, slowness, rigidity, damping, count_k):
    wavenum = (jnp.arange(count_k, dtype=jnp.float32) + 0.5) * (4.0 / count_k)
    spread = angular[None, :, None] * slowness[:, None, None]
    vertical = jnp.sqrt(wavenum[None, None, :] * wavenum[None, None, :] + spread * spread)
    impedance = rigidity[:, None, None] * vertical
    beneath = jnp.concatenate([impedance[1:], impedance[-1:]], axis=0)
    reflect = (impedance - beneath) / (impedance + beneath)
    fading = jnp.exp(-2.0 * step_depth * vertical * damping[:, None, None])
    two_way = 2.0 * step_depth * vertical
    trip_re = fading * jnp.cos(two_way)
    trip_im = -fading * jnp.sin(two_way)

    def upward(state_in, layer_data):
        refl_re, refl_im = state_in
        coefficient, along_re, along_im = layer_data
        upper_re = coefficient + refl_re
        upper_im = refl_im
        lower_re = 1.0 + coefficient * refl_re
        lower_im = coefficient * refl_im
        magnitude = lower_re * lower_re + lower_im * lower_im
        ratio_re = (upper_re * lower_re + upper_im * lower_im) / magnitude
        ratio_im = (upper_im * lower_re - upper_re * lower_im) / magnitude
        fresh_re = along_re * ratio_re - along_im * ratio_im
        fresh_im = along_re * ratio_im + along_im * ratio_re
        return ((fresh_re, fresh_im), (fresh_re, fresh_im))
    bottom = jnp.zeros(vertical.shape[1:], jnp.float32)
    _, (refl_re, refl_im) = lax.scan(upward, (bottom, bottom), (reflect, trip_re, trip_im), reverse=True)
    travel = step_depth * vertical
    phases = jnp.cumsum(travel, axis=0) - travel
    absorbed = travel * damping[:, None, None]
    losses = jnp.cumsum(absorbed, axis=0) - absorbed
    down_size = jnp.exp(-losses)
    down_re = down_size * jnp.cos(phases)
    down_im = -down_size * jnp.sin(phases)
    weight = 1.0 / math.sqrt(count_k)
    kernel_re = weight * (down_re * (1.0 + refl_re) - down_im * refl_im)
    kernel_im = weight * (down_re * refl_im + down_im * (1.0 + refl_re))
    return jnp.transpose(jnp.stack([kernel_re, kernel_im]), (0, 2, 1, 3))

def offset_basis(count_k, count_r):
    modulus = count_k * count_r // 2
    odd_index = 2 * jnp.arange(count_k, dtype=jnp.int32) + 1
    spots = jnp.arange(count_r, dtype=jnp.int32)
    turns = odd_index[:, None] * spots[None, :] % modulus
    return jnp.cos(turns.astype(jnp.float32) * (2.0 * math.pi / modulus)).astype(jnp.bfloat16)

def time_basis(freq_ids, count_f, count_steps, first_time):
    period = 2 * count_f
    times = first_time + jnp.arange(count_steps, dtype=jnp.int32)
    turns = (freq_ids[None, :] + 1) * times[:, None] % period
    angles = turns.astype(jnp.float32) * (2.0 * math.pi / period)
    weight = 1.0 / math.sqrt(count_f)
    return jnp.stack([weight * jnp.cos(angles), -weight * jnp.sin(angles)], axis=1)

def shifted(grid_block, step_x, step_y, step_z):
    width_x = grid_block.shape[0] - 4
    width_y = grid_block.shape[1] - 4
    width_z = grid_block.shape[2] - 4
    return grid_block[2 + step_x:2 + step_x + width_x, 2 + step_y:2 + step_y + width_y, 2 + step_z:2 + step_z + width_z]

def curvature(grid_block, first_axis):
    summed = None
    for offset, factor in [(-2, -1.0), (-1, 16.0), (0, -30.0), (1, 16.0), (2, -1.0)]:
        moves = tuple((offset if index == first_axis else 0 for index in range(3)))
        contrib = factor * shifted(grid_block, moves[0], moves[1], moves[2])
        summed = contrib if summed is None else summed + contrib
    return summed / 12.0

def mixed(grid_block, first_axis, second_axis):
    summed = None
    for sign_a, sign_b, factor in [(1, 1, 1.0), (1, -1, -1.0), (-1, 1, -1.0), (-1, -1, 1.0)]:
        moves = tuple((sign_a if index == first_axis else sign_b if index == second_axis else 0 for index in range(3)))
        contrib = factor * shifted(grid_block, moves[0], moves[1], moves[2])
        summed = contrib if summed is None else summed + contrib
    return summed / 4.0

def elastic(padded, moduli):
    first_lame = moduli[0]
    shear_mod = moduli[1]
    stiffness = first_lame + 2.0 * shear_mod
    coupling = first_lame + shear_mod
    result = []
    for component in range(3):
        update = stiffness * curvature(padded[component], component)
        for partner in range(3):
            if partner != component:
                update = update + shear_mod * curvature(padded[component], partner)
                update = update + coupling * mixed(padded[partner], component, partner)
        result.append(update)
    return jnp.stack(result)

def reference(layer_slowness, layer_rigidity, layer_damping, layer_of_level, slot_offset, slot_level, slot_target, live_count, moduli, field_old, field_now):
    slowness = level_table(layer_slowness, layer_of_level)
    rigidity = level_table(layer_rigidity, layer_of_level)
    damping = level_table(layer_damping, layer_of_level)
    freq_all = jnp.arange(F, dtype=jnp.int32)
    angular = (freq_all + 1).astype(jnp.float32) * (4.0 / F)
    kernel = wave_kernel(angular, slowness, rigidity, damping, NK).astype(jnp.bfloat16)
    cosines = offset_basis(NK, NR).astype(jnp.float32)
    waveforms = time_basis(freq_all, F, STEPS, TSTART)
    lookup = slot_level * NR + slot_offset

    def one_frequency(summed, inputs):
        kernel_f, wave_f = inputs
        spectrum = jnp.dot(kernel_f.astype(jnp.float32).reshape(2 * ND, NK), cosines, precision=lax.Precision.HIGHEST)
        picked = jnp.take(spectrum.reshape(2, ND * NR), lookup, axis=1).astype(jnp.bfloat16)
        picked = lax.optimization_barrier(picked).astype(jnp.float32)
        return (summed + jnp.dot(wave_f, picked, precision=lax.Precision.HIGHEST), None)
    traces, _ = lax.scan(one_frequency, jnp.zeros((STEPS, SLOTS), jnp.float32), (jnp.transpose(kernel, (1, 0, 2, 3)), jnp.transpose(waveforms, (2, 0, 1))))
    slot_ids = jnp.arange(SLOTS, dtype=jnp.int32)
    owner = slot_ids // Q_DEV
    within = slot_ids % Q_DEV
    occupied = (within < live_count[owner]).astype(jnp.float32)
    cells = CX * CY * NZ
    component = slot_target // cells
    local_cell = slot_target % cells
    cell_x = local_cell // (CY * NZ)
    cell_y = local_cell // NZ % CY
    cell_z = local_cell % NZ
    grid_x = owner // N_GY * CX + cell_x
    grid_y = owner % N_GY * CY + cell_y
    target = ((component * NX + grid_x) * NY + grid_y) * NZ + cell_z
    previous, current = (field_old, field_now)
    for instant in range(STEPS):
        padded = jnp.pad(current, ((0, 0), (2, 2), (2, 2), (2, 2)))
        advanced = 2.0 * current - previous + elastic(padded, moduli)
        advanced = advanced.reshape(-1).at[target].add(traces[instant] * occupied).reshape(current.shape)
        previous, current = (current, advanced)
    return (current, previous)
```

```python
import math

import jax
import jax.numpy as jnp
from jax import lax
from jax.sharding import PartitionSpec as P

F = 128
NK = 1024
NR = 2048
ND = 32
STEPS = 4
TSTART = 32


step_depth = 0.25


def padded_2(block, sides, width):
    for axis, dim in sides:
        count = lax.axis_size(axis)
        forward = [(i, i + 1) for i in range(count - 1)]
        backward = [(target, source) for source, target in forward]
        low = lax.ppermute(
            lax.slice_in_dim(block, block.shape[dim] - width, None, axis=dim), axis, forward
        )
        high = lax.ppermute(lax.slice_in_dim(block, 0, width, axis=dim), axis, backward)
        block = jnp.concatenate([low, block, high], axis=dim)
    return block


def level_table(values, layer_of_level):
    one_hot = (
        layer_of_level[:, None] == jnp.arange(values.shape[0], dtype=jnp.int32)[None, :]
    ).astype(jnp.float32)
    return jnp.sum(one_hot * values[None, :], axis=1)


def wave_kernel(wave_ids, slowness, rigidity, damping):
    wavenum = (wave_ids.astype(jnp.float32) + 0.5) * (4.0 / NK)
    angular = (jnp.arange(F, dtype=jnp.int32) + 1).astype(jnp.float32) * (4.0 / F)
    spread = angular[None, None, :] * slowness[:, None, None]
    vertical = jnp.sqrt((wavenum * wavenum)[None, :, None] + spread * spread)
    impedance = rigidity[:, None, None] * vertical
    beneath = jnp.concatenate([impedance[1:], impedance[-1:]], axis=0)
    reflect = (impedance - beneath) / (impedance + beneath)
    fading = jnp.exp(-2.0 * step_depth * vertical * damping[:, None, None])
    two_way = 2.0 * step_depth * vertical
    trip_re = fading * jnp.cos(two_way)
    trip_im = -fading * jnp.sin(two_way)

    def upward(state_in, layer_data):
        refl_re, refl_im = state_in
        coefficient, along_re, along_im = layer_data
        upper_re = coefficient + refl_re
        lower_re = 1.0 + coefficient * refl_re
        lower_im = coefficient * refl_im
        magnitude = lower_re * lower_re + lower_im * lower_im
        ratio_re = (upper_re * lower_re + refl_im * lower_im) / magnitude
        ratio_im = (refl_im * lower_re - upper_re * lower_im) / magnitude
        fresh_re = along_re * ratio_re - along_im * ratio_im
        fresh_im = along_re * ratio_im + along_im * ratio_re
        return ((fresh_re, fresh_im), (fresh_re, fresh_im))

    bottom = jnp.zeros(vertical.shape[1:], jnp.float32)
    _, (refl_re, refl_im) = lax.scan(
        upward, (bottom, bottom), (reflect, trip_re, trip_im), reverse=True
    )
    travel = step_depth * vertical
    phases = jnp.cumsum(travel, axis=0) - travel
    absorbed = travel * damping[:, None, None]
    losses = jnp.cumsum(absorbed, axis=0) - absorbed
    down_size = jnp.exp(-losses)
    down_re = down_size * jnp.cos(phases)
    down_im = -down_size * jnp.sin(phases)
    weight = 1.0 / math.sqrt(NK)
    kernel_re = weight * (down_re * (1.0 + refl_re) - down_im * refl_im)
    kernel_im = weight * (down_re * refl_im + down_im * (1.0 + refl_re))
    return kernel_re.astype(jnp.bfloat16), kernel_im.astype(jnp.bfloat16)


def time_basis(freq_ids, count_f, count_steps, first_time):
    period = 2 * count_f
    times = first_time + jnp.arange(count_steps, dtype=jnp.int32)
    turns = (freq_ids[None, :] + 1) * times[:, None] % period
    angles = turns.astype(jnp.float32) * (2.0 * math.pi / period)
    weight = 1.0 / math.sqrt(count_f)
    return jnp.stack([weight * jnp.cos(angles), -weight * jnp.sin(angles)], axis=1)


def shifted(grid_block, step_x, step_y, step_z):
    width_x = grid_block.shape[0] - 4
    width_y = grid_block.shape[1] - 4
    width_z = grid_block.shape[2] - 4
    return grid_block[
        2 + step_x : 2 + step_x + width_x,
        2 + step_y : 2 + step_y + width_y,
        2 + step_z : 2 + step_z + width_z,
    ]


def curvature(grid_block, first_axis):
    summed = None
    for offset, factor in [(-2, -1.0), (-1, 16.0), (0, -30.0), (1, 16.0), (2, -1.0)]:
        moves = tuple((offset if index == first_axis else 0 for index in range(3)))
        contrib = factor * shifted(grid_block, moves[0], moves[1], moves[2])
        summed = contrib if summed is None else summed + contrib
    return summed / 12.0


def mixed(grid_block, first_axis, second_axis):
    summed = None
    for sign_a, sign_b, factor in [(1, 1, 1.0), (1, -1, -1.0), (-1, 1, -1.0), (-1, -1, 1.0)]:
        moves = tuple(
            (
                sign_a if index == first_axis else sign_b if index == second_axis else 0
                for index in range(3)
            )
        )
        contrib = factor * shifted(grid_block, moves[0], moves[1], moves[2])
        summed = contrib if summed is None else summed + contrib
    return summed / 4.0


def elastic(padded, moduli):
    first_lame = moduli[0]
    shear_mod = moduli[1]
    stiffness = first_lame + 2.0 * shear_mod
    coupling = first_lame + shear_mod
    result = []
    for component in range(3):
        update = stiffness * curvature(padded[component], component)
        for partner in range(3):
            if partner != component:
                update = update + shear_mod * curvature(padded[component], partner)
                update = update + coupling * mixed(padded[partner], component, partner)
        result.append(update)
    return jnp.stack(result)


def shards(
    layer_slowness,
    layer_rigidity,
    layer_damping,
    layer_of_level,
    slot_offset,
    slot_level,
    slot_target,
    live_count,
    moduli,
    field_old,
    field_now,
):
    size_gy = lax.axis_size("gy")
    groups = lax.axis_size("gx") * size_gy
    device = lax.axis_index("gx") * size_gy + lax.axis_index("gy")
    per_device = NK // groups
    slots_dev = slot_target.shape[0]
    slowness = level_table(layer_slowness, layer_of_level)
    rigidity = level_table(layer_rigidity, layer_of_level)
    damping = level_table(layer_damping, layer_of_level)
    wave_ids = device * per_device + jnp.arange(per_device, dtype=jnp.int32)
    kernel_re, kernel_im = wave_kernel(wave_ids, slowness, rigidity, damping)
    waves = time_basis(jnp.arange(F, dtype=jnp.int32), F, STEPS, TSTART)
    both = jnp.concatenate([kernel_re, kernel_im], axis=2).astype(jnp.float32)
    summed = jnp.dot(
        both.reshape(ND * per_device, 2 * F),
        waves.reshape(STEPS, 2 * F).T,
        precision=lax.Precision.HIGHEST,
    )
    mine = jnp.transpose(summed.reshape(ND, per_device, STEPS), (1, 2, 0)).reshape(
        per_device, STEPS * ND
    )
    gathered = lax.all_gather(mine, ("gx", "gy"), axis=0, tiled=True)
    offsets = lax.dynamic_slice_in_dim(slot_offset, device * slots_dev, slots_dev)
    levels = lax.dynamic_slice_in_dim(slot_level, device * slots_dev, slots_dev)
    odd_index = 2 * jnp.arange(NK, dtype=jnp.int32) + 1
    modulus = NK * NR // 2
    turns = offsets[:, None] * odd_index[None, :] % modulus
    cosines = jnp.cos(turns.astype(jnp.float32) * (2.0 * math.pi / modulus)).astype(jnp.bfloat16)
    picked = jnp.dot(cosines.astype(jnp.float32), gathered, precision=lax.Precision.HIGHEST)
    level_hot = (levels[:, None] == jnp.arange(ND, dtype=jnp.int32)[None, :]).astype(jnp.float32)
    traces = jnp.sum(picked.reshape(slots_dev, STEPS, ND) * level_hot[:, None, :], axis=2).T
    occupied = (jnp.arange(slots_dev, dtype=jnp.int32) < live_count[0]).astype(jnp.float32)
    block_x = field_now.shape[1]
    block_y = field_now.shape[2]
    depth = field_now.shape[3]
    columns = slot_target // depth
    layer_z = slot_target % depth
    weighted = traces * occupied[None, :]
    column_hot = (
        jnp.arange(3 * block_x * block_y, dtype=jnp.int32)[:, None] == columns[None, :]
    ).astype(jnp.float32)
    depth_hot = (layer_z[:, None] == jnp.arange(depth, dtype=jnp.int32)[None, :]).astype(
        jnp.float32
    )
    spread_traces = weighted[:, :, None] * depth_hot[None, :, :]
    sources = jnp.einsum("ag,ngz->naz", column_hot, spread_traces, precision=lax.Precision.HIGHEST)
    sources = sources.reshape(STEPS, 3, block_x, block_y, depth)
    previous, current = (field_old, field_now)
    for instant in range(STEPS):
        padded = padded_2(current, (("gx", 1), ("gy", 2)), 2)
        padded = jnp.pad(padded, ((0, 0), (0, 0), (0, 0), (2, 2)))
        advanced = 2.0 * current - previous + elastic(padded, moduli)
        advanced = advanced + sources[instant]
        previous, current = (current, advanced)
    return (current, previous)


def solution(mesh):
    in_specs = (
        P(),
        P(),
        P(),
        P(),
        P(),
        P(),
        P(("gx", "gy")),
        P(("gx", "gy")),
        P(None, "gx", "gy", None),
        P(None, "gx", "gy", None),
        P(None, "gx", "gy", None),
    )
    out_specs = (P(None, "gx", "gy", None), P(None, "gx", "gy", None))
    return jax.shard_map(shards, mesh=mesh, in_specs=in_specs, out_specs=out_specs, check_vma=False)
```

```python
import functools
import math

import jax
import jax.numpy as jnp
import ml_dtypes
import numpy as np
from jax import lax
from jax.experimental import pallas as pl
from jax.experimental.pallas import tpu as pltpu
from jax.sharding import PartitionSpec as P

F = 128
NK = 1024
NR = 2048
ND = 32
STEPS = 4
TSTART = 32
GX = 16
GY = 8
C = 32
NZ = 256
Q = 256
GROUPS = 8
XG = 4
ROWS = XG * C
LINKS = 8
MESH = pl.DeviceIdType.MESH
BF = jnp.bfloat16
F32 = jnp.float32


def constants():
    y2 = np.zeros((ROWS, ROWS + 32), np.float32)
    y1 = np.zeros((ROWS, ROWS + 32), np.float32)
    low, high = ROWS, ROWS + 16

    def place(x, y):
        if y < 0:
            return low + 2 * (x + 1) + y + 2
        if y >= C:
            return high + 2 * (x + 1) + y - C
        return x * C + y

    for x in range(XG):
        for y in range(C):
            row = x * C + y
            for shift, factor in ((-2, -1.0), (-1, 16.0), (0, -30.0), (1, 16.0), (2, -1.0)):
                y2[row, place(x, y + shift)] += factor
            y1[row, place(x, y + 1)] += 1.0
            y1[row, place(x, y - 1)] -= 1.0
    cross = np.zeros((3, ROWS, ROWS + 96), np.float32)
    for kind in range(3):
        cross[kind, :, :ROWS] = 3.0 * y1[:, :ROWS]
        cross[kind, :, ROWS + 64 :] = 3.0 * y1[:, ROWS:]
        for x in range(XG):
            for y, beyond, sign in ((0, -1, -3.0), (C - 1, C, 3.0)):
                for step in (-1, 1):
                    outside = (kind == 0 and x + step < 0) or (kind == 2 and x + step >= XG)
                    if outside:
                        spot = ROWS + 32 + 15 if beyond < 0 else ROWS + 48
                    else:
                        spot = place(x + step, beyond)
                    cross[kind, x * C + y, spot] += sign * step
    pick = np.zeros((3, 32, 6 * C), np.float32)
    for kind in range(3):
        for i in range(6):
            x = i - 1 + kind if kind != 1 else i
            if kind == 0:
                x = i - 1
            elif kind == 2:
                x = i + 1
            if 0 <= x < 6:
                for k in range(2):
                    pick[kind, 2 * i + k, x * C + C - 2 + k] = 1.0
                    pick[kind, 16 + 2 * i + k, x * C + k] = 1.0
    z2 = np.zeros((NZ, NZ), np.float32)
    z1 = np.zeros((NZ, NZ), np.float32)
    for z in range(NZ):
        for shift, factor in ((-2, -1.0), (-1, 16.0), (0, -30.0), (1, 16.0), (2, -1.0)):
            if 0 <= z + shift < NZ:
                z2[z + shift, z] += factor
        if z + 1 < NZ:
            z1[z + 1, z] += 1.0
        if z > 0:
            z1[z - 1, z] -= 1.0
    period = 2 * F
    turns = (np.arange(F)[None, :] + 1) * (TSTART + np.arange(STEPS)[:, None]) % period
    angles = turns * (2.0 * math.pi / period)
    weight = 1.0 / math.sqrt(F)
    waves = np.concatenate([weight * np.cos(angles), -weight * np.sin(angles)], axis=1).T
    waves = np.repeat(waves.astype(np.float32), ND, axis=1)
    upper = waves.astype(ml_dtypes.bfloat16)
    lower = (waves - upper.astype(np.float32)).astype(ml_dtypes.bfloat16)
    ones = np.zeros((STEPS, STEPS * ND, NZ), np.float32)
    for n in range(STEPS):
        ones[n, n * ND : (n + 1) * ND] = 1.0
    half = ml_dtypes.bfloat16
    return dict(
        y2=y2.astype(half),
        y1=y1.astype(half),
        cross=cross.astype(half),
        pick=pick.astype(half),
        z2=z2.astype(half),
        z1=z1.astype(half),
        z3=(3.0 * z1).astype(half),
        waves=np.concatenate([upper, lower], axis=1),
        ones=ones.astype(half),
    )


def dot(a, b):
    return jnp.dot(a, b, preferred_element_type=F32)


def advance(window, lows, highs, clows, chighs, now, before, lam, mu, sources, y2, y1, cross, z2, z1, z3):
    wide = [w.astype(F32) for w in window]
    inner = [w[2 : 2 + XG].reshape(ROWS, NZ) for w in window]
    second = [
        (16.0 * (w[1:5] + w[3:7]) - (w[0:4] + w[4:8]) - 30.0 * w[2:6]).reshape(ROWS, NZ)
        for w in wide
    ]
    first = [(w[3:7] - w[1:5]).reshape(ROWS, NZ) for w in wide]
    ends = [jnp.concatenate([lows[c], highs[c]], axis=0) for c in range(3)]
    tall = [jnp.concatenate([inner[c], ends[c]], axis=0) for c in range(3)]
    along_y = [dot(y2, tall[c]) for c in range(3)]
    along_z = [dot(inner[c], z2) for c in range(3)]
    skew_z = dot(tall[2], z1)
    skew_y = dot(y1, tall[1])
    mix_0 = dot(
        cross[:, : ROWS + 64],
        jnp.concatenate([first[1].astype(BF), ends[1], clows[1], chighs[1]], axis=0),
    ) + dot(first[2].astype(BF), z3)
    mix_1 = dot(
        cross,
        jnp.concatenate(
            [
                (first[0] + skew_z[:ROWS]).astype(BF),
                ends[0],
                clows[0],
                chighs[0],
                skew_z[ROWS:].astype(BF),
            ],
            axis=0,
        ),
    )
    mix_2 = dot((first[0] + skew_y).astype(BF), z3)
    couple = [second[0] + mix_0, along_y[1] + mix_1, along_z[2] + mix_2]
    joint = lam + mu
    result = []
    for c in range(3):
        lap = second[c] + (along_y[c] + along_z[c])
        moved = (mu * lap + joint * couple[c]) * (1.0 / 12.0)
        result.append((2.0 * now[c] - before[c]) + (moved + sources[c]))
    return result


def sine(x):
    y = x * x
    poly = -2.5052108e-08
    for coefficient in (2.7557319e-06, -1.9841270e-04, 8.3333333e-03, -1.6666667e-01, 1.0):
        poly = poly * y + coefficient
    return x * poly


def cosine(x):
    y = x * x
    poly = -2.7557319e-07
    for coefficient in (2.4801587e-05, -1.3888889e-03, 4.1666667e-02, -0.5, 1.0):
        poly = poly * y + coefficient
    return poly


def lane_spread(row):
    return jnp.transpose(jnp.broadcast_to(row.astype(F32), (128, 128))).astype(jnp.int32)


def main_kernel(
    slow_ref, rigid_ref, damp_ref, level_ref, live_ref, target_ref,
    y2_ref, y1_ref, cross_ref, pick_ref, z2_ref, z1_ref, z3_ref, waves_ref, ones_ref,
    offsets_hbm, levels_hbm, moduli_hbm, old_hbm, now_hbm,
    last_hbm, prior_hbm, half_hbm, side_hbm, corner_hbm, spread_hbm,
    field, mod, half, side_out, side_in, corner, hot, gathered, basis, spread,
    slot_tile, zbuf, ebuf, dbuf, kbuf,
    load_sem, store_sem, send_sem, recv_sem, gsend_sem, grecv_sem,
):
    gx = lax.axis_index("gx")
    gy = lax.axis_index("gy")
    device = gx * GY + gy
    px, pz = gx // 4, gx % 4
    py, core = gy // 2, gy % 2
    block = core * 64 + px * 16 + pz * 4 + py

    loads = [
        pltpu.make_async_copy(now_hbm, field.at[0], load_sem.at[0]),
        pltpu.make_async_copy(old_hbm, field.at[1], load_sem.at[1]),
        pltpu.make_async_copy(moduli_hbm, mod, load_sem.at[2]),
        pltpu.make_async_copy(
            offsets_hbm.at[pl.ds(pl.multiple_of(device // 4 * 8, 8), 8)], slot_tile.at[0], load_sem.at[3]
        ),
        pltpu.make_async_copy(
            levels_hbm.at[pl.ds(pl.multiple_of(device // 4 * 8, 8), 8)], slot_tile.at[1], load_sem.at[4]
        ),
    ]
    for load in loads:
        load.start()

    for p in range(2):
        half[p, :, 0:2] = jnp.zeros((3, 2, C, NZ), BF)
        half[p, :, C + 2 : C + 4] = jnp.zeros((3, 2, C, NZ), BF)
        corner[p] = jnp.zeros(corner.shape[1:], BF)
        for s in range(2):
            side_in[p, s] = jnp.zeros(side_in.shape[2:], BF)

    steps = [(1, 0), (-1, 0), (0, 1), (0, -1), (1, 1), (1, -1), (-1, 1), (-1, -1)]

    def exists(dx, dy):
        ok = None
        for delta, place, size in ((dx, gx, GX), (dy, gy, GY)):
            if delta == 1:
                part = place < size - 1
            elif delta == -1:
                part = place > 0
            else:
                continue
            ok = part if ok is None else jnp.logical_and(ok, part)
        return ok

    barrier = pltpu.get_barrier_semaphore()
    for dx, dy in steps:
        @pl.when(exists(dx, dy))
        def _():
            pl.semaphore_signal(barrier, inc=1, device_id=(gx + dx, gy + dy), device_id_type=MESH)

    def ring_y(k):
        return (gx, (py + k) % 4 * 2 + core)

    def ring_z(k):
        return (px * 4 + (pz + k) % 4, gy)

    def ring_x(k):
        return ((px + k) % 4 * 4 + pz, gy)

    for ring in (ring_y, ring_z, ring_x):
        for k in (1, 2, 3):
            pl.semaphore_signal(barrier, inc=1, device_id=ring(k), device_id_type=MESH)
    twin = (gx, py * 2 + 1 - core)
    pl.semaphore_signal(barrier, inc=1, device_id=twin, device_id_type=MESH)

    rows = lax.broadcasted_iota(jnp.int32, (8, 128), 0) + block * 8
    wavenum = (rows.astype(F32) + 0.5) * (4.0 / NK)
    square_k = wavenum * wavenum
    omega = (lax.broadcasted_iota(jnp.int32, (8, 128), 1) + 1).astype(F32) * (4.0 / F)

    def downward(i, carry):
        down_re, down_im = carry
        layer = level_ref[i]
        part = omega * slow_ref[layer]
        vertical = jnp.sqrt(square_k + part * part)
        fade = jnp.exp(vertical * (-0.25 * damp_ref[layer]))
        angle = 0.125 * vertical
        s, c = sine(angle), cosine(angle)
        leg_re = fade * (1.0 - 2.0 * s * s)
        leg_im = fade * (-2.0 * s * c)
        zbuf[i] = rigid_ref[layer] * vertical
        ebuf[0, i] = leg_re
        ebuf[1, i] = leg_im
        dbuf[0, i] = down_re
        dbuf[1, i] = down_im
        return down_re * leg_re - down_im * leg_im, down_re * leg_im + down_im * leg_re

    one = jnp.ones((8, 128), F32)
    zero = jnp.zeros((8, 128), F32)
    lax.fori_loop(0, ND, downward, (one, zero), unroll=4)
    zbuf[ND] = zbuf[ND - 1]

    def upward(step, carry):
        refl_re, refl_im = carry
        i = ND - 1 - step
        upper, under = zbuf[i], zbuf[i + 1]
        r = (upper - under) / (upper + under)
        leg_re, leg_im = ebuf[0, i], ebuf[1, i]
        trip_re = leg_re * leg_re - leg_im * leg_im
        trip_im = 2.0 * leg_re * leg_im
        upper_re = r + refl_re
        lower_re = 1.0 + r * refl_re
        lower_im = r * refl_im
        scale = 1.0 / (lower_re * lower_re + lower_im * lower_im)
        ratio_re = (upper_re * lower_re + refl_im * lower_im) * scale
        ratio_im = (refl_im * lower_re - upper_re * lower_im) * scale
        fresh_re = trip_re * ratio_re - trip_im * ratio_im
        fresh_im = trip_re * ratio_im + trip_im * ratio_re
        down_re, down_im = dbuf[0, i], dbuf[1, i]
        kbuf[i, :, 0:128] = (down_re * (1.0 + fresh_re) - down_im * fresh_im) * (1.0 / 32.0)
        kbuf[i, :, 128:256] = (down_re * fresh_im + down_im * (1.0 + fresh_re)) * (1.0 / 32.0)
        return fresh_re, fresh_im

    lax.fori_loop(0, ND, upward, (zero, zero), unroll=4)
    product = dot(kbuf[...].reshape(ND * 8, 2 * F).astype(BF), waves_ref[...])
    product = product[:, :128] + product[:, 128:]
    lane = lax.broadcasted_iota(jnp.int32, (8, 128), 1) % ND
    mine = zero
    for d in range(ND):
        mine = jnp.where(lane == d, product[8 * d : 8 * d + 8], mine)
    gathered[block] = mine

    count = 10
    for dx, dy in steps:
        count = count + exists(dx, dy).astype(jnp.int32)
    pl.semaphore_wait(barrier, count)

    def stage(index, ring, start, size):
        copies = []
        for k in (1, 2, 3):
            piece = gathered.at[pl.ds(start, size)]
            copies.append(
                pltpu.make_async_remote_copy(
                    src_ref=piece,
                    dst_ref=piece,
                    send_sem=gsend_sem.at[3 * index + k - 1],
                    recv_sem=grecv_sem.at[3 * index + k - 1],
                    device_id=ring(k),
                    device_id_type=MESH,
                )
            )
        for copy in copies:
            copy.start()
        return copies

    def finish(copies):
        for copy in copies:
            copy.wait()

    stage_y = stage(0, ring_y, block, 1)

    def to_half(g, carry):
        x = g * XG
        for c in range(3):
            half[0, c, pl.ds(x + 2, XG)] = field[0, c, pl.ds(x, XG)].astype(BF)
        return carry

    def kind_of(g):
        return (g + GROUPS - 2) // (GROUPS - 1)

    def exchange(n):
        p = n % 2

        def fill(g, carry):
            kind = jnp.where(g == 0, 0, jnp.where(g == GROUPS - 1, 2, 1))
            x = jnp.where(g == 0, 0, jnp.where(g == GROUPS - 1, C - 6, g * XG - 1))
            for c in range(3):
                tile = dot(pick_ref[kind], half[p, c, pl.ds(x + 2, 6)].reshape(6 * C, NZ)).astype(BF)
                side_out[p, 0, c, g] = tile[:16]
                side_out[p, 1, c, g] = tile[16:]
            return carry

        lax.fori_loop(0, GROUPS, fill, 0)
        pairs = [
            (half.at[p, :, pl.ds(C, 2)], half.at[p, :, pl.ds(0, 2)]),
            (half.at[p, :, pl.ds(2, 2)], half.at[p, :, pl.ds(C + 2, 2)]),
            (side_out.at[p, 0], side_in.at[p, 0]),
            (side_out.at[p, 1], side_in.at[p, 1]),
            (half.at[p, pl.ds(0, 2), C + 1, pl.ds(16, 16)], corner.at[p, 0, 0]),
            (half.at[p, pl.ds(0, 2), C + 1, pl.ds(0, 16)], corner.at[p, 0, 1]),
            (half.at[p, pl.ds(0, 2), 2, pl.ds(16, 16)], corner.at[p, 1, 0]),
            (half.at[p, pl.ds(0, 2), 2, pl.ds(0, 16)], corner.at[p, 1, 1]),
        ]
        copies = []
        for index, ((dx, dy), (source, target)) in enumerate(zip(steps, pairs)):
            copies.append(
                pltpu.make_async_remote_copy(
                    src_ref=source,
                    dst_ref=target,
                    send_sem=send_sem.at[n, index],
                    recv_sem=recv_sem.at[n, index],
                    device_id=(gx + dx, gy + dy),
                    device_id_type=MESH,
                )
            )
        for (dx, dy), copy in zip(steps, copies):
            @pl.when(exists(dx, dy))
            def _():
                copy.start()

        return copies

    def settle(copies):
        for (dx, dy), copy in zip(steps, copies):
            @pl.when(exists(dx, dy))
            def _():
                copy.wait_send()

            @pl.when(exists(-dx, -dy))
            def _():
                copy.wait_recv()

    loads[0].wait()
    lax.fori_loop(0, GROUPS, to_half, 0)
    copies = exchange(0)
    finish(stage_y)
    stage_z = stage(1, ring_z, block // 4 * 4, 4)

    loads[3].wait()
    loads[4].wait()
    row = device % 4 * 2
    mask = NK * NR // 2 - 1
    for h in range(2):
        part = pl.ds(128 * h, 128)
        q = lane_spread(slot_tile[0, pl.ds(row + h, 1)])
        lanes = lax.broadcasted_iota(jnp.int32, (128, 128), 1)
        for b in range(NK // 128):
            turns = (2 * (lanes + 128 * b) + 1) * q
            turns = ((turns + (mask + 1) // 2) & mask) - (mask + 1) // 2
            s = sine(turns.astype(F32) * (math.pi / (mask + 1)))
            basis[part, 128 * b : 128 * b + 128] = (1.0 - 2.0 * s * s).astype(BF)
    finish(stage_z)
    stage_x = stage(2, ring_x, block // 16 * 16, 16)

    def build_hot(g, carry):
        ids = lax.broadcasted_iota(jnp.int32, (ROWS, Q), 0) + g * ROWS
        columns = target_ref[...] // NZ
        for c in range(3):
            same = ids + c * C * C == columns
            hot[c, g] = jnp.where(same, 1.0, 0.0).astype(BF)
        return carry

    lax.fori_loop(0, GROUPS, build_hot, 0)
    finish(stage_x)
    whole = gathered.at[pl.ds(core * 64, 64)]
    swap = pltpu.make_async_remote_copy(
        src_ref=whole,
        dst_ref=whole,
        send_sem=gsend_sem.at[9],
        recv_sem=grecv_sem.at[9],
        device_id=twin,
        device_id_type=MESH,
    )
    swap.start()
    swap.wait()

    total = gathered[...].reshape(NK, 128)
    upper = total.astype(BF)
    lower = (total - upper.astype(F32)).astype(BF)
    picked = dot(basis[...], jnp.concatenate([upper, lower], axis=1))
    picked = picked[:, :128] + picked[:, 128:]
    for h in range(2):
        part = slice(128 * h, 128 * h + 128)
        lanes = lax.broadcasted_iota(jnp.int32, (128, 128), 1)
        ids = lax.broadcasted_iota(jnp.int32, (128, 128), 0) + 128 * h
        level = lane_spread(slot_tile[1, pl.ds(row + h, 1)])
        keep = jnp.logical_and(lanes % ND == level, ids < live_ref[0])
        chosen = jnp.where(keep, picked[part], 0.0).astype(BF)
        depth = lane_spread(target_ref[:, 128 * h : 128 * h + 128] % NZ)
        for n in range(STEPS):
            values = dot(chosen, ones_ref[n])
            for b in range(2):
                same = lanes + 128 * b == depth
                spread[n, part, 128 * b : 128 * b + 128] = jnp.where(
                    same, values[:, 128 * b : 128 * b + 128], 0.0
                ).astype(BF)

    loads[1].wait()
    loads[2].wait()
    for n in range(STEPS - 1):
        p = n % 2
        settle(copies)

        def group(g, carry):
            x = g * XG
            kind = jnp.where(g == 0, 0, jnp.where(g == GROUPS - 1, 2, 1))
            right = g // (GROUPS // 2)
            window = [half[p, c, pl.ds(x, XG + 4)] for c in range(3)]
            lows = [side_in[p, 0, c, g] for c in range(3)]
            highs = [side_in[p, 1, c, g] for c in range(3)]
            clows = [corner[p, right, 0, c] for c in range(2)]
            chighs = [corner[p, right, 1, c] for c in range(2)]
            sources = [dot(hot[c, g], spread[n]) for c in range(3)]
            result = advance(
                window, lows, highs, clows, chighs,
                [field[p, c, pl.ds(x, XG)].reshape(ROWS, NZ) for c in range(3)],
                [field[1 - p, c, pl.ds(x, XG)].reshape(ROWS, NZ) for c in range(3)],
                mod[0, pl.ds(x, XG)].reshape(ROWS, NZ),
                mod[1, pl.ds(x, XG)].reshape(ROWS, NZ),
                sources,
                y2_ref[...], y1_ref[...], cross_ref[kind], z2_ref[...], z1_ref[...], z3_ref[...],
            )
            for c in range(3):
                fresh = result[c].reshape(XG, C, NZ)
                field[1 - p, c, pl.ds(x, XG)] = fresh
                half[1 - p, c, pl.ds(x + 2, XG)] = fresh.astype(BF)
            return carry

        lax.fori_loop(0, GROUPS, group, 0)
        copies = exchange(n + 1)

    p = (STEPS - 1) % 2
    stores = [
        pltpu.make_async_copy(field.at[p], last_hbm, store_sem.at[0]),
        pltpu.make_async_copy(field.at[1 - p], prior_hbm, store_sem.at[1]),
        pltpu.make_async_copy(spread.at[STEPS - 1], spread_hbm, store_sem.at[2]),
        pltpu.make_async_copy(half.at[p], half_hbm, store_sem.at[3]),
        pltpu.make_async_copy(side_in.at[p], side_hbm, store_sem.at[4]),
        pltpu.make_async_copy(corner.at[p], corner_hbm, store_sem.at[5]),
    ]
    for store in stores[:3]:
        store.start()
    settle(copies)
    for store in stores[3:]:
        store.start()
    for store in stores:
        store.wait()


def last_kernel(
    target_ref, y2_ref, y1_ref, cross_ref, z2_ref, z1_ref, z3_ref,
    half, side, corner, spread, now_ref, before_ref, mod, final_ref, copy_ref,
):
    g = pl.program_id(0)
    x = g * XG
    kind = jnp.where(g == 0, 0, jnp.where(g == GROUPS - 1, 2, 1))
    right = g // (GROUPS // 2)
    ids = lax.broadcasted_iota(jnp.int32, (ROWS, Q), 0) + g * ROWS
    columns = target_ref[...] // NZ
    sources = [
        dot(jnp.where(ids + c * C * C == columns, 1.0, 0.0).astype(BF), spread[...]) for c in range(3)
    ]
    result = advance(
        [half[c, pl.ds(x, XG + 4)] for c in range(3)],
        [side[0, c, g] for c in range(3)],
        [side[1, c, g] for c in range(3)],
        [corner[right, 0, c] for c in range(2)],
        [corner[right, 1, c] for c in range(2)],
        [now_ref[c].reshape(ROWS, NZ) for c in range(3)],
        [before_ref[c].reshape(ROWS, NZ) for c in range(3)],
        mod[0].reshape(ROWS, NZ),
        mod[1].reshape(ROWS, NZ),
        sources,
        y2_ref[...], y1_ref[...], cross_ref[kind], z2_ref[...], z1_ref[...], z3_ref[...],
    )
    for c in range(3):
        final_ref[c] = result[c].reshape(XG, C, NZ)
        copy_ref[c] = now_ref[c]


def shards(
    layer_slowness, layer_rigidity, layer_damping, layer_of_level,
    slot_offset, slot_level, slot_target, live_count, moduli, field_old, field_now,
):
    fixed = constants()
    smem = pl.BlockSpec(memory_space=pltpu.SMEM)
    vmem = pl.BlockSpec(memory_space=pltpu.VMEM)
    any_space = pl.BlockSpec(memory_space=pl.ANY)
    target = slot_target.reshape(1, Q)
    block = jax.ShapeDtypeStruct((3, C, C, NZ), F32)
    names = ("y2", "y1", "cross", "pick", "z2", "z1", "z3", "waves", "ones")
    dma = pltpu.SemaphoreType.DMA
    last, prior, half, side, corner, spread = pl.pallas_call(
        main_kernel,
        out_shape=[
            block,
            block,
            jax.ShapeDtypeStruct((3, C + 4, C, NZ), BF),
            jax.ShapeDtypeStruct((2, 3, GROUPS, 16, NZ), BF),
            jax.ShapeDtypeStruct((2, 2, 2, 16, NZ), BF),
            jax.ShapeDtypeStruct((Q, NZ), BF),
        ],
        in_specs=[smem] * 5 + [vmem] * (1 + len(names)) + [any_space] * 5,
        out_specs=[any_space] * 6,
        scratch_shapes=[
            pltpu.VMEM((2, 3, C, C, NZ), F32),
            pltpu.VMEM((2, C, C, NZ), F32),
            pltpu.VMEM((2, 3, C + 4, C, NZ), BF),
            pltpu.VMEM((2, 2, 3, GROUPS, 16, NZ), BF),
            pltpu.VMEM((2, 2, 3, GROUPS, 16, NZ), BF),
            pltpu.VMEM((2, 2, 2, 2, 16, NZ), BF),
            pltpu.VMEM((3, GROUPS, ROWS, Q), BF),
            pltpu.VMEM((NK // 8, 8, 128), F32),
            pltpu.VMEM((Q, NK), BF),
            pltpu.VMEM((STEPS, Q, NZ), BF),
            pltpu.VMEM((2, 8, 128), jnp.int32),
            pltpu.VMEM((ND + 1, 8, 128), F32),
            pltpu.VMEM((2, ND, 8, 128), F32),
            pltpu.VMEM((2, ND, 8, 128), F32),
            pltpu.VMEM((ND, 8, 2 * F), F32),
            dma((5,)),
            dma((6,)),
            dma((STEPS, LINKS)),
            dma((STEPS, LINKS)),
            dma((10,)),
            dma((10,)),
        ],
        compiler_params=pltpu.CompilerParams(
            collective_id=0, has_side_effects=True, vmem_limit_bytes=48 * 1024 * 1024
        ),
    )(
        layer_slowness, layer_rigidity, layer_damping, layer_of_level, live_count, target,
        *[jnp.asarray(fixed[name]) for name in names],
        slot_offset.reshape(Q, 128), slot_level.reshape(Q, 128), moduli, field_old, field_now,
    )
    names = ("y2", "y1", "cross", "z2", "z1", "z3")

    def full(shape):
        return pl.BlockSpec(shape, lambda g: (0,) * len(shape))

    rows = pl.BlockSpec((3, XG, C, NZ), lambda g: (0, g, 0, 0))
    matrices = [jnp.asarray(fixed[name]) for name in names]
    return pl.pallas_call(
        last_kernel,
        grid=(GROUPS,),
        out_shape=[block, block],
        in_specs=[full((1, Q))]
        + [full(m.shape) for m in matrices]
        + [full(half.shape), full(side.shape), full(corner.shape), full(spread.shape), rows, rows]
        + [pl.BlockSpec((2, XG, C, NZ), lambda g: (0, g, 0, 0))],
        out_specs=[rows, rows],
        compiler_params=pltpu.CompilerParams(vmem_limit_bytes=48 * 1024 * 1024),
    )(target, *matrices, half, side, corner, spread, last, prior, moduli)


def solution(mesh):
    in_specs = (
        P(),
        P(),
        P(),
        P(),
        P(),
        P(),
        P(("gx", "gy")),
        P(("gx", "gy")),
        P(None, "gx", "gy", None),
        P(None, "gx", "gy", None),
        P(None, "gx", "gy", None),
    )
    out_specs = (P(None, "gx", "gy", None), P(None, "gx", "gy", None))
    return jax.shard_map(shards, mesh=mesh, in_specs=in_specs, out_specs=out_specs, check_vma=False)
```

```python
import functools
import math

import jax
import jax.numpy as jnp
import ml_dtypes
import numpy as np
from jax import lax
from jax.experimental import pallas as pl
from jax.experimental.pallas import tpu as pltpu
from jax.sharding import PartitionSpec as P

F = 128
NK = 1024
NR = 2048
ND = 32
STEPS = 4
TSTART = 32
GX = 16
GY = 8
C = 32
NZ = 256
Q = 256
GROUPS = 8
XG = 4
ROWS = XG * C
LINKS = 12
VMEM = 63 * 1024 * 1024
MESH = pl.DeviceIdType.MESH
BF = jnp.bfloat16
F32 = jnp.float32


def constants():
    y2 = np.zeros((ROWS, ROWS + 32), np.float32)
    y1 = np.zeros((ROWS, ROWS + 32), np.float32)
    low, high = ROWS, ROWS + 16

    def place(x, y):
        if y < 0:
            return low + 2 * (x + 1) + y + 2
        if y >= C:
            return high + 2 * (x + 1) + y - C
        return x * C + y

    for x in range(XG):
        for y in range(C):
            row = x * C + y
            for shift, factor in ((-2, -1.0), (-1, 16.0), (1, 16.0), (2, -1.0)):
                y2[row, place(x, y + shift)] += factor
            y1[row, place(x, y + 1)] += 1.0
            y1[row, place(x, y - 1)] -= 1.0
    cross = np.zeros((3, ROWS, ROWS + 96), np.float32)
    for kind in range(3):
        cross[kind, :, :ROWS] = 3.0 * y1[:, :ROWS]
        cross[kind, :, ROWS + 64 :] = 3.0 * y1[:, ROWS:]
        for x in range(XG):
            for y, beyond, sign in ((0, -1, -3.0), (C - 1, C, 3.0)):
                for step in (-1, 1):
                    outside = (kind == 0 and x + step < 0) or (kind == 2 and x + step >= XG)
                    if outside:
                        spot = ROWS + 32 + 15 if beyond < 0 else ROWS + 48
                    else:
                        spot = place(x + step, beyond)
                    cross[kind, x * C + y, spot] += sign * step
    pick = np.zeros((3, 32, 6 * C), np.float32)
    for kind in range(3):
        for i in range(6):
            x = i - 1 + kind
            if 0 <= x < 6:
                for k in range(2):
                    pick[kind, 2 * i + k, x * C + C - 2 + k] = 1.0
                    pick[kind, 16 + 2 * i + k, x * C + k] = 1.0
    z2 = np.zeros((NZ, NZ), np.float32)
    z1 = np.zeros((NZ, NZ), np.float32)
    for z in range(NZ):
        for shift, factor in ((-2, -1.0), (-1, 16.0), (1, 16.0), (2, -1.0)):
            if 0 <= z + shift < NZ:
                z2[z + shift, z] += factor
        if z + 1 < NZ:
            z1[z + 1, z] += 1.0
        if z > 0:
            z1[z - 1, z] -= 1.0
    period = 2 * F
    turns = (np.arange(F)[None, :] + 1) * (TSTART + np.arange(STEPS)[:, None]) % period
    angles = turns * (2.0 * math.pi / period)
    weight = 1.0 / math.sqrt(F)
    waves = np.concatenate([weight * np.cos(angles), -weight * np.sin(angles)], axis=1).T
    waves = np.repeat(waves.astype(np.float32), ND, axis=1)
    upper = waves.astype(ml_dtypes.bfloat16)
    lower = (waves - upper.astype(np.float32)).astype(ml_dtypes.bfloat16)
    half = ml_dtypes.bfloat16
    parts = [y2, y1, *cross, z2, z1, 3.0 * z1, *pick]
    parts = [np.pad(part, ((0, 0), (0, 256 - part.shape[1]))).astype(half) for part in parts]
    return np.concatenate(parts + [np.concatenate([upper, lower], axis=1)])


AT_Y2, AT_Y1, AT_CROSS, AT_Z2, AT_Z1, AT_Z3 = 0, 128, 256, 640, 896, 1152
AT_PICK, AT_WAVES, TABLE = 1408, 1504, 1760
SHORT = AT_PICK


def matrices(table, kind):
    return (
        table[AT_Y2 : AT_Y2 + ROWS, : ROWS + 32],
        table[AT_Y1 : AT_Y1 + ROWS, : ROWS + 32],
        table[pl.ds(pl.multiple_of(AT_CROSS + ROWS * kind, ROWS), ROWS)],
        table[AT_Z2 : AT_Z2 + NZ],
        table[AT_Z1 : AT_Z1 + NZ],
        table[AT_Z3 : AT_Z3 + NZ],
    )


def dot(a, b):
    return jnp.dot(a, b, preferred_element_type=F32)


def beside(*parts):
    return jnp.concatenate(parts, axis=1)


def below(*parts):
    return jnp.concatenate(parts, axis=0)


def advance(window, lows, highs, clows, chighs, now, before, lam, mu, sources, y2, y1, cross, z2, z1, z3):
    wide = [w.astype(F32) for w in window]
    inner = [w[2 : 2 + XG].reshape(ROWS, NZ) for w in window]
    second = [(16.0 * (w[1:5] + w[3:7]) - (w[0:4] + w[4:8])).reshape(ROWS, NZ) for w in wide]
    first = [(w[3:7] - w[1:5]).reshape(ROWS, NZ) for w in wide]
    tall = [below(inner[c], lows[c], highs[c]) for c in range(3)]
    skew_z = dot(tall[2], z1)
    skew_y = dot(y1, tall[1])
    lap = [dot(beside(inner[c], y2), below(z2, tall[c])) for c in range(3)]
    mix_0 = dot(
        beside(first[2].astype(BF), cross[:, : ROWS + 64]),
        below(z3, first[1].astype(BF), lows[1], highs[1], clows[1], chighs[1]),
    )
    mix_1 = dot(
        beside(cross, y2),
        below(
            (first[0] + skew_z[:ROWS]).astype(BF), lows[0], highs[0], clows[0], chighs[0],
            skew_z[ROWS:].astype(BF), lows[0], highs[0], tall[1],
        ),
    )
    mix_2 = dot(beside(inner[2], (first[0] + skew_y).astype(BF)), below(z2, z3))
    couple = [second[0] + mix_0, mix_1, mix_2]
    shear = mu * (1.0 / 12.0)
    joint = (lam + mu) * (1.0 / 12.0)
    centre = 2.0 - 90.0 * shear - 30.0 * joint
    result = []
    for c in range(3):
        moved = shear * (second[c] + lap[c]) + joint * couple[c]
        if sources is not None:
            moved = moved + sources[c]
        result.append((centre * now[c] - before[c]) + moved)
    return result


def sine(x):
    y = x * x
    poly = -2.5052108e-08
    for coefficient in (2.7557319e-06, -1.9841270e-04, 8.3333333e-03, -1.6666667e-01, 1.0):
        poly = poly * y + coefficient
    return x * poly


def cosine(x):
    y = x * x
    poly = -2.7557319e-07
    for coefficient in (2.4801587e-05, -1.3888889e-03, 4.1666667e-02, -0.5, 1.0):
        poly = poly * y + coefficient
    return poly


def lane_spread(row):
    return jnp.transpose(jnp.broadcast_to(row.astype(F32), (128, 128))).astype(jnp.int32)


def main_kernel(
    slow_ref, rigid_ref, damp_ref, level_ref, live_ref, target_ref,
    table_hbm, offsets_hbm, levels_hbm, moduli_hbm, old_hbm, now_hbm,
    last_hbm, prior_hbm, half_hbm, side_hbm, corner_hbm, spread_hbm,
    field, mod, half, side_out, side_in, corner, hot, gathered, basis, spread,
    table, slot_tile, zbuf, ebuf, dbuf, kbuf,
    load_sem, store_sem, group_sem, send_sem, recv_sem, gsend_sem, grecv_sem,
):
    gx = lax.axis_index("gx")
    gy = lax.axis_index("gy")
    device = gx * GY + gy
    px, pz = gx // 4, gx % 4
    py, core = gy // 2, gy % 2
    block = core * 64 + px * 16 + pz * 4 + py

    loads = [
        pltpu.make_async_copy(now_hbm, field.at[0], load_sem.at[0]),
        pltpu.make_async_copy(old_hbm, field.at[1], load_sem.at[1]),
        pltpu.make_async_copy(moduli_hbm, mod, load_sem.at[2]),
        pltpu.make_async_copy(
            offsets_hbm.at[pl.ds(pl.multiple_of(device // 4 * 8, 8), 8)], slot_tile.at[0], load_sem.at[3]
        ),
        pltpu.make_async_copy(
            levels_hbm.at[pl.ds(pl.multiple_of(device // 4 * 8, 8), 8)], slot_tile.at[1], load_sem.at[4]
        ),
        pltpu.make_async_copy(table_hbm, table, load_sem.at[5]),
    ]
    for load in loads:
        load.start()

    for p in range(2):
        half[p, :, 0:2] = jnp.zeros((3, 2, C, NZ), BF)
        half[p, :, C + 2 : C + 4] = jnp.zeros((3, 2, C, NZ), BF)
        corner[p] = jnp.zeros(corner.shape[1:], BF)
        for s in range(2):
            side_in[p, s] = jnp.zeros(side_in.shape[2:], BF)

    steps = [(1, 0), (-1, 0), (0, 1), (0, -1), (1, 1), (1, -1), (-1, 1), (-1, -1)]

    def exists(dx, dy):
        ok = None
        for delta, place, size in ((dx, gx, GX), (dy, gy, GY)):
            if delta == 1:
                part = place < size - 1
            elif delta == -1:
                part = place > 0
            else:
                continue
            ok = part if ok is None else jnp.logical_and(ok, part)
        return ok

    barrier = pltpu.get_barrier_semaphore()
    for dx, dy in steps:
        @pl.when(exists(dx, dy))
        def _():
            pl.semaphore_signal(barrier, inc=1, device_id=(gx + dx, gy + dy), device_id_type=MESH)

    def ring_y(k):
        return (gx, (py + k) % 4 * 2 + core)

    def ring_z(k):
        return (px * 4 + (pz + k) % 4, gy)

    def ring_x(k):
        return ((px + k) % 4 * 4 + pz, gy)

    for ring in (ring_y, ring_z, ring_x):
        for k in (1, 2, 3):
            pl.semaphore_signal(barrier, inc=1, device_id=ring(k), device_id_type=MESH)
    twin = (gx, py * 2 + 1 - core)
    pl.semaphore_signal(barrier, inc=1, device_id=twin, device_id_type=MESH)

    rows = lax.broadcasted_iota(jnp.int32, (8, 128), 0) + block * 8
    wavenum = (rows.astype(F32) + 0.5) * (4.0 / NK)
    square_k = wavenum * wavenum
    omega = (lax.broadcasted_iota(jnp.int32, (8, 128), 1) + 1).astype(F32) * (4.0 / F)

    def downward(i, carry):
        down_re, down_im = carry
        layer = level_ref[i]
        part = omega * slow_ref[layer]
        vertical = jnp.sqrt(square_k + part * part)
        fade = jnp.exp(vertical * (-0.25 * damp_ref[layer]))
        angle = 0.125 * vertical
        s, c = sine(angle), cosine(angle)
        leg_re = fade * (1.0 - 2.0 * s * s)
        leg_im = fade * (-2.0 * s * c)
        zbuf[i] = rigid_ref[layer] * vertical
        ebuf[0, i] = leg_re
        ebuf[1, i] = leg_im
        dbuf[0, i] = down_re
        dbuf[1, i] = down_im
        return down_re * leg_re - down_im * leg_im, down_re * leg_im + down_im * leg_re

    one = jnp.ones((8, 128), F32)
    zero = jnp.zeros((8, 128), F32)
    lax.fori_loop(0, ND, downward, (one, zero), unroll=4)
    zbuf[ND] = zbuf[ND - 1]

    def upward(step, carry):
        refl_re, refl_im = carry
        i = ND - 1 - step
        upper, under = zbuf[i], zbuf[i + 1]
        r = (upper - under) / (upper + under)
        leg_re, leg_im = ebuf[0, i], ebuf[1, i]
        trip_re = leg_re * leg_re - leg_im * leg_im
        trip_im = 2.0 * leg_re * leg_im
        upper_re = r + refl_re
        lower_re = 1.0 + r * refl_re
        lower_im = r * refl_im
        scale = 1.0 / (lower_re * lower_re + lower_im * lower_im)
        ratio_re = (upper_re * lower_re + refl_im * lower_im) * scale
        ratio_im = (refl_im * lower_re - upper_re * lower_im) * scale
        fresh_re = trip_re * ratio_re - trip_im * ratio_im
        fresh_im = trip_re * ratio_im + trip_im * ratio_re
        down_re, down_im = dbuf[0, i], dbuf[1, i]
        kbuf[i, :, 0:128] = (down_re * (1.0 + fresh_re) - down_im * fresh_im) * (1.0 / 32.0)
        kbuf[i, :, 128:256] = (down_re * fresh_im + down_im * (1.0 + fresh_re)) * (1.0 / 32.0)
        return fresh_re, fresh_im

    lax.fori_loop(0, ND, upward, (zero, zero), unroll=4)
    loads[5].wait()
    product = dot(kbuf[...].reshape(ND * 8, 2 * F).astype(BF), table[AT_WAVES : AT_WAVES + 2 * F])
    product = product[:, :128] + product[:, 128:]
    lane = lax.broadcasted_iota(jnp.int32, (8, 128), 1) % ND
    mine = zero
    for d in range(ND):
        mine = jnp.where(lane == d, product[8 * d : 8 * d + 8], mine)
    gathered[block] = mine

    count = 10
    for dx, dy in steps:
        count = count + exists(dx, dy).astype(jnp.int32)
    pl.semaphore_wait(barrier, count)

    def stage(index, ring, start, size):
        copies = []
        for k in (1, 2, 3):
            piece = gathered.at[pl.ds(start, size)]
            copies.append(
                pltpu.make_async_remote_copy(
                    src_ref=piece,
                    dst_ref=piece,
                    send_sem=gsend_sem.at[3 * index + k - 1],
                    recv_sem=grecv_sem.at[3 * index + k - 1],
                    device_id=ring(k),
                    device_id_type=MESH,
                )
            )
        for copy in copies:
            copy.start()
        return copies

    def finish(copies):
        for copy in copies:
            copy.wait()

    stage_y = stage(0, ring_y, block, 1)

    batches = [(6, 2), (0, 3), (3, 3)]

    def message(n, index):
        p = n % 2
        if index < 2:
            move = (1, 0) if index == 0 else (-1, 0)
            source = half.at[p, :, pl.ds(C if index == 0 else 2, 2)]
            target = half.at[p, :, pl.ds(0 if index == 0 else C + 2, 2)]
        elif index < 6:
            move = (1 if index < 4 else -1, 1 if index % 2 == 0 else -1)
            source = half.at[
                p, pl.ds(0, 2), C + 1 if move[0] == 1 else 2, pl.ds(16 if move[1] == 1 else 0, 16)
            ]
            target = corner.at[p, 0 if move[0] == 1 else 2, 0 if move[1] == 1 else 1]
        else:
            s, (first, size) = (index - 6) // 3, batches[(index - 6) % 3]
            move = (0, 1) if s == 0 else (0, -1)
            source = side_out.at[p, s, pl.ds(first, size)]
            target = side_in.at[p, s, pl.ds(first, size)]
        copy = pltpu.make_async_remote_copy(
            src_ref=source,
            dst_ref=target,
            send_sem=send_sem.at[n, index],
            recv_sem=recv_sem.at[n, index],
            device_id=(gx + move[0], gy + move[1]),
            device_id_type=MESH,
        )
        return copy, exists(*move), exists(-move[0], -move[1])

    def start(n, *indices):
        for index in indices:
            copy, there, _ = message(n, index)

            @pl.when(there)
            def _():
                copy.start()

    def arrive(n, *indices):
        for index in indices:
            copy, _, here = message(n, index)

            @pl.when(here)
            def _():
                copy.wait_recv()

    def sent(n):
        for index in range(LINKS):
            copy, there, _ = message(n, index)

            @pl.when(there)
            def _():
                copy.wait_send()

    def kind_of(g):
        return jnp.where(g == 0, 0, jnp.where(g == GROUPS - 1, 2, 1))

    def fill(n, first, size):
        p = n % 2

        def one_tile(g, carry):
            kind = kind_of(g)
            x = jnp.where(g == 0, 0, jnp.where(g == GROUPS - 1, C - 6, g * XG - 1))
            pick = table[pl.ds(pl.multiple_of(AT_PICK + 32 * kind, 32), 32), : 6 * C]
            for c in range(3):
                tile = dot(pick, half[p, c, pl.ds(x + 2, 6)].reshape(6 * C, NZ)).astype(BF)
                side_out[p, 0, g, c] = tile[:16]
                side_out[p, 1, g, c] = tile[16:]
            return carry

        lax.fori_loop(first, first + size, one_tile, 0)

    def group_at(i):
        return jnp.where(i < 3, GROUPS - 1 - i, i - 3)

    def publish(n, i):
        @pl.when(i == 0)
        def _():
            start(n, 0, 2, 3)

        @pl.when(i == 2)
        def _():
            fill(n, *batches[0])
            start(n, 6, 9)

        @pl.when(i == 3)
        def _():
            start(n, 1, 4, 5)

        @pl.when(i == 6)
        def _():
            fill(n, *batches[1])
            start(n, 7, 10)

        @pl.when(i == 7)
        def _():
            fill(n, *batches[2])
            start(n, 8, 11)

    def receive(n, i):
        @pl.when(i == 0)
        def _():
            arrive(n, 1, 4, 5, 6, 9)

        @pl.when(i == 2)
        def _():
            arrive(n, 8, 11)

        @pl.when(i == 3)
        def _():
            arrive(n, 0, 2, 3, 7, 10)

    def update(n, g, sources):
        p = n % 2
        x = g * XG
        kind = kind_of(g)
        return advance(
            [half[p, c, pl.ds(x, XG + 4)] for c in range(3)],
            [side_in[p, 0, g, c] for c in range(3)],
            [side_in[p, 1, g, c] for c in range(3)],
            [corner[p, kind, 0, c] for c in range(2)],
            [corner[p, kind, 1, c] for c in range(2)],
            [field[p, c, pl.ds(x, XG)].reshape(ROWS, NZ) for c in range(3)],
            [field[1 - p, c, pl.ds(x, XG)].reshape(ROWS, NZ) for c in range(3)],
            mod[0, pl.ds(x, XG)].reshape(ROWS, NZ),
            mod[1, pl.ds(x, XG)].reshape(ROWS, NZ),
            sources,
            *matrices(table, kind),
        )

    def injected(n, g):
        values = dot(hot[g].reshape(3 * ROWS, Q), spread[n])
        return [values[ROWS * c : ROWS * c + ROWS] for c in range(3)]

    def keep(n, g, c, fresh):
        x = g * XG
        fresh = fresh.reshape(XG, C, NZ)
        field[n % 2, c, pl.ds(x, XG)] = fresh
        half[n % 2, c, pl.ds(x + 2, XG)] = fresh.astype(BF)

    def to_half(g, carry):
        x = g * XG
        for c in range(3):
            half[0, c, pl.ds(x + 2, XG)] = field[0, c, pl.ds(x, XG)].astype(BF)
        return carry

    loads[0].wait()
    lax.fori_loop(0, GROUPS, to_half, 0)
    start(0, 0, 1, 2, 3, 4, 5)
    fill(0, 0, GROUPS)
    start(0, 6, 7, 8, 9, 10, 11)
    finish(stage_y)
    stage_z = stage(1, ring_z, block // 4 * 4, 4)

    loads[3].wait()
    loads[4].wait()
    row = device % 4 * 2
    mask = NK * NR // 2 - 1
    for h in range(2):
        part = pl.ds(128 * h, 128)
        q = lane_spread(slot_tile[0, pl.ds(row + h, 1)])
        lanes = lax.broadcasted_iota(jnp.int32, (128, 128), 1)
        for b in range(NK // 128):
            turns = (2 * (lanes + 128 * b) + 1) * q
            turns = ((turns + (mask + 1) // 2) & mask) - (mask + 1) // 2
            s = sine(turns.astype(F32) * (math.pi / (mask + 1)))
            basis[part, 128 * b : 128 * b + 128] = (1.0 - 2.0 * s * s).astype(BF)
    finish(stage_z)
    stage_x = stage(2, ring_x, block // 16 * 16, 16)

    def build_hot(g, carry):
        ids = lax.broadcasted_iota(jnp.int32, (ROWS, Q), 0) + g * ROWS
        columns = target_ref[...] // NZ
        for c in range(3):
            same = ids + c * C * C == columns
            hot[g, c] = jnp.where(same, 1.0, 0.0).astype(BF)
        return carry

    lax.fori_loop(0, GROUPS, build_hot, 0)
    loads[1].wait()
    loads[2].wait()
    whole = gathered.at[pl.ds(core * 64, 64)]
    swap = pltpu.make_async_remote_copy(
        src_ref=whole,
        dst_ref=whole,
        send_sem=gsend_sem.at[9],
        recv_sem=grecv_sem.at[9],
        device_id=twin,
        device_id_type=MESH,
    )

    def first_step(i, carry):
        receive(0, i)

        @pl.when(i == 4)
        def _():
            finish(stage_x)
            swap.start()

        g = group_at(i)
        result = update(0, g, None)
        for c in range(3):
            field[1, c, pl.ds(g * XG, XG)] = result[c].reshape(XG, C, NZ)
        return carry

    lax.fori_loop(0, GROUPS, first_step, 0)
    swap.wait()

    total = gathered[...].reshape(NK, 128)
    upper = total.astype(BF)
    lower = (total - upper.astype(F32)).astype(BF)
    picked = dot(basis[...], jnp.concatenate([upper, lower], axis=1))
    picked = picked[:, :128] + picked[:, 128:]
    ones = jnp.ones((128, NZ), BF)
    for h in range(2):
        part = slice(128 * h, 128 * h + 128)
        lanes = lax.broadcasted_iota(jnp.int32, (128, 128), 1)
        ids = lax.broadcasted_iota(jnp.int32, (128, 128), 0) + 128 * h
        level = lane_spread(slot_tile[1, pl.ds(row + h, 1)])
        live = jnp.logical_and(lanes % ND == level, ids < live_ref[0])
        chosen = jnp.where(live, picked[part], 0.0)
        depth = lane_spread(target_ref[:, 128 * h : 128 * h + 128] % NZ)
        for n in range(STEPS):
            values = dot(jnp.where(lanes // ND == n, chosen, 0.0).astype(BF), ones)
            for b in range(2):
                same = lanes + 128 * b == depth
                spread[n, part, 128 * b : 128 * b + 128] = jnp.where(
                    same, values[:, 128 * b : 128 * b + 128], 0.0
                ).astype(BF)

    def first_sources(i, carry):
        g = group_at(i)
        sources = injected(0, g)
        for c in range(3):
            keep(1, g, c, field[1, c, pl.ds(g * XG, XG)].reshape(ROWS, NZ) + sources[c])
        publish(1, i)
        return carry

    lax.fori_loop(0, GROUPS, first_sources, 0)

    spread_store = pltpu.make_async_copy(spread.at[STEPS - 1], spread_hbm, store_sem.at[0])
    spread_store.start()
    prior_store = pltpu.make_async_copy(field.at[0], prior_hbm, store_sem.at[1])

    def last_stores(g):
        x = g * XG
        return (
            pltpu.make_async_copy(
                field.at[1, :, pl.ds(x, XG)], last_hbm.at[:, pl.ds(x, XG)], group_sem.at[0, g]
            ),
            pltpu.make_async_copy(
                half.at[1, :, pl.ds(x + 2, XG)], half_hbm.at[:, pl.ds(x + 2, XG)], group_sem.at[1, g]
            ),
        )

    for n in range(1, STEPS - 1):
        sent(n - 1)
        if n == STEPS - 2:
            prior_store.start()

        def later_step(i, carry):
            receive(n, i)
            g = group_at(i)
            result = update(n, g, injected(n, g))
            for c in range(3):
                keep(n + 1, g, c, result[c])
            publish(n + 1, i)
            if n == STEPS - 2:
                for store in last_stores(g):
                    store.start()
            return carry

        lax.fori_loop(0, GROUPS, later_step, 0)

    last = STEPS - 1
    arrive(last, 0, 1)
    ends = [
        pltpu.make_async_copy(half.at[1, :, pl.ds(x, 2)], half_hbm.at[:, pl.ds(x, 2)], store_sem.at[k])
        for x, k in ((0, 2), (C + 2, 3))
    ]
    for store in ends:
        store.start()
    arrive(last, 2, 3, 4, 5)
    corner_store = pltpu.make_async_copy(corner.at[1], corner_hbm, store_sem.at[4])
    corner_store.start()
    arrive(last, 6, 7, 8, 9, 10, 11)
    side_store = pltpu.make_async_copy(side_in.at[1], side_hbm, store_sem.at[5])
    side_store.start()
    sent(last - 1)
    sent(last)
    for store in (spread_store, prior_store, *ends, corner_store, side_store):
        store.wait()

    def drain(g, carry):
        for store in last_stores(g):
            store.wait()
        return carry

    lax.fori_loop(0, GROUPS, drain, 0)


def last_kernel(
    target_ref,
    table_hbm, half_hbm, side_hbm, corner_hbm, spread_hbm, now_hbm, before_hbm, moduli_hbm,
    final_hbm, copy_hbm,
    table, half, side, corner, spread, now, before, mod, final,
    sem, half_sem, load_sem, store_sem,
):
    small = [
        pltpu.make_async_copy(source, target, sem.at[k])
        for k, (source, target) in enumerate(
            (
                (table_hbm.at[pl.ds(0, SHORT)], table),
                (spread_hbm, spread),
                (side_hbm, side),
                (corner_hbm, corner),
            )
        )
    ]

    def half_load(k):
        x = k * XG
        return pltpu.make_async_copy(half_hbm.at[:, pl.ds(x, XG)], half.at[:, pl.ds(x, XG)], half_sem.at[k])

    def group_loads(g):
        part = pl.ds(g * XG, XG)
        return [
            pltpu.make_async_copy(source.at[:, part], target.at[:, part], load_sem.at[k, g])
            for k, (source, target) in enumerate(
                ((now_hbm, now), (before_hbm, before), (moduli_hbm, mod))
            )
        ]

    def group_stores(g):
        part = pl.ds(g * XG, XG)
        return [
            pltpu.make_async_copy(source.at[:, part], target.at[:, part], store_sem.at[k, g])
            for k, (source, target) in enumerate(((final, final_hbm), (now, copy_hbm)))
        ]

    half_load(0).start()
    for load in small:
        load.start()

    def begin(g, carry):
        half_load(g + 1).start()
        for load in group_loads(g):
            load.start()
        return carry

    lax.fori_loop(0, GROUPS, begin, 0)
    half_load(0).wait()
    for load in small:
        load.wait()

    def group(g, carry):
        x = g * XG
        half_load(g + 1).wait()
        for load in group_loads(g):
            load.wait()
        stores = group_stores(g)
        stores[1].start()
        kind = jnp.where(g == 0, 0, jnp.where(g == GROUPS - 1, 2, 1))
        ids = lax.broadcasted_iota(jnp.int32, (ROWS, Q), 0) + g * ROWS
        columns = target_ref[...] // NZ
        hot = [jnp.where(ids + c * C * C == columns, 1.0, 0.0).astype(BF) for c in range(3)]
        values = dot(below(*hot), spread[...])
        result = advance(
            [half[c, pl.ds(x, XG + 4)] for c in range(3)],
            [side[0, g, c] for c in range(3)],
            [side[1, g, c] for c in range(3)],
            [corner[kind, 0, c] for c in range(2)],
            [corner[kind, 1, c] for c in range(2)],
            [now[c, pl.ds(x, XG)].reshape(ROWS, NZ) for c in range(3)],
            [before[c, pl.ds(x, XG)].reshape(ROWS, NZ) for c in range(3)],
            mod[0, pl.ds(x, XG)].reshape(ROWS, NZ),
            mod[1, pl.ds(x, XG)].reshape(ROWS, NZ),
            [values[ROWS * c : ROWS * c + ROWS] for c in range(3)],
            *matrices(table, kind),
        )
        for c in range(3):
            final[c, pl.ds(x, XG)] = result[c].reshape(XG, C, NZ)
        stores[0].start()
        return carry

    lax.fori_loop(0, GROUPS, group, 0)

    def drain(g, carry):
        for store in group_stores(g):
            store.wait()
        return carry

    lax.fori_loop(0, GROUPS, drain, 0)


def shards(
    layer_slowness, layer_rigidity, layer_damping, layer_of_level,
    slot_offset, slot_level, slot_target, live_count, moduli, field_old, field_now,
):
    fixed = jnp.asarray(constants())
    smem = pl.BlockSpec(memory_space=pltpu.SMEM)
    vmem = pl.BlockSpec(memory_space=pltpu.VMEM)
    any_space = pl.BlockSpec(memory_space=pl.ANY)
    target = slot_target.reshape(1, Q)
    block = jax.ShapeDtypeStruct((3, C, C, NZ), F32)
    dma = pltpu.SemaphoreType.DMA
    last, prior, half, side, corner, spread = pl.pallas_call(
        main_kernel,
        out_shape=[
            block,
            block,
            jax.ShapeDtypeStruct((3, C + 4, C, NZ), BF),
            jax.ShapeDtypeStruct((2, GROUPS, 3, 16, NZ), BF),
            jax.ShapeDtypeStruct((3, 2, 2, 16, NZ), BF),
            jax.ShapeDtypeStruct((Q, NZ), BF),
        ],
        in_specs=[smem] * 5 + [vmem] + [any_space] * 6,
        out_specs=[any_space] * 6,
        scratch_shapes=[
            pltpu.VMEM((2, 3, C, C, NZ), F32),
            pltpu.VMEM((2, C, C, NZ), F32),
            pltpu.VMEM((2, 3, C + 4, C, NZ), BF),
            pltpu.VMEM((2, 2, GROUPS, 3, 16, NZ), BF),
            pltpu.VMEM((2, 2, GROUPS, 3, 16, NZ), BF),
            pltpu.VMEM((2, 3, 2, 2, 16, NZ), BF),
            pltpu.VMEM((GROUPS, 3, ROWS, Q), BF),
            pltpu.VMEM((NK // 8, 8, 128), F32),
            pltpu.VMEM((Q, NK), BF),
            pltpu.VMEM((STEPS, Q, NZ), BF),
            pltpu.VMEM((TABLE, NZ), BF),
            pltpu.VMEM((2, 8, 128), jnp.int32),
            pltpu.VMEM((ND + 1, 8, 128), F32),
            pltpu.VMEM((2, ND, 8, 128), F32),
            pltpu.VMEM((2, ND, 8, 128), F32),
            pltpu.VMEM((ND, 8, 2 * F), F32),
            dma((6,)),
            dma((6,)),
            dma((2, GROUPS)),
            dma((STEPS, LINKS)),
            dma((STEPS, LINKS)),
            dma((10,)),
            dma((10,)),
        ],
        compiler_params=pltpu.CompilerParams(
            collective_id=0, has_side_effects=True, vmem_limit_bytes=VMEM
        ),
    )(
        layer_slowness, layer_rigidity, layer_damping, layer_of_level, live_count, target,
        fixed,
        slot_offset.reshape(Q, 128), slot_level.reshape(Q, 128), moduli, field_old, field_now,
    )

    return pl.pallas_call(
        last_kernel,
        out_shape=[block, block],
        in_specs=[vmem] + [any_space] * 8,
        out_specs=[any_space] * 2,
        scratch_shapes=[
            pltpu.VMEM((SHORT, NZ), BF),
            pltpu.VMEM(half.shape, BF),
            pltpu.VMEM(side.shape, BF),
            pltpu.VMEM(corner.shape, BF),
            pltpu.VMEM(spread.shape, BF),
            pltpu.VMEM((3, C, C, NZ), F32),
            pltpu.VMEM((3, C, C, NZ), F32),
            pltpu.VMEM((2, C, C, NZ), F32),
            pltpu.VMEM((3, C, C, NZ), F32),
            dma((4,)),
            dma((GROUPS + 1,)),
            dma((3, GROUPS)),
            dma((2, GROUPS)),
        ],
        compiler_params=pltpu.CompilerParams(vmem_limit_bytes=VMEM),
    )(target, fixed, half, side, corner, spread, last, prior, moduli)


def solution(mesh):
    in_specs = (
        P(),
        P(),
        P(),
        P(),
        P(),
        P(),
        P(("gx", "gy")),
        P(("gx", "gy")),
        P(None, "gx", "gy", None),
        P(None, "gx", "gy", None),
        P(None, "gx", "gy", None),
    )
    out_specs = (P(None, "gx", "gy", None), P(None, "gx", "gy", None))
    return jax.shard_map(shards, mesh=mesh, in_specs=in_specs, out_specs=out_specs, check_vma=False)
```

```python
import functools
import math

import jax
import jax.numpy as jnp
import ml_dtypes
import numpy as np
from jax import lax
from jax.experimental import pallas as pl
from jax.experimental.pallas import tpu as pltpu
from jax.sharding import PartitionSpec as P

F = 128
NK = 1024
NR = 2048
ND = 32
STEPS = 4
TSTART = 32
GX = 16
GY = 8
C = 32
NZ = 256
Q = 256
GROUPS = 8
XG = 4
ROWS = XG * C
LINKS = 12
VMEM = 63 * 1024 * 1024
MESH = pl.DeviceIdType.MESH
BF = jnp.bfloat16
F32 = jnp.float32


def constants():
    low, high = ROWS, ROWS + 16

    def place(x, y, kind):
        if y < 0:
            return low + 8 * (y + 2) + x + (0, 1, 4)[kind]
        if y >= C:
            return high + 8 * (y - C) + x + (0, 1, 4)[kind]
        return x * C + y

    y2 = np.zeros((3, ROWS, ROWS + 32), np.float32)
    y1 = np.zeros((3, ROWS, ROWS + 32), np.float32)
    cross = np.zeros((3, ROWS, ROWS + 96), np.float32)
    for kind in range(3):
        for x in range(XG):
            for y in range(C):
                row = x * C + y
                for shift, factor in ((-2, -1.0), (-1, 16.0), (1, 16.0), (2, -1.0)):
                    y2[kind, row, place(x, y + shift, kind)] += factor
                y1[kind, row, place(x, y + 1, kind)] += 1.0
                y1[kind, row, place(x, y - 1, kind)] -= 1.0
        cross[kind, :, :ROWS] = 3.0 * y1[kind, :, :ROWS]
        cross[kind, :, ROWS + 64 :] = 3.0 * y1[kind, :, ROWS:]
        for x in range(XG):
            for y, beyond, sign in ((0, -1, -3.0), (C - 1, C, 3.0)):
                for step in (-1, 1):
                    outside = (kind == 0 and x + step < 0) or (kind == 2 and x + step >= XG)
                    if outside:
                        spot = ROWS + 32 + 15 if beyond < 0 else ROWS + 48
                    else:
                        spot = place(x + step, beyond, kind)
                    cross[kind, x * C + y, spot] += sign * step
    z2 = np.zeros((NZ, NZ), np.float32)
    z1 = np.zeros((NZ, NZ), np.float32)
    for z in range(NZ):
        for shift, factor in ((-2, -1.0), (-1, 16.0), (1, 16.0), (2, -1.0)):
            if 0 <= z + shift < NZ:
                z2[z + shift, z] += factor
        if z + 1 < NZ:
            z1[z + 1, z] += 1.0
        if z > 0:
            z1[z - 1, z] -= 1.0
    period = 2 * F
    turns = (np.arange(F)[None, :] + 1) * (TSTART + np.arange(STEPS)[:, None]) % period
    angles = turns * (2.0 * math.pi / period)
    weight = 1.0 / math.sqrt(F)
    waves = np.concatenate([weight * np.cos(angles), -weight * np.sin(angles)], axis=1).T
    waves = np.repeat(waves.astype(np.float32), ND, axis=1)
    upper = waves.astype(ml_dtypes.bfloat16)
    lower = (waves - upper.astype(np.float32)).astype(ml_dtypes.bfloat16)
    half = ml_dtypes.bfloat16
    parts = [*y2, *y1, *cross, z2, z1, 3.0 * z1]
    parts = [np.pad(part, ((0, 0), (0, 256 - part.shape[1]))).astype(half) for part in parts]
    return np.concatenate(parts + [np.concatenate([upper, lower], axis=1)])


AT_Y2, AT_Y1, AT_CROSS, AT_Z2, AT_Z1, AT_Z3 = 0, 384, 768, 1152, 1408, 1664
AT_WAVES, TABLE = 1920, 2176
SHORT = AT_WAVES


def matrices(table, kind):
    def part(at):
        return table[pl.ds(pl.multiple_of(at + ROWS * kind, ROWS), ROWS)]

    return (
        part(AT_Y2)[:, : ROWS + 32],
        part(AT_Y1)[:, : ROWS + 32],
        part(AT_CROSS),
        table[AT_Z2 : AT_Z2 + NZ],
        table[AT_Z1 : AT_Z1 + NZ],
        table[AT_Z3 : AT_Z3 + NZ],
    )


def rows_at(g):
    return pl.ds(pl.multiple_of(g * ROWS, ROWS), ROWS)


def dot(a, b):
    return jnp.dot(a, b, preferred_element_type=F32)


def beside(*parts):
    return jnp.concatenate(parts, axis=1)


def below(*parts):
    return jnp.concatenate(parts, axis=0)


def advance(window, lows, highs, clows, chighs, now, before, lam, mu, sources, y2, y1, cross, z2, z1, z3):
    wide = [w.astype(F32) for w in window]
    inner = [w[2 : 2 + XG].reshape(ROWS, NZ) for w in window]
    second = [(16.0 * (w[1:5] + w[3:7]) - (w[0:4] + w[4:8])).reshape(ROWS, NZ) for w in wide]
    first = [(w[3:7] - w[1:5]).reshape(ROWS, NZ) for w in wide]
    tall = [below(inner[c], lows[c], highs[c]) for c in range(3)]
    skew_z = dot(tall[2], z1)
    skew_y = dot(y1, tall[1])
    lap = [dot(beside(inner[c], y2), below(z2, tall[c])) for c in range(3)]
    mix_0 = dot(
        beside(first[2].astype(BF), cross[:, : ROWS + 64]),
        below(z3, first[1].astype(BF), lows[1], highs[1], clows[1], chighs[1]),
    )
    mix_1 = dot(
        beside(cross, y2),
        below(
            (first[0] + skew_z[:ROWS]).astype(BF), lows[0], highs[0], clows[0], chighs[0],
            skew_z[ROWS:].astype(BF), lows[0], highs[0], tall[1],
        ),
    )
    mix_2 = dot(beside(inner[2], (first[0] + skew_y).astype(BF)), below(z2, z3))
    couple = [second[0] + mix_0, mix_1, mix_2]
    shear = mu * (1.0 / 12.0)
    joint = (lam + mu) * (1.0 / 12.0)
    centre = 2.0 - 90.0 * shear - 30.0 * joint
    result = []
    for c in range(3):
        moved = shear * (second[c] + lap[c]) + joint * couple[c]
        if sources is not None:
            moved = moved + sources[c]
        result.append((centre * now[c] - before[c]) + moved)
    return result


def sine(x):
    y = x * x
    poly = -2.5052108e-08
    for coefficient in (2.7557319e-06, -1.9841270e-04, 8.3333333e-03, -1.6666667e-01, 1.0):
        poly = poly * y + coefficient
    return x * poly


def cosine(x):
    y = x * x
    poly = -2.7557319e-07
    for coefficient in (2.4801587e-05, -1.3888889e-03, 4.1666667e-02, -0.5, 1.0):
        poly = poly * y + coefficient
    return poly


def lane_spread(row):
    return jnp.transpose(jnp.broadcast_to(row.astype(F32), (128, 128))).astype(jnp.int32)


def main_kernel(
    slow_ref, rigid_ref, damp_ref, level_ref, live_ref, target_ref,
    table_hbm, offsets_hbm, levels_hbm, moduli_hbm, old_hbm, now_hbm,
    last_hbm, prior_hbm, half_hbm, side_hbm, corner_hbm, spread_hbm,
    field, mod, half, side_out, side_in, corner, hot, gathered, basis, spread,
    depth_hot, part_out, part_in,
    table, slot_tile, zbuf, ebuf, dbuf, kbuf,
    load_sem, store_sem, group_sem, send_sem, recv_sem, gsend_sem, grecv_sem,
    slot_sem, rsend_sem, rrecv_sem,
):
    gx = lax.axis_index("gx")
    gy = lax.axis_index("gy")
    device = gx * GY + gy
    px, pz = gx // 4, gx % 4
    py, core = gy // 2, gy % 2
    block = core * 64 + px * 16 + pz * 4 + py

    loads = [
        pltpu.make_async_copy(now_hbm, field.at[0], load_sem.at[0]),
        pltpu.make_async_copy(old_hbm, field.at[1], load_sem.at[1]),
        pltpu.make_async_copy(moduli_hbm, mod, load_sem.at[2]),
        pltpu.make_async_copy(table_hbm, table, load_sem.at[3]),
    ]
    slot_loads = []
    for x in range(4):
        at = pl.ds(pl.multiple_of(x * 64 + pz * 16 + py // 2 * 8, 8), 8)
        for k, ref in enumerate((offsets_hbm, levels_hbm)):
            slot_loads.append(pltpu.make_async_copy(ref.at[at], slot_tile.at[k, x], slot_sem.at[k, x]))
    for load in loads[:1] + slot_loads + loads[3:] + loads[1:3]:
        load.start()

    for p in range(2):
        half[p, :, 0:2] = jnp.zeros((3, 2, C, NZ), BF)
        half[p, :, C + 2 : C + 4] = jnp.zeros((3, 2, C, NZ), BF)
        corner[p] = jnp.zeros(corner.shape[1:], BF)
        for s in range(2):
            side_in[p, s] = jnp.zeros(side_in.shape[2:], BF)

    steps = [(1, 0), (-1, 0), (0, 1), (0, -1), (1, 1), (1, -1), (-1, 1), (-1, -1)]

    def exists(dx, dy):
        ok = None
        for delta, place, size in ((dx, gx, GX), (dy, gy, GY)):
            if delta == 1:
                part = place < size - 1
            elif delta == -1:
                part = place > 0
            else:
                continue
            ok = part if ok is None else jnp.logical_and(ok, part)
        return ok

    barrier = pltpu.get_barrier_semaphore()
    for dx, dy in steps:
        @pl.when(exists(dx, dy))
        def _():
            pl.semaphore_signal(barrier, inc=1, device_id=(gx + dx, gy + dy), device_id_type=MESH)

    def in_plane(k):
        return (px * 4 + (pz + k // 4) % 4, (py + k % 4) % 4 * 2 + core)

    def owner(k):
        return ((px + k // 2) % 4 * 4 + pz, py * 2 + (core + k) % 2)

    for k in range(1, 16):
        pl.semaphore_signal(barrier, inc=1, device_id=in_plane(k), device_id_type=MESH)
    for k in range(1, 8):
        pl.semaphore_signal(barrier, inc=1, device_id=owner(k), device_id_type=MESH)

    rows = lax.broadcasted_iota(jnp.int32, (8, 128), 0) + block * 8
    wavenum = (rows.astype(F32) + 0.5) * (4.0 / NK)
    square_k = wavenum * wavenum
    omega = (lax.broadcasted_iota(jnp.int32, (8, 128), 1) + 1).astype(F32) * (4.0 / F)

    def downward(i, carry):
        down_re, down_im = carry
        layer = level_ref[i]
        part = omega * slow_ref[layer]
        vertical = jnp.sqrt(square_k + part * part)
        fade = jnp.exp(vertical * (-0.25 * damp_ref[layer]))
        angle = 0.125 * vertical
        s, c = sine(angle), cosine(angle)
        leg_re = fade * (1.0 - 2.0 * s * s)
        leg_im = fade * (-2.0 * s * c)
        zbuf[i] = rigid_ref[layer] * vertical
        ebuf[0, i] = leg_re
        ebuf[1, i] = leg_im
        dbuf[0, i] = down_re
        dbuf[1, i] = down_im
        return down_re * leg_re - down_im * leg_im, down_re * leg_im + down_im * leg_re

    one = jnp.ones((8, 128), F32)
    zero = jnp.zeros((8, 128), F32)
    lax.fori_loop(0, ND, downward, (one, zero), unroll=4)
    zbuf[ND] = zbuf[ND - 1]

    def upward(step, carry):
        refl_re, refl_im = carry
        i = ND - 1 - step
        upper, under = zbuf[i], zbuf[i + 1]
        r = (upper - under) / (upper + under)
        leg_re, leg_im = ebuf[0, i], ebuf[1, i]
        trip_re = leg_re * leg_re - leg_im * leg_im
        trip_im = 2.0 * leg_re * leg_im
        upper_re = r + refl_re
        lower_re = 1.0 + r * refl_re
        lower_im = r * refl_im
        scale = 1.0 / (lower_re * lower_re + lower_im * lower_im)
        ratio_re = (upper_re * lower_re + refl_im * lower_im) * scale
        ratio_im = (refl_im * lower_re - upper_re * lower_im) * scale
        fresh_re = trip_re * ratio_re - trip_im * ratio_im
        fresh_im = trip_re * ratio_im + trip_im * ratio_re
        down_re, down_im = dbuf[0, i], dbuf[1, i]
        kbuf[i, :, 0:128] = (down_re * (1.0 + fresh_re) - down_im * fresh_im) * (1.0 / 32.0)
        kbuf[i, :, 128:256] = (down_re * fresh_im + down_im * (1.0 + fresh_re)) * (1.0 / 32.0)
        return fresh_re, fresh_im

    lax.fori_loop(0, ND, upward, (zero, zero), unroll=4)
    loads[3].wait()
    product = dot(kbuf[...].reshape(ND * 8, 2 * F).astype(BF), table[AT_WAVES : AT_WAVES + 2 * F])
    product = product[:, :128] + product[:, 128:]
    lane = lax.broadcasted_iota(jnp.int32, (8, 128), 1) % ND
    mine = zero
    for d in range(ND):
        mine = jnp.where(lane == d, product[8 * d : 8 * d + 8], mine)
    seat = pz * 4 + py
    gathered[seat] = mine

    count = 22
    for dx, dy in steps:
        count = count + exists(dx, dy).astype(jnp.int32)
    pl.semaphore_wait(barrier, count)

    gathers = [
        pltpu.make_async_remote_copy(
            src_ref=gathered.at[seat],
            dst_ref=gathered.at[seat],
            send_sem=gsend_sem.at[k],
            recv_sem=grecv_sem.at[k],
            device_id=in_plane(k),
            device_id_type=MESH,
        )
        for k in range(1, 16)
    ]
    for copy in gathers:
        copy.start()

    batches = [(6, 2), (0, 3), (3, 3)]

    def message(n, index):
        p = n % 2
        if index < 2:
            move = (1, 0) if index == 0 else (-1, 0)
            source = half.at[p, :, pl.ds(C if index == 0 else 2, 2)]
            target = half.at[p, :, pl.ds(0 if index == 0 else C + 2, 2)]
        elif index < 6:
            move = (1 if index < 4 else -1, 1 if index % 2 == 0 else -1)
            source = half.at[
                p, pl.ds(0, 2), C + 1 if move[0] == 1 else 2, pl.ds(16 if move[1] == 1 else 0, 16)
            ]
            target = corner.at[p, 0 if move[0] == 1 else 2, 0 if move[1] == 1 else 1]
        else:
            s, (first, size) = (index - 6) // 3, batches[(index - 6) % 3]
            move = (0, 1) if s == 0 else (0, -1)
            source = side_out.at[p, s, pl.ds(first, size)]
            target = side_in.at[p, s, pl.ds(first, size)]
        copy = pltpu.make_async_remote_copy(
            src_ref=source,
            dst_ref=target,
            send_sem=send_sem.at[n, index],
            recv_sem=recv_sem.at[n, index],
            device_id=(gx + move[0], gy + move[1]),
            device_id_type=MESH,
        )
        return copy, exists(*move), exists(-move[0], -move[1])

    def start(n, *indices):
        for index in indices:
            copy, there, _ = message(n, index)

            @pl.when(there)
            def _():
                copy.start()

    def arrive(n, *indices):
        for index in indices:
            copy, _, here = message(n, index)

            @pl.when(here)
            def _():
                copy.wait_recv()

    def sent(n):
        for index in range(LINKS):
            copy, there, _ = message(n, index)

            @pl.when(there)
            def _():
                copy.wait_send()

    def kind_of(g):
        return jnp.where(g == 0, 0, jnp.where(g == GROUPS - 1, 2, 1))

    def fill(n, first, size):
        p = n % 2

        def one_tile(g, carry):
            x = jnp.where(g == 0, 0, jnp.where(g == GROUPS - 1, C - 8, g * XG - 1))
            place = lax.broadcasted_iota(jnp.int32, (8, NZ), 0)
            for c in range(3):
                for s, y in ((0, C - 2), (1, 0)):
                    rows = [jnp.zeros((8, NZ), F32)] * 2
                    for i in range(8):
                        at = pl.multiple_of((x + i) * C + y // 8 * 8, 8)
                        tile = field[p, c, pl.ds(at, 8)]
                        for k in range(2):
                            line = jnp.broadcast_to(tile[y % 8 + k : y % 8 + k + 1], (8, NZ))
                            rows[k] = jnp.where(place == i, line, rows[k])
                    side_out[p, s, g, c] = below(*rows).astype(BF)
            return carry

        lax.fori_loop(first, first + size, one_tile, 0)

    def group_at(i):
        return jnp.where(i < 3, GROUPS - 1 - i, i - 3)

    def publish(n, i):
        @pl.when(i == 0)
        def _():
            start(n, 0, 2, 3)

        @pl.when(i == 2)
        def _():
            fill(n, *batches[0])
            start(n, 6, 9)

        @pl.when(i == 3)
        def _():
            start(n, 1, 4, 5)

        @pl.when(i == 6)
        def _():
            fill(n, *batches[1])
            start(n, 7, 10)

        @pl.when(i == 7)
        def _():
            fill(n, *batches[2])
            start(n, 8, 11)

    def receive(n, i):
        @pl.when(i == 0)
        def _():
            arrive(n, 1, 4, 5, 6, 9)

        @pl.when(i == 2)
        def _():
            arrive(n, 8, 11)

        @pl.when(i == 3)
        def _():
            arrive(n, 0, 2, 3, 7, 10)

    def update(n, g, sources):
        p = n % 2
        x = g * XG
        kind = kind_of(g)
        return advance(
            [half[p, c, pl.ds(x, XG + 4)] for c in range(3)],
            [side_in[p, 0, g, c] for c in range(3)],
            [side_in[p, 1, g, c] for c in range(3)],
            [corner[p, kind, 0, c] for c in range(2)],
            [corner[p, kind, 1, c] for c in range(2)],
            [field[p, c, rows_at(g)] for c in range(3)],
            [field[1 - p, c, rows_at(g)] for c in range(3)],
            mod[0, rows_at(g)],
            mod[1, rows_at(g)],
            sources,
            *matrices(table, kind),
        )

    def injected(n, g):
        values = dot(hot[g].reshape(3 * ROWS, Q), spread[n])
        return [values[ROWS * c : ROWS * c + ROWS] for c in range(3)]

    def keep(n, g, c, fresh):
        field[n % 2, c, rows_at(g)] = fresh
        half[n % 2, c, pl.ds(g * XG + 2, XG)] = fresh.astype(BF).reshape(XG, C, NZ)

    def to_half(g, carry):
        x = g * XG
        for c in range(3):
            half[0, c, pl.ds(x + 2, XG)] = field[0, c, rows_at(g)].astype(BF).reshape(XG, C, NZ)
        return carry

    loads[0].wait()
    lax.fori_loop(0, GROUPS, to_half, 0)
    start(0, 0, 1, 2, 3, 4, 5)
    fill(0, 0, GROUPS)
    start(0, 6, 7, 8, 9, 10, 11)

    for load in slot_loads:
        load.wait()
    first_row = py % 2 * 4
    mask = NK * NR // 2 - 1
    across = lax.broadcasted_iota(jnp.int32, (128, 128), 1)
    along = lax.broadcasted_iota(jnp.int32, (128, 128), 0)
    odd_index = 2 * (along + (core * 4 + px) * 128) + 1

    def cosines(t, carry):
        q = slot_tile[0, t // 4, pl.ds(first_row + t % 4, 1)]
        turns = odd_index * q
        turns = ((turns + (mask + 1) // 2) & mask) - (mask + 1) // 2
        s = sine(turns.astype(F32) * (math.pi / (mask + 1)))
        basis[t] = (1.0 - 2.0 * s * s).astype(BF)
        return carry

    lax.fori_loop(0, 16, cosines, 0)
    for copy in gathers:
        copy.wait()
    total = jnp.transpose(gathered[...].reshape(128, 128))
    upper = total.astype(BF)
    lower = (total - upper.astype(F32)).astype(BF)
    both = beside(upper, lower)

    def partial(u, carry):
        cos = beside(basis[2 * u], basis[2 * u + 1])
        sums = dot(both, below(cos, cos))
        row = first_row + u % 2 * 2
        level = beside(*[slot_tile[1, u // 2, pl.ds(row + h, 1)] for h in range(2)])
        depth = lax.broadcasted_iota(jnp.int32, (STEPS * ND, Q), 0) % ND
        sums = jnp.where(depth == level, sums, 0.0).reshape(STEPS, ND, Q)
        sums = jnp.sum(sums, axis=1)
        part_out[u] = below(sums[:, :128], sums[:, 128:])
        return carry

    lax.fori_loop(0, 8, partial, 0)
    returns = []
    for k in range(1, 8):
        to = (px + k // 2) % 4 * 2 + (core + k) % 2
        returns.append(
            pltpu.make_async_remote_copy(
                src_ref=part_out.at[to],
                dst_ref=part_in.at[k],
                send_sem=rsend_sem.at[k],
                recv_sem=rrecv_sem.at[k],
                device_id=owner(k),
                device_id_type=MESH,
            )
        )
    for copy in returns:
        copy.start()

    def build_hot(g, carry):
        ids = lax.broadcasted_iota(jnp.int32, (ROWS, Q), 0) + g * ROWS
        columns = target_ref[...] // NZ
        for c in range(3):
            same = ids + c * C * C == columns
            hot[g, c] = jnp.where(same, 1.0, 0.0).astype(BF)
        return carry

    lax.fori_loop(0, GROUPS, build_hot, 0)
    for h in range(2):
        depth = lane_spread(target_ref[:, 128 * h : 128 * h + 128] % NZ)
        for b in range(2):
            depth_hot[128 * h : 128 * h + 128, 128 * b : 128 * b + 128] = jnp.where(
                across + 128 * b == depth, 1.0, 0.0
            ).astype(BF)
    for copy in returns:
        copy.wait()
    traces = part_out[px * 2 + core]
    for k in range(1, 8):
        traces = traces + part_in[k]
    slot = lax.broadcasted_iota(jnp.int32, (8, 128), 1) + lax.broadcasted_iota(jnp.int32, (8, 128), 0) // 4 * 128
    traces = jnp.where(slot < live_ref[0], traces, 0.0)
    for h in range(2):
        part = slice(128 * h, 128 * h + 128)
        for n in range(STEPS):
            line = jnp.broadcast_to(traces[4 * h + n : 4 * h + n + 1], (128, 128))
            diagonal = jnp.where(along == across, line, 0.0).astype(BF)
            spread[n, part] = dot(diagonal, depth_hot[part]).astype(BF)
    loads[1].wait()
    loads[2].wait()

    spread_store = pltpu.make_async_copy(spread.at[STEPS - 1], spread_hbm, store_sem.at[0])
    spread_store.start()
    prior_store = pltpu.make_async_copy(field.at[0], prior_hbm, store_sem.at[1])

    def last_stores(g):
        x = g * XG
        return (
            pltpu.make_async_copy(
                field.at[1, :, rows_at(g)], last_hbm.at[:, rows_at(g)], group_sem.at[0, g]
            ),
            pltpu.make_async_copy(
                half.at[1, :, pl.ds(x + 2, XG)], half_hbm.at[:, pl.ds(x + 2, XG)], group_sem.at[1, g]
            ),
        )

    for n in range(STEPS - 1):
        if n > 0:
            sent(n - 1)
        if n == STEPS - 2:
            prior_store.start()

        def later_step(i, carry):
            receive(n, i)
            g = group_at(i)
            result = update(n, g, injected(n, g))
            for c in range(3):
                keep(n + 1, g, c, result[c])
            publish(n + 1, i)
            if n == STEPS - 2:
                for store in last_stores(g):
                    store.start()
            return carry

        lax.fori_loop(0, GROUPS, later_step, 0)

    last = STEPS - 1
    arrive(last, 0, 1)
    ends = [
        pltpu.make_async_copy(half.at[1, :, pl.ds(x, 2)], half_hbm.at[:, pl.ds(x, 2)], store_sem.at[k])
        for x, k in ((0, 2), (C + 2, 3))
    ]
    for store in ends:
        store.start()
    arrive(last, 2, 3, 4, 5)
    corner_store = pltpu.make_async_copy(corner.at[1], corner_hbm, store_sem.at[4])
    corner_store.start()
    arrive(last, 6, 7, 8, 9, 10, 11)
    side_store = pltpu.make_async_copy(side_in.at[1], side_hbm, store_sem.at[5])
    side_store.start()
    sent(last - 1)
    sent(last)
    for store in (spread_store, prior_store, *ends, corner_store, side_store):
        store.wait()

    def drain(g, carry):
        for store in last_stores(g):
            store.wait()
        return carry

    lax.fori_loop(0, GROUPS, drain, 0)


def last_kernel(
    target_ref,
    table_hbm, half_hbm, side_hbm, corner_hbm, spread_hbm, now_hbm, before_hbm, moduli_hbm,
    final_hbm, copy_hbm,
    table, half, side, corner, spread, now, before, mod, final,
    sem, half_sem, load_sem, store_sem,
):
    small = [
        pltpu.make_async_copy(source, target, sem.at[k])
        for k, (source, target) in enumerate(
            (
                (table_hbm.at[pl.ds(0, SHORT)], table),
                (spread_hbm, spread),
                (side_hbm, side),
                (corner_hbm, corner),
            )
        )
    ]

    def half_load(k):
        x = k * XG
        return pltpu.make_async_copy(half_hbm.at[:, pl.ds(x, XG)], half.at[:, pl.ds(x, XG)], half_sem.at[k])

    def group_loads(g):
        part = rows_at(g)
        return [
            pltpu.make_async_copy(source.at[:, part], target.at[:, part], load_sem.at[k, g])
            for k, (source, target) in enumerate(
                ((now_hbm, now), (before_hbm, before), (moduli_hbm, mod))
            )
        ]

    def group_stores(g):
        part = rows_at(g)
        return [
            pltpu.make_async_copy(source.at[:, part], target.at[:, part], store_sem.at[k, g])
            for k, (source, target) in enumerate(((final, final_hbm), (now, copy_hbm)))
        ]

    half_load(0).start()
    for load in small:
        load.start()

    def begin(g, carry):
        half_load(g + 1).start()
        for load in group_loads(g):
            load.start()
        return carry

    lax.fori_loop(0, GROUPS, begin, 0)
    half_load(0).wait()
    for load in small:
        load.wait()

    def group(g, carry):
        x = g * XG
        half_load(g + 1).wait()
        for load in group_loads(g):
            load.wait()
        stores = group_stores(g)
        stores[1].start()
        kind = jnp.where(g == 0, 0, jnp.where(g == GROUPS - 1, 2, 1))
        ids = lax.broadcasted_iota(jnp.int32, (ROWS, Q), 0) + g * ROWS
        columns = target_ref[...] // NZ
        hot = [jnp.where(ids + c * C * C == columns, 1.0, 0.0).astype(BF) for c in range(3)]
        values = dot(below(*hot), spread[...])
        result = advance(
            [half[c, pl.ds(x, XG + 4)] for c in range(3)],
            [side[0, g, c] for c in range(3)],
            [side[1, g, c] for c in range(3)],
            [corner[kind, 0, c] for c in range(2)],
            [corner[kind, 1, c] for c in range(2)],
            [now[c, rows_at(g)] for c in range(3)],
            [before[c, rows_at(g)] for c in range(3)],
            mod[0, rows_at(g)],
            mod[1, rows_at(g)],
            [values[ROWS * c : ROWS * c + ROWS] for c in range(3)],
            *matrices(table, kind),
        )
        for c in range(3):
            final[c, rows_at(g)] = result[c]
        stores[0].start()
        return carry

    lax.fori_loop(0, GROUPS, group, 0)

    def drain(g, carry):
        for store in group_stores(g):
            store.wait()
        return carry

    lax.fori_loop(0, GROUPS, drain, 0)


def shards(
    layer_slowness, layer_rigidity, layer_damping, layer_of_level,
    slot_offset, slot_level, slot_target, live_count, moduli, field_old, field_now,
):
    fixed = jnp.asarray(constants())
    smem = pl.BlockSpec(memory_space=pltpu.SMEM)
    vmem = pl.BlockSpec(memory_space=pltpu.VMEM)
    any_space = pl.BlockSpec(memory_space=pl.ANY)
    target = slot_target.reshape(1, Q)
    block = jax.ShapeDtypeStruct((3, C * C, NZ), F32)
    whole = (3, C, C, NZ)
    moduli = moduli.reshape(2, C * C, NZ)
    field_old, field_now = field_old.reshape(block.shape), field_now.reshape(block.shape)
    dma = pltpu.SemaphoreType.DMA
    last, prior, half, side, corner, spread = pl.pallas_call(
        main_kernel,
        out_shape=[
            block,
            block,
            jax.ShapeDtypeStruct((3, C + 4, C, NZ), BF),
            jax.ShapeDtypeStruct((2, GROUPS, 3, 16, NZ), BF),
            jax.ShapeDtypeStruct((3, 2, 2, 16, NZ), BF),
            jax.ShapeDtypeStruct((Q, NZ), BF),
        ],
        in_specs=[smem] * 5 + [vmem] + [any_space] * 6,
        out_specs=[any_space] * 6,
        scratch_shapes=[
            pltpu.VMEM((2, 3, C * C, NZ), F32),
            pltpu.VMEM((2, C * C, NZ), F32),
            pltpu.VMEM((2, 3, C + 4, C, NZ), BF),
            pltpu.VMEM((2, 2, GROUPS, 3, 16, NZ), BF),
            pltpu.VMEM((2, 2, GROUPS, 3, 16, NZ), BF),
            pltpu.VMEM((2, 3, 2, 2, 16, NZ), BF),
            pltpu.VMEM((GROUPS, 3, ROWS, Q), BF),
            pltpu.VMEM((16, 8, 128), F32),
            pltpu.VMEM((16, 128, 128), BF),
            pltpu.VMEM((STEPS, Q, NZ), BF),
            pltpu.VMEM((Q, NZ), BF),
            pltpu.VMEM((8, 8, 128), F32),
            pltpu.VMEM((8, 8, 128), F32),
            pltpu.VMEM((TABLE, NZ), BF),
            pltpu.VMEM((2, 4, 8, 128), jnp.int32),
            pltpu.VMEM((ND + 1, 8, 128), F32),
            pltpu.VMEM((2, ND, 8, 128), F32),
            pltpu.VMEM((2, ND, 8, 128), F32),
            pltpu.VMEM((ND, 8, 2 * F), F32),
            dma((4,)),
            dma((6,)),
            dma((2, GROUPS)),
            dma((STEPS, LINKS)),
            dma((STEPS, LINKS)),
            dma((16,)),
            dma((16,)),
            dma((2, 4)),
            dma((8,)),
            dma((8,)),
        ],
        compiler_params=pltpu.CompilerParams(
            collective_id=0, has_side_effects=True, vmem_limit_bytes=VMEM
        ),
    )(
        layer_slowness, layer_rigidity, layer_damping, layer_of_level, live_count, target,
        fixed,
        slot_offset.reshape(Q, 128), slot_level.reshape(Q, 128), moduli, field_old, field_now,
    )

    final, copied = pl.pallas_call(
        last_kernel,
        out_shape=[block, block],
        in_specs=[vmem] + [any_space] * 8,
        out_specs=[any_space] * 2,
        scratch_shapes=[
            pltpu.VMEM((SHORT, NZ), BF),
            pltpu.VMEM(half.shape, BF),
            pltpu.VMEM(side.shape, BF),
            pltpu.VMEM(corner.shape, BF),
            pltpu.VMEM(spread.shape, BF),
            pltpu.VMEM(block.shape, F32),
            pltpu.VMEM(block.shape, F32),
            pltpu.VMEM(moduli.shape, F32),
            pltpu.VMEM(block.shape, F32),
            dma((4,)),
            dma((GROUPS + 1,)),
            dma((3, GROUPS)),
            dma((2, GROUPS)),
        ],
        compiler_params=pltpu.CompilerParams(vmem_limit_bytes=VMEM),
    )(target, fixed, half, side, corner, spread, last, prior, moduli)
    return final.reshape(whole), copied.reshape(whole)


def solution(mesh):
    in_specs = (
        P(),
        P(),
        P(),
        P(),
        P(),
        P(),
        P(("gx", "gy")),
        P(("gx", "gy")),
        P(None, "gx", "gy", None),
        P(None, "gx", "gy", None),
        P(None, "gx", "gy", None),
    )
    out_specs = (P(None, "gx", "gy", None), P(None, "gx", "gy", None))
    return jax.shard_map(shards, mesh=mesh, in_specs=in_specs, out_specs=out_specs, check_vma=False)
```

```python
import functools
import math

import jax
import jax.numpy as jnp
import ml_dtypes
import numpy as np
from jax import lax
from jax.experimental import pallas as pl
from jax.experimental.pallas import tpu as pltpu
from jax.sharding import PartitionSpec as P

F = 128
NK = 1024
NR = 2048
ND = 32
STEPS = 4
TSTART = 32
GX = 16
GY = 8
C = 32
NZ = 256
Q = 256
GROUPS = 8
XG = 4
ROWS = XG * C
SINGLES = 6
LINKS = 6 + 2 * (SINGLES + 1)
VMEM = 63 * 1024 * 1024
MESH = pl.DeviceIdType.MESH
BF = jnp.bfloat16
F32 = jnp.float32


def constants():
    low, high = ROWS, ROWS + 16

    def place(x, y, kind):
        if y < 0:
            return low + 8 * (y + 2) + x + (0, 1, 4)[kind]
        if y >= C:
            return high + 8 * (y - C) + x + (0, 1, 4)[kind]
        return x * C + y

    y2 = np.zeros((3, ROWS, ROWS + 32), np.float32)
    y1 = np.zeros((3, ROWS, ROWS + 32), np.float32)
    cross = np.zeros((3, ROWS, ROWS + 96), np.float32)
    for kind in range(3):
        for x in range(XG):
            for y in range(C):
                row = x * C + y
                for shift, factor in ((-2, -1.0), (-1, 16.0), (1, 16.0), (2, -1.0)):
                    y2[kind, row, place(x, y + shift, kind)] += factor
                y1[kind, row, place(x, y + 1, kind)] += 1.0
                y1[kind, row, place(x, y - 1, kind)] -= 1.0
        cross[kind, :, :ROWS] = 3.0 * y1[kind, :, :ROWS]
        cross[kind, :, ROWS + 64 :] = 3.0 * y1[kind, :, ROWS:]
        for x in range(XG):
            for y, beyond, sign in ((0, -1, -3.0), (C - 1, C, 3.0)):
                for step in (-1, 1):
                    outside = (kind == 0 and x + step < 0) or (kind == 2 and x + step >= XG)
                    if outside:
                        spot = ROWS + 32 + 15 if beyond < 0 else ROWS + 48
                    else:
                        spot = place(x + step, beyond, kind)
                    cross[kind, x * C + y, spot] += sign * step
    z2 = np.zeros((NZ, NZ), np.float32)
    z1 = np.zeros((NZ, NZ), np.float32)
    for z in range(NZ):
        for shift, factor in ((-2, -1.0), (-1, 16.0), (1, 16.0), (2, -1.0)):
            if 0 <= z + shift < NZ:
                z2[z + shift, z] += factor
        if z + 1 < NZ:
            z1[z + 1, z] += 1.0
        if z > 0:
            z1[z - 1, z] -= 1.0
    period = 2 * F
    turns = (np.arange(F)[None, :] + 1) * (TSTART + np.arange(STEPS)[:, None]) % period
    angles = turns * (2.0 * math.pi / period)
    weight = 1.0 / math.sqrt(F)
    waves = np.concatenate([weight * np.cos(angles), -weight * np.sin(angles)], axis=1).T
    waves = np.repeat(waves.astype(np.float32), ND, axis=1)
    upper = waves.astype(ml_dtypes.bfloat16)
    lower = (waves - upper.astype(np.float32)).astype(ml_dtypes.bfloat16)
    half = ml_dtypes.bfloat16
    parts = [*y2, *y1, *cross, z2, z1, 3.0 * z1]
    parts = [np.pad(part, ((0, 0), (0, 256 - part.shape[1]))).astype(half) for part in parts]
    return np.concatenate(parts + [np.concatenate([upper, lower], axis=1)])


AT_Y2, AT_Y1, AT_CROSS, AT_Z2, AT_Z1, AT_Z3 = 0, 384, 768, 1152, 1408, 1664
AT_WAVES, TABLE = 1920, 2176
SHORT = AT_WAVES


def matrices(table, kind):
    def part(at):
        return table[pl.ds(pl.multiple_of(at + ROWS * kind, ROWS), ROWS)]

    return (
        part(AT_Y2)[:, : ROWS + 32],
        part(AT_Y1)[:, : ROWS + 32],
        part(AT_CROSS),
        table[AT_Z2 : AT_Z2 + NZ],
        table[AT_Z1 : AT_Z1 + NZ],
        table[AT_Z3 : AT_Z3 + NZ],
    )


def rows_at(g):
    return pl.ds(pl.multiple_of(g * ROWS, ROWS), ROWS)


def group_at(i):
    return jnp.where(i % 2 == 0, GROUPS - 1 - i // 2, i // 2)


def place_of(g):
    return jnp.where(g < GROUPS // 2, 2 * g + 1, 2 * (GROUPS - 1 - g))


def kind_of(g):
    return jnp.where(g == 0, 0, jnp.where(g == GROUPS - 1, 2, 1))


def dot(a, b):
    return jnp.dot(a, b, preferred_element_type=F32)


def beside(*parts):
    return jnp.concatenate(parts, axis=1)


def below(*parts):
    return jnp.concatenate(parts, axis=0)


def advance(window, lows, highs, clows, chighs, now, before, lam, mu, sources, y2, y1, cross, z2, z1, z3):
    wide = [w.astype(F32) for w in window]
    inner = [w[2 : 2 + XG].reshape(ROWS, NZ) for w in window]
    second = [(16.0 * (w[1:5] + w[3:7]) - (w[0:4] + w[4:8])).reshape(ROWS, NZ) for w in wide]
    first = [(w[3:7] - w[1:5]).reshape(ROWS, NZ) for w in wide]
    tall = [below(inner[c], lows[c], highs[c]) for c in range(3)]
    skew_z = dot(tall[2], z1)
    skew_y = dot(y1, tall[1])
    lap = [dot(beside(inner[c], y2), below(z2, tall[c])) for c in range(3)]
    mix_0 = dot(
        beside(first[2].astype(BF), cross[:, : ROWS + 64]),
        below(z3, first[1].astype(BF), lows[1], highs[1], clows[1], chighs[1]),
    )
    mix_1 = dot(
        beside(cross, y2),
        below(
            (first[0] + skew_z[:ROWS]).astype(BF), lows[0], highs[0], clows[0], chighs[0],
            skew_z[ROWS:].astype(BF), lows[0], highs[0], tall[1],
        ),
    )
    mix_2 = dot(beside(inner[2], (first[0] + skew_y).astype(BF)), below(z2, z3))
    couple = [second[0] + mix_0, mix_1, mix_2]
    shear = mu * (1.0 / 12.0)
    joint = (lam + mu) * (1.0 / 12.0)
    centre = 2.0 - 90.0 * shear - 30.0 * joint
    result = []
    for c in range(3):
        moved = shear * (second[c] + lap[c]) + joint * couple[c]
        if sources is not None:
            moved = moved + sources[c]
        result.append((centre * now[c] - before[c]) + moved)
    return result


def sine(x):
    y = x * x
    poly = -2.5052108e-08
    for coefficient in (2.7557319e-06, -1.9841270e-04, 8.3333333e-03, -1.6666667e-01, 1.0):
        poly = poly * y + coefficient
    return x * poly


def cosine(x):
    y = x * x
    poly = -2.7557319e-07
    for coefficient in (2.4801587e-05, -1.3888889e-03, 4.1666667e-02, -0.5, 1.0):
        poly = poly * y + coefficient
    return poly


def lane_spread(row):
    return jnp.transpose(jnp.broadcast_to(row.astype(F32), (128, 128))).astype(jnp.int32)


def main_kernel(
    slow_ref, rigid_ref, damp_ref, level_ref, live_ref, target_ref,
    table_hbm, offsets_hbm, levels_hbm, moduli_hbm, old_hbm, now_hbm,
    last_hbm, prior_hbm, half_hbm, side_hbm, corner_hbm, spread_hbm,
    field, mod, half, side_out, side_in, corner, hot, gathered, basis, spread,
    depth_hot, part_out, part_in,
    table, slot_tile, zbuf, ebuf, dbuf, kbuf,
    load_sem, store_sem, group_sem, send_sem, recv_sem, gsend_sem, grecv_sem,
    slot_sem, rsend_sem, rrecv_sem,
):
    gx = lax.axis_index("gx")
    gy = lax.axis_index("gy")
    device = gx * GY + gy
    px, pz = gx // 4, gx % 4
    py, core = gy // 2, gy % 2
    block = core * 64 + px * 16 + pz * 4 + py

    loads = [
        pltpu.make_async_copy(now_hbm, field.at[0], load_sem.at[0]),
        pltpu.make_async_copy(old_hbm, field.at[1], load_sem.at[1]),
        pltpu.make_async_copy(moduli_hbm, mod, load_sem.at[2]),
        pltpu.make_async_copy(table_hbm, table, load_sem.at[3]),
    ]
    slot_loads = []
    for x in range(4):
        at = pl.ds(pl.multiple_of(x * 64 + pz * 16 + py // 2 * 8, 8), 8)
        for k, ref in enumerate((offsets_hbm, levels_hbm)):
            slot_loads.append(pltpu.make_async_copy(ref.at[at], slot_tile.at[k, x], slot_sem.at[k, x]))
    for load in loads[:1] + slot_loads + loads[3:] + loads[1:3]:
        load.start()

    for p in range(2):
        half[p, :, 0:2] = jnp.zeros((3, 2, C, NZ), BF)
        half[p, :, C + 2 : C + 4] = jnp.zeros((3, 2, C, NZ), BF)
        corner[p] = jnp.zeros(corner.shape[1:], BF)
        for s in range(2):
            side_in[p, s] = jnp.zeros(side_in.shape[2:], BF)

    steps = [(1, 0), (-1, 0), (0, 1), (0, -1), (1, 1), (1, -1), (-1, 1), (-1, -1)]

    def exists(dx, dy):
        ok = None
        for delta, place, size in ((dx, gx, GX), (dy, gy, GY)):
            if delta == 1:
                part = place < size - 1
            elif delta == -1:
                part = place > 0
            else:
                continue
            ok = part if ok is None else jnp.logical_and(ok, part)
        return ok

    barrier = pltpu.get_barrier_semaphore()
    for dx, dy in steps:
        @pl.when(exists(dx, dy))
        def _():
            pl.semaphore_signal(barrier, inc=1, device_id=(gx + dx, gy + dy), device_id_type=MESH)

    def in_plane(k):
        return (px * 4 + (pz + k // 4) % 4, (py + k % 4) % 4 * 2 + core)

    def owner(k):
        return ((px + k // 2) % 4 * 4 + pz, py * 2 + (core + k) % 2)

    for k in range(1, 16):
        pl.semaphore_signal(barrier, inc=1, device_id=in_plane(k), device_id_type=MESH)
    for k in range(1, 8):
        pl.semaphore_signal(barrier, inc=1, device_id=owner(k), device_id_type=MESH)

    rows = lax.broadcasted_iota(jnp.int32, (8, 128), 0) + block * 8
    wavenum = (rows.astype(F32) + 0.5) * (4.0 / NK)
    square_k = wavenum * wavenum
    omega = (lax.broadcasted_iota(jnp.int32, (8, 128), 1) + 1).astype(F32) * (4.0 / F)

    def downward(i, carry):
        down_re, down_im = carry
        layer = level_ref[i]
        part = omega * slow_ref[layer]
        vertical = jnp.sqrt(square_k + part * part)
        fade = jnp.exp(vertical * (-0.25 * damp_ref[layer]))
        angle = 0.125 * vertical
        s, c = sine(angle), cosine(angle)
        leg_re = fade * (1.0 - 2.0 * s * s)
        leg_im = fade * (-2.0 * s * c)
        zbuf[i] = rigid_ref[layer] * vertical
        ebuf[0, i] = leg_re
        ebuf[1, i] = leg_im
        dbuf[0, i] = down_re
        dbuf[1, i] = down_im
        return down_re * leg_re - down_im * leg_im, down_re * leg_im + down_im * leg_re

    one = jnp.ones((8, 128), F32)
    zero = jnp.zeros((8, 128), F32)
    lax.fori_loop(0, ND, downward, (one, zero), unroll=4)
    zbuf[ND] = zbuf[ND - 1]

    def upward(step, carry):
        refl_re, refl_im = carry
        i = ND - 1 - step
        upper, under = zbuf[i], zbuf[i + 1]
        r = (upper - under) / (upper + under)
        leg_re, leg_im = ebuf[0, i], ebuf[1, i]
        trip_re = leg_re * leg_re - leg_im * leg_im
        trip_im = 2.0 * leg_re * leg_im
        upper_re = r + refl_re
        lower_re = 1.0 + r * refl_re
        lower_im = r * refl_im
        scale = 1.0 / (lower_re * lower_re + lower_im * lower_im)
        ratio_re = (upper_re * lower_re + refl_im * lower_im) * scale
        ratio_im = (refl_im * lower_re - upper_re * lower_im) * scale
        fresh_re = trip_re * ratio_re - trip_im * ratio_im
        fresh_im = trip_re * ratio_im + trip_im * ratio_re
        down_re, down_im = dbuf[0, i], dbuf[1, i]
        kbuf[i, :, 0:128] = (down_re * (1.0 + fresh_re) - down_im * fresh_im) * (1.0 / 32.0)
        kbuf[i, :, 128:256] = (down_re * fresh_im + down_im * (1.0 + fresh_re)) * (1.0 / 32.0)
        return fresh_re, fresh_im

    lax.fori_loop(0, ND, upward, (zero, zero), unroll=4)
    loads[3].wait()
    product = dot(kbuf[...].reshape(ND * 8, 2 * F).astype(BF), table[AT_WAVES : AT_WAVES + 2 * F])
    product = product[:, :128] + product[:, 128:]
    lane = lax.broadcasted_iota(jnp.int32, (8, 128), 1) % ND
    mine = zero
    for d in range(ND):
        mine = jnp.where(lane == d, product[8 * d : 8 * d + 8], mine)
    seat = pz * 4 + py
    gathered[seat] = mine

    count = 22
    for dx, dy in steps:
        count = count + exists(dx, dy).astype(jnp.int32)
    pl.semaphore_wait(barrier, count)

    gathers = [
        pltpu.make_async_remote_copy(
            src_ref=gathered.at[seat],
            dst_ref=gathered.at[seat],
            send_sem=gsend_sem.at[k],
            recv_sem=grecv_sem.at[k],
            device_id=in_plane(k),
            device_id_type=MESH,
        )
        for k in range(1, 16)
    ]
    for copy in gathers:
        copy.start()

    def send(n, move, source, target, index):
        copy = pltpu.make_async_remote_copy(
            src_ref=source,
            dst_ref=target,
            send_sem=send_sem.at[n, index],
            recv_sem=recv_sem.at[n, index],
            device_id=(gx + move[0], gy + move[1]),
            device_id_type=MESH,
        )
        return copy, exists(*move), exists(-move[0], -move[1])

    def message(n, index):
        p = n % 2
        if index < 2:
            move = (1, 0) if index == 0 else (-1, 0)
            source = half.at[p, :, pl.ds(C if index == 0 else 2, 2)]
            target = half.at[p, :, pl.ds(0 if index == 0 else C + 2, 2)]
        else:
            move = (1 if index < 4 else -1, 1 if index % 2 == 0 else -1)
            source = half.at[
                p, pl.ds(0, 2), C + 1 if move[0] == 1 else 2, pl.ds(16 if move[1] == 1 else 0, 16)
            ]
            target = corner.at[p, 0 if move[0] == 1 else 2, 0 if move[1] == 1 else 1]
        return send(n, move, source, target, index)

    def tiles(n, i, size):
        return [
            send(
                n,
                (0, 1) if s == 0 else (0, -1),
                side_out.at[n % 2, s, pl.ds(i, size)],
                side_in.at[n % 2, s, pl.ds(i, size)],
                6 + (SINGLES + 1) * s + i,
            )
            for s in range(2)
        ]

    def start(messages):
        for copy, there, _ in messages:

            @pl.when(there)
            def _():
                copy.start()

    def arrive(messages):
        for copy, _, here in messages:

            @pl.when(here)
            def _():
                copy.wait_recv()

    def everything(n):
        return [message(n, index) for index in range(6)] + [
            one for i in range(SINGLES + 1) for one in tiles(n, i, 1 if i < SINGLES else 2)
        ]

    def sent(n):
        for copy, there, _ in everything(n):

            @pl.when(there)
            def _():
                copy.wait_send()

    def fill(n, first, size):
        p = n % 2

        def one_tile(i, carry):
            g = group_at(i)
            x = jnp.where(g == 0, 0, jnp.where(g == GROUPS - 1, C - 8, g * XG - 1))
            place = lax.broadcasted_iota(jnp.int32, (8, NZ), 0)
            for c in range(3):
                for s, y in ((0, C - 2), (1, 0)):
                    rows = [jnp.zeros((8, NZ), F32)] * 2
                    for k in range(8):
                        at = pl.multiple_of((x + k) * C + y // 8 * 8, 8)
                        tile = field[p, c, pl.ds(at, 8)]
                        for j in range(2):
                            line = jnp.broadcast_to(tile[y % 8 + j : y % 8 + j + 1], (8, NZ))
                            rows[j] = jnp.where(place == k, line, rows[j])
                    side_out[p, s, i, c] = below(*rows).astype(BF)
            return carry

        lax.fori_loop(first, first + size, one_tile, 0)

    def publish(n, i):
        @pl.when(i == 0)
        def _():
            start([message(n, index) for index in (0, 2, 3)])

        @pl.when(i == 1)
        def _():
            start([message(n, index) for index in (1, 4, 5)])

        @pl.when(i >= 2)
        def _():
            fill(n, i - 2, 1)
            start(tiles(n, i - 2, 1))

        @pl.when(i == GROUPS - 1)
        def _():
            fill(n, SINGLES, 2)
            start(tiles(n, SINGLES, 2))

    def receive(n, i):
        @pl.when(i == 0)
        def _():
            arrive([message(n, index) for index in (1, 4, 5)])

        @pl.when(i == 1)
        def _():
            arrive([message(n, index) for index in (0, 2, 3)])

        @pl.when(i < SINGLES)
        def _():
            arrive(tiles(n, i, 1))

        @pl.when(i == SINGLES)
        def _():
            arrive(tiles(n, SINGLES, 2))

    def update(n, g, sources):
        p = n % 2
        x = g * XG
        kind = kind_of(g)
        return advance(
            [half[p, c, pl.ds(x, XG + 4)] for c in range(3)],
            [side_in[p, 0, place_of(g), c] for c in range(3)],
            [side_in[p, 1, place_of(g), c] for c in range(3)],
            [corner[p, kind, 0, c] for c in range(2)],
            [corner[p, kind, 1, c] for c in range(2)],
            [field[p, c, rows_at(g)] for c in range(3)],
            [field[1 - p, c, rows_at(g)] for c in range(3)],
            mod[0, rows_at(g)],
            mod[1, rows_at(g)],
            sources,
            *matrices(table, kind),
        )

    def injected(n, g):
        values = dot(hot[g].reshape(3 * ROWS, Q), spread[n])
        return [values[ROWS * c : ROWS * c + ROWS] for c in range(3)]

    def keep(n, g, c, fresh):
        field[n % 2, c, rows_at(g)] = fresh
        half[n % 2, c, pl.ds(g * XG + 2, XG)] = fresh.astype(BF).reshape(XG, C, NZ)

    def to_half(g, carry):
        x = g * XG
        for c in range(3):
            half[0, c, pl.ds(x + 2, XG)] = field[0, c, rows_at(g)].astype(BF).reshape(XG, C, NZ)
        return carry

    loads[0].wait()
    lax.fori_loop(0, GROUPS, to_half, 0)
    start([message(0, index) for index in range(6)])
    fill(0, 0, GROUPS)
    start(everything(0)[6:])

    for load in slot_loads:
        load.wait()
    first_row = py % 2 * 4
    mask = NK * NR // 2 - 1
    across = lax.broadcasted_iota(jnp.int32, (128, 128), 1)
    along = lax.broadcasted_iota(jnp.int32, (128, 128), 0)
    odd_index = 2 * (along + (core * 4 + px) * 128) + 1

    def cosines(t, carry):
        q = slot_tile[0, t // 4, pl.ds(first_row + t % 4, 1)]
        turns = odd_index * q
        turns = ((turns + (mask + 1) // 2) & mask) - (mask + 1) // 2
        s = sine(turns.astype(F32) * (math.pi / (mask + 1)))
        basis[t] = (1.0 - 2.0 * s * s).astype(BF)
        return carry

    lax.fori_loop(0, 16, cosines, 0)
    returns = []
    for k in range(1, 8):
        to = (px + k // 2) % 4 * 2 + (core + k) % 2
        returns.append(
            pltpu.make_async_remote_copy(
                src_ref=part_out.at[to],
                dst_ref=part_in.at[k],
                send_sem=rsend_sem.at[k],
                recv_sem=rrecv_sem.at[k],
                device_id=owner(k),
                device_id_type=MESH,
            )
        )
    def build_hot(g, carry):
        ids = lax.broadcasted_iota(jnp.int32, (ROWS, Q), 0) + g * ROWS
        columns = target_ref[...] // NZ
        for c in range(3):
            same = ids + c * C * C == columns
            hot[g, c] = jnp.where(same, 1.0, 0.0).astype(BF)
        return carry

    lax.fori_loop(0, GROUPS, build_hot, 0)
    for h in range(2):
        depth = lane_spread(target_ref[:, 128 * h : 128 * h + 128] % NZ)
        for b in range(2):
            depth_hot[128 * h : 128 * h + 128, 128 * b : 128 * b + 128] = jnp.where(
                across + 128 * b == depth, 1.0, 0.0
            ).astype(BF)
    def sum_up():
        for copy in gathers:
            copy.wait()
        total = jnp.transpose(gathered[...].reshape(128, 128))
        upper = total.astype(BF)
        lower = (total - upper.astype(F32)).astype(BF)
        both = beside(upper, lower)

        def partial(u, carry):
            cos = beside(basis[2 * u], basis[2 * u + 1])
            sums = dot(both, below(cos, cos))
            row = first_row + u % 2 * 2
            level = beside(*[slot_tile[1, u // 2, pl.ds(row + h, 1)] for h in range(2)])
            depth = lax.broadcasted_iota(jnp.int32, (STEPS * ND, Q), 0) % ND
            sums = jnp.where(depth == level, sums, 0.0).reshape(STEPS, ND, Q)
            sums = jnp.sum(sums, axis=1)
            part_out[u] = below(sums[:, :128], sums[:, 128:])
            return carry

        lax.fori_loop(0, 8, partial, 0)
        for copy in returns:
            copy.start()

    loads[1].wait()
    loads[2].wait()

    def first_step(i, carry):
        receive(0, i)
        pl.when(i == 2)(sum_up)
        g = group_at(i)
        result = update(0, g, None)
        for c in range(3):
            field[1, c, rows_at(g)] = result[c]
        return carry

    lax.fori_loop(0, GROUPS, first_step, 0)
    for copy in returns:
        copy.wait()
    traces = part_out[px * 2 + core]
    for k in range(1, 8):
        traces = traces + part_in[k]
    slot = lax.broadcasted_iota(jnp.int32, (8, 128), 1) + lax.broadcasted_iota(jnp.int32, (8, 128), 0) // 4 * 128
    traces = jnp.where(slot < live_ref[0], traces, 0.0)
    for h in range(2):
        part = slice(128 * h, 128 * h + 128)
        for n in range(STEPS):
            line = jnp.broadcast_to(traces[4 * h + n : 4 * h + n + 1], (128, 128))
            diagonal = jnp.where(along == across, line, 0.0).astype(BF)
            spread[n, part] = dot(diagonal, depth_hot[part]).astype(BF)

    def first_sources(i, carry):
        g = group_at(i)
        sources = injected(0, g)
        for c in range(3):
            keep(1, g, c, field[1, c, rows_at(g)] + sources[c])
        publish(1, i)
        return carry

    lax.fori_loop(0, GROUPS, first_sources, 0)

    spread_store = pltpu.make_async_copy(spread.at[STEPS - 1], spread_hbm, store_sem.at[0])
    spread_store.start()
    prior_store = pltpu.make_async_copy(field.at[0], prior_hbm, store_sem.at[1])

    def last_stores(g):
        x = g * XG
        return (
            pltpu.make_async_copy(
                field.at[1, :, rows_at(g)], last_hbm.at[:, rows_at(g)], group_sem.at[0, g]
            ),
            pltpu.make_async_copy(
                half.at[1, :, pl.ds(x + 2, XG)], half_hbm.at[:, pl.ds(x + 2, XG)], group_sem.at[1, g]
            ),
        )

    for n in range(1, STEPS - 1):
        sent(n - 1)
        if n == STEPS - 2:
            prior_store.start()

        def later_step(i, carry):
            receive(n, i)
            g = group_at(i)
            result = update(n, g, injected(n, g))
            for c in range(3):
                keep(n + 1, g, c, result[c])
            publish(n + 1, i)
            if n == STEPS - 2:
                for store in last_stores(g):
                    store.start()
            return carry

        lax.fori_loop(0, GROUPS, later_step, 0)

    last = STEPS - 1
    arrive([message(last, index) for index in (0, 1)])
    ends = [
        pltpu.make_async_copy(half.at[1, :, pl.ds(x, 2)], half_hbm.at[:, pl.ds(x, 2)], store_sem.at[k])
        for x, k in ((0, 2), (C + 2, 3))
    ]
    for store in ends:
        store.start()
    arrive([message(last, index) for index in (2, 3, 4, 5)])
    corner_store = pltpu.make_async_copy(corner.at[1], corner_hbm, store_sem.at[4])
    corner_store.start()
    arrive(everything(last)[6:])
    side_store = pltpu.make_async_copy(side_in.at[1], side_hbm, store_sem.at[5])
    side_store.start()
    sent(last - 1)
    sent(last)
    for store in (spread_store, prior_store, *ends, corner_store, side_store):
        store.wait()

    def drain(g, carry):
        for store in last_stores(g):
            store.wait()
        return carry

    lax.fori_loop(0, GROUPS, drain, 0)


def last_kernel(
    target_ref,
    table_hbm, half_hbm, side_hbm, corner_hbm, spread_hbm, now_hbm, before_hbm, moduli_hbm,
    final_hbm, copy_hbm,
    table, half, side, corner, spread, now, before, mod, final,
    sem, half_sem, load_sem, store_sem,
):
    small = [
        pltpu.make_async_copy(source, target, sem.at[k])
        for k, (source, target) in enumerate(
            (
                (table_hbm.at[pl.ds(0, SHORT)], table),
                (spread_hbm, spread),
                (side_hbm, side),
                (corner_hbm, corner),
            )
        )
    ]

    def half_load(k):
        x = k * XG
        return pltpu.make_async_copy(half_hbm.at[:, pl.ds(x, XG)], half.at[:, pl.ds(x, XG)], half_sem.at[k])

    def group_loads(g):
        part = rows_at(g)
        return [
            pltpu.make_async_copy(source.at[:, part], target.at[:, part], load_sem.at[k, g])
            for k, (source, target) in enumerate(
                ((now_hbm, now), (before_hbm, before), (moduli_hbm, mod))
            )
        ]

    def group_stores(g):
        part = rows_at(g)
        return [
            pltpu.make_async_copy(source.at[:, part], target.at[:, part], store_sem.at[k, g])
            for k, (source, target) in enumerate(((final, final_hbm), (now, copy_hbm)))
        ]

    def begin(g):
        half_load(g + 1).start()
        for load in group_loads(g):
            load.start()

    ahead = 3
    half_load(0).start()
    small[0].start()
    begin(0)
    for load in small[1:]:
        load.start()
    for g in range(1, ahead):
        begin(g)
    half_load(0).wait()
    for load in small:
        load.wait()

    def group(g, carry):
        x = g * XG

        @pl.when(g + ahead < GROUPS)
        def _():
            begin(g + ahead)

        half_load(g + 1).wait()
        for load in group_loads(g):
            load.wait()
        stores = group_stores(g)
        stores[1].start()
        kind = kind_of(g)
        ids = lax.broadcasted_iota(jnp.int32, (ROWS, Q), 0) + g * ROWS
        columns = target_ref[...] // NZ
        hot = [jnp.where(ids + c * C * C == columns, 1.0, 0.0).astype(BF) for c in range(3)]
        values = dot(below(*hot), spread[...])
        result = advance(
            [half[c, pl.ds(x, XG + 4)] for c in range(3)],
            [side[0, place_of(g), c] for c in range(3)],
            [side[1, place_of(g), c] for c in range(3)],
            [corner[kind, 0, c] for c in range(2)],
            [corner[kind, 1, c] for c in range(2)],
            [now[c, rows_at(g)] for c in range(3)],
            [before[c, rows_at(g)] for c in range(3)],
            mod[0, rows_at(g)],
            mod[1, rows_at(g)],
            [values[ROWS * c : ROWS * c + ROWS] for c in range(3)],
            *matrices(table, kind),
        )
        for c in range(3):
            final[c, rows_at(g)] = result[c]
        stores[0].start()
        return carry

    lax.fori_loop(0, GROUPS, group, 0)

    def drain(g, carry):
        for store in group_stores(g):
            store.wait()
        return carry

    lax.fori_loop(0, GROUPS, drain, 0)


def shards(
    layer_slowness, layer_rigidity, layer_damping, layer_of_level,
    slot_offset, slot_level, slot_target, live_count, moduli, field_old, field_now,
):
    fixed = jnp.asarray(constants())
    smem = pl.BlockSpec(memory_space=pltpu.SMEM)
    vmem = pl.BlockSpec(memory_space=pltpu.VMEM)
    any_space = pl.BlockSpec(memory_space=pl.ANY)
    target = slot_target.reshape(1, Q)
    block = jax.ShapeDtypeStruct((3, C * C, NZ), F32)
    whole = (3, C, C, NZ)
    moduli = moduli.reshape(2, C * C, NZ)
    field_old, field_now = field_old.reshape(block.shape), field_now.reshape(block.shape)
    dma = pltpu.SemaphoreType.DMA
    last, prior, half, side, corner, spread = pl.pallas_call(
        main_kernel,
        out_shape=[
            block,
            block,
            jax.ShapeDtypeStruct((3, C + 4, C, NZ), BF),
            jax.ShapeDtypeStruct((2, GROUPS, 3, 16, NZ), BF),
            jax.ShapeDtypeStruct((3, 2, 2, 16, NZ), BF),
            jax.ShapeDtypeStruct((Q, NZ), BF),
        ],
        in_specs=[smem] * 5 + [vmem] + [any_space] * 6,
        out_specs=[any_space] * 6,
        scratch_shapes=[
            pltpu.VMEM((2, 3, C * C, NZ), F32),
            pltpu.VMEM((2, C * C, NZ), F32),
            pltpu.VMEM((2, 3, C + 4, C, NZ), BF),
            pltpu.VMEM((2, 2, GROUPS, 3, 16, NZ), BF),
            pltpu.VMEM((2, 2, GROUPS, 3, 16, NZ), BF),
            pltpu.VMEM((2, 3, 2, 2, 16, NZ), BF),
            pltpu.VMEM((GROUPS, 3, ROWS, Q), BF),
            pltpu.VMEM((16, 8, 128), F32),
            pltpu.VMEM((16, 128, 128), BF),
            pltpu.VMEM((STEPS, Q, NZ), BF),
            pltpu.VMEM((Q, NZ), BF),
            pltpu.VMEM((8, 8, 128), F32),
            pltpu.VMEM((8, 8, 128), F32),
            pltpu.VMEM((TABLE, NZ), BF),
            pltpu.VMEM((2, 4, 8, 128), jnp.int32),
            pltpu.VMEM((ND + 1, 8, 128), F32),
            pltpu.VMEM((2, ND, 8, 128), F32),
            pltpu.VMEM((2, ND, 8, 128), F32),
            pltpu.VMEM((ND, 8, 2 * F), F32),
            dma((4,)),
            dma((6,)),
            dma((2, GROUPS)),
            dma((STEPS, LINKS)),
            dma((STEPS, LINKS)),
            dma((16,)),
            dma((16,)),
            dma((2, 4)),
            dma((8,)),
            dma((8,)),
        ],
        compiler_params=pltpu.CompilerParams(
            collective_id=0, has_side_effects=True, vmem_limit_bytes=VMEM
        ),
    )(
        layer_slowness, layer_rigidity, layer_damping, layer_of_level, live_count, target,
        fixed,
        slot_offset.reshape(Q, 128), slot_level.reshape(Q, 128), moduli, field_old, field_now,
    )

    final, copied = pl.pallas_call(
        last_kernel,
        out_shape=[block, block],
        in_specs=[vmem] + [any_space] * 8,
        out_specs=[any_space] * 2,
        scratch_shapes=[
            pltpu.VMEM((SHORT, NZ), BF),
            pltpu.VMEM(half.shape, BF),
            pltpu.VMEM(side.shape, BF),
            pltpu.VMEM(corner.shape, BF),
            pltpu.VMEM(spread.shape, BF),
            pltpu.VMEM(block.shape, F32),
            pltpu.VMEM(block.shape, F32),
            pltpu.VMEM(moduli.shape, F32),
            pltpu.VMEM(block.shape, F32),
            dma((4,)),
            dma((GROUPS + 1,)),
            dma((3, GROUPS)),
            dma((2, GROUPS)),
        ],
        compiler_params=pltpu.CompilerParams(vmem_limit_bytes=VMEM),
    )(target, fixed, half, side, corner, spread, last, prior, moduli)
    return final.reshape(whole), copied.reshape(whole)


def solution(mesh):
    in_specs = (
        P(),
        P(),
        P(),
        P(),
        P(),
        P(),
        P(("gx", "gy")),
        P(("gx", "gy")),
        P(None, "gx", "gy", None),
        P(None, "gx", "gy", None),
        P(None, "gx", "gy", None),
    )
    out_specs = (P(None, "gx", "gy", None), P(None, "gx", "gy", None))
    return jax.shard_map(shards, mesh=mesh, in_specs=in_specs, out_specs=out_specs, check_vma=False)
```

```python
import functools
import math

import jax
import jax.numpy as jnp
import ml_dtypes
import numpy as np
from jax import lax
from jax.experimental import pallas as pl
from jax.experimental.pallas import tpu as pltpu
from jax.sharding import PartitionSpec as P

F = 128
NK = 1024
NR = 2048
ND = 32
STEPS = 4
TSTART = 32
GX = 16
GY = 8
C = 32
NZ = 256
Q = 256
GROUPS = 8
XG = 4
ROWS = XG * C
TILES = 4
LINKS = 6 + 2 * TILES
ORDER = (7, 0, 6, 5, 1, 4, 2, 3)
VMEM = 63 * 1024 * 1024
MESH = pl.DeviceIdType.MESH
BF = jnp.bfloat16
F32 = jnp.float32


def constants():
    low, high = ROWS, ROWS + 16

    def place(x, y, half):
        if y < 0:
            return low + 8 * (y + 2) + x + XG * half
        if y >= C:
            return high + 8 * (y - C) + x + XG * half
        return x * C + y

    y2 = np.zeros((2, ROWS, ROWS + 32), np.float32)
    y1 = np.zeros((2, ROWS, ROWS + 32), np.float32)
    for half in range(2):
        for x in range(XG):
            for y in range(C):
                row = x * C + y
                for shift, factor in ((-2, -1.0), (-1, 16.0), (1, 16.0), (2, -1.0)):
                    y2[half, row, place(x, y + shift, half)] += factor
                y1[half, row, place(x, y + 1, half)] += 1.0
                y1[half, row, place(x, y - 1, half)] -= 1.0
    cross = np.zeros((4, ROWS, ROWS + 96), np.float32)
    for kind in range(4):
        half = kind // 2
        cross[kind, :, :ROWS] = 3.0 * y1[half, :, :ROWS]
        cross[kind, :, ROWS + 64 :] = 3.0 * y1[half, :, ROWS:]
        for x in range(XG):
            for y, beyond, sign in ((0, -1, -3.0), (C - 1, C, 3.0)):
                for step in (-1, 1):
                    if (half == 0 and x + step < 0) or (half == 1 and x + step >= XG):
                        spot = ROWS + (32 if beyond < 0 else 48)
                        if kind in (0, 3):
                            spot += 15 if beyond < 0 else 0
                        else:
                            spot += (8 if beyond < 0 else 0) + (7 if half == 0 else 0)
                    else:
                        spot = place(x + step, beyond, half)
                    cross[kind, x * C + y, spot] += sign * step
    z2 = np.zeros((NZ, NZ), np.float32)
    z1 = np.zeros((NZ, NZ), np.float32)
    for z in range(NZ):
        for shift, factor in ((-2, -1.0), (-1, 16.0), (1, 16.0), (2, -1.0)):
            if 0 <= z + shift < NZ:
                z2[z + shift, z] += factor
        if z + 1 < NZ:
            z1[z + 1, z] += 1.0
        if z > 0:
            z1[z - 1, z] -= 1.0
    period = 2 * F
    turns = (np.arange(F)[None, :] + 1) * (TSTART + np.arange(STEPS)[:, None]) % period
    angles = turns * (2.0 * math.pi / period)
    weight = 1.0 / math.sqrt(F)
    waves = np.concatenate([weight * np.cos(angles), -weight * np.sin(angles)], axis=1).T
    waves = np.repeat(waves.astype(np.float32), ND, axis=1)
    upper = waves.astype(ml_dtypes.bfloat16)
    lower = (waves - upper.astype(np.float32)).astype(ml_dtypes.bfloat16)
    half = ml_dtypes.bfloat16
    parts = [*y2, *y1, *cross, z2, z1, 3.0 * z1]
    parts = [np.pad(part, ((0, 0), (0, 256 - part.shape[1]))).astype(half) for part in parts]
    return np.concatenate(parts + [np.concatenate([upper, lower], axis=1)])


AT_Y2, AT_Y1, AT_CROSS, AT_Z2, AT_Z1, AT_Z3 = 0, 256, 512, 1024, 1280, 1536
AT_WAVES, TABLE = 1792, 2048
SHORT = AT_WAVES


def matrices(table, g):
    kind = jnp.where(g == 0, 0, jnp.where(g == GROUPS - 1, 3, 1 + g % 2))

    def part(at, k):
        return table[pl.ds(pl.multiple_of(at + ROWS * k, ROWS), ROWS)]

    return (
        part(AT_Y2, g % 2)[:, : ROWS + 32],
        part(AT_Y1, g % 2)[:, : ROWS + 32],
        part(AT_CROSS, kind),
        table[AT_Z2 : AT_Z2 + NZ],
        table[AT_Z1 : AT_Z1 + NZ],
        table[AT_Z3 : AT_Z3 + NZ],
    )


def halo_tiles(side, g):
    own = g // 2 + 1
    other = own - 1 + 2 * (g % 2)
    return (
        [side[0, own, c] for c in range(3)],
        [side[1, own, c] for c in range(3)],
        [side[0, other, c] for c in range(2)],
        [side[1, other, c] for c in range(2)],
    )


def rows_at(g):
    return pl.ds(pl.multiple_of(g * ROWS, ROWS), ROWS)


def group_at(i):
    g = ORDER[-1]
    for k in range(GROUPS - 1):
        g = jnp.where(i == k, ORDER[k], g)
    return g


def dot(a, b):
    return jnp.dot(a, b, preferred_element_type=F32)


def beside(*parts):
    return jnp.concatenate(parts, axis=1)


def below(*parts):
    return jnp.concatenate(parts, axis=0)


def advance(window, lows, highs, clows, chighs, now, before, lam, mu, sources, y2, y1, cross, z2, z1, z3):
    wide = [w.astype(F32) for w in window]
    inner = [w[2 : 2 + XG].reshape(ROWS, NZ) for w in window]
    second = [(16.0 * (w[1:5] + w[3:7]) - (w[0:4] + w[4:8])).reshape(ROWS, NZ) for w in wide]
    first = [(w[3:7] - w[1:5]).reshape(ROWS, NZ) for w in wide]
    tall = [below(inner[c], lows[c], highs[c]) for c in range(3)]
    skew_z = dot(tall[2], z1)
    skew_y = dot(y1, tall[1])
    lap = [dot(beside(inner[c], y2), below(z2, tall[c])) for c in range(3)]
    mix_0 = dot(
        beside(first[2].astype(BF), cross[:, : ROWS + 64]),
        below(z3, first[1].astype(BF), lows[1], highs[1], clows[1], chighs[1]),
    )
    mix_1 = dot(
        beside(cross, y2),
        below(
            (first[0] + skew_z[:ROWS]).astype(BF), lows[0], highs[0], clows[0], chighs[0],
            skew_z[ROWS:].astype(BF), lows[0], highs[0], tall[1],
        ),
    )
    mix_2 = dot(beside(inner[2], (first[0] + skew_y).astype(BF)), below(z2, z3))
    couple = [second[0] + mix_0, mix_1, mix_2]
    shear = mu * (1.0 / 12.0)
    joint = (lam + mu) * (1.0 / 12.0)
    centre = 2.0 - 90.0 * shear - 30.0 * joint
    result = []
    for c in range(3):
        moved = shear * (second[c] + lap[c]) + joint * couple[c]
        if sources is not None:
            moved = moved + sources[c]
        result.append((centre * now[c] - before[c]) + moved)
    return result


def sine(x):
    y = x * x
    poly = -2.5052108e-08
    for coefficient in (2.7557319e-06, -1.9841270e-04, 8.3333333e-03, -1.6666667e-01, 1.0):
        poly = poly * y + coefficient
    return x * poly


def cosine(x):
    y = x * x
    poly = -2.7557319e-07
    for coefficient in (2.4801587e-05, -1.3888889e-03, 4.1666667e-02, -0.5, 1.0):
        poly = poly * y + coefficient
    return poly


def lane_spread(row):
    return jnp.transpose(jnp.broadcast_to(row.astype(F32), (128, 128))).astype(jnp.int32)


def main_kernel(
    slow_ref, rigid_ref, damp_ref, level_ref, live_ref, target_ref,
    table_hbm, offsets_hbm, levels_hbm, moduli_hbm, old_hbm, now_hbm,
    last_hbm, prior_hbm, half_hbm, side_hbm, spread_hbm,
    field, mod, half, side_out, side_in, hot, gathered, basis, spread,
    depth_hot, part_out, part_in,
    table, slot_tile, zbuf, ebuf, dbuf, kbuf,
    load_sem, store_sem, group_sem, send_sem, recv_sem, gsend_sem, grecv_sem,
    slot_sem, rsend_sem, rrecv_sem,
):
    gx = lax.axis_index("gx")
    gy = lax.axis_index("gy")
    device = gx * GY + gy
    px, pz = gx // 4, gx % 4
    py, core = gy // 2, gy % 2
    block = core * 64 + px * 16 + pz * 4 + py

    loads = [
        pltpu.make_async_copy(now_hbm, field.at[0], load_sem.at[0]),
        pltpu.make_async_copy(old_hbm, field.at[1], load_sem.at[1]),
        pltpu.make_async_copy(moduli_hbm, mod, load_sem.at[2]),
        pltpu.make_async_copy(table_hbm, table, load_sem.at[3]),
    ]
    slot_loads = []
    for x in range(4):
        at = pl.ds(pl.multiple_of(x * 64 + pz * 16 + py // 2 * 8, 8), 8)
        for k, ref in enumerate((offsets_hbm, levels_hbm)):
            slot_loads.append(pltpu.make_async_copy(ref.at[at], slot_tile.at[k, x], slot_sem.at[k, x]))
    for load in loads[:1] + slot_loads + loads[3:] + loads[1:3]:
        load.start()

    for p in range(2):
        half[p, :, 0:2] = jnp.zeros((3, 2, C, NZ), BF)
        half[p, :, C + 2 : C + 4] = jnp.zeros((3, 2, C, NZ), BF)
        for s in range(2):
            side_in[p, s] = jnp.zeros(side_in.shape[2:], BF)

    steps = [(1, 0), (-1, 0), (0, 1), (0, -1), (1, 1), (1, -1), (-1, 1), (-1, -1)]

    def exists(dx, dy):
        ok = None
        for delta, place, size in ((dx, gx, GX), (dy, gy, GY)):
            if delta == 1:
                part = place < size - 1
            elif delta == -1:
                part = place > 0
            else:
                continue
            ok = part if ok is None else jnp.logical_and(ok, part)
        return ok

    barrier = pltpu.get_barrier_semaphore()
    for dx, dy in steps:
        @pl.when(exists(dx, dy))
        def _():
            pl.semaphore_signal(barrier, inc=1, device_id=(gx + dx, gy + dy), device_id_type=MESH)

    def in_plane(k):
        return (px * 4 + (pz + k // 4) % 4, (py + k % 4) % 4 * 2 + core)

    def owner(k):
        return ((px + k // 2) % 4 * 4 + pz, py * 2 + (core + k) % 2)

    for k in range(1, 16):
        pl.semaphore_signal(barrier, inc=1, device_id=in_plane(k), device_id_type=MESH)
    for k in range(1, 8):
        pl.semaphore_signal(barrier, inc=1, device_id=owner(k), device_id_type=MESH)

    rows = lax.broadcasted_iota(jnp.int32, (8, 128), 0) + block * 8
    wavenum = (rows.astype(F32) + 0.5) * (4.0 / NK)
    square_k = wavenum * wavenum
    omega = (lax.broadcasted_iota(jnp.int32, (8, 128), 1) + 1).astype(F32) * (4.0 / F)

    def downward(i, carry):
        down_re, down_im = carry
        layer = level_ref[i]
        part = omega * slow_ref[layer]
        vertical = jnp.sqrt(square_k + part * part)
        fade = jnp.exp(vertical * (-0.25 * damp_ref[layer]))
        angle = 0.125 * vertical
        s, c = sine(angle), cosine(angle)
        leg_re = fade * (1.0 - 2.0 * s * s)
        leg_im = fade * (-2.0 * s * c)
        zbuf[i] = rigid_ref[layer] * vertical
        ebuf[0, i] = leg_re
        ebuf[1, i] = leg_im
        dbuf[0, i] = down_re
        dbuf[1, i] = down_im
        return down_re * leg_re - down_im * leg_im, down_re * leg_im + down_im * leg_re

    one = jnp.ones((8, 128), F32)
    zero = jnp.zeros((8, 128), F32)
    lax.fori_loop(0, ND, downward, (one, zero), unroll=4)
    zbuf[ND] = zbuf[ND - 1]

    def upward(step, carry):
        refl_re, refl_im = carry
        i = ND - 1 - step
        upper, under = zbuf[i], zbuf[i + 1]
        r = (upper - under) / (upper + under)
        leg_re, leg_im = ebuf[0, i], ebuf[1, i]
        trip_re = leg_re * leg_re - leg_im * leg_im
        trip_im = 2.0 * leg_re * leg_im
        upper_re = r + refl_re
        lower_re = 1.0 + r * refl_re
        lower_im = r * refl_im
        scale = 1.0 / (lower_re * lower_re + lower_im * lower_im)
        ratio_re = (upper_re * lower_re + refl_im * lower_im) * scale
        ratio_im = (refl_im * lower_re - upper_re * lower_im) * scale
        fresh_re = trip_re * ratio_re - trip_im * ratio_im
        fresh_im = trip_re * ratio_im + trip_im * ratio_re
        down_re, down_im = dbuf[0, i], dbuf[1, i]
        kbuf[i, :, 0:128] = (down_re * (1.0 + fresh_re) - down_im * fresh_im) * (1.0 / 32.0)
        kbuf[i, :, 128:256] = (down_re * fresh_im + down_im * (1.0 + fresh_re)) * (1.0 / 32.0)
        return fresh_re, fresh_im

    lax.fori_loop(0, ND, upward, (zero, zero), unroll=4)
    loads[3].wait()
    product = dot(kbuf[...].reshape(ND * 8, 2 * F).astype(BF), table[AT_WAVES : AT_WAVES + 2 * F])
    product = product[:, :128] + product[:, 128:]
    lane = lax.broadcasted_iota(jnp.int32, (8, 128), 1) % ND
    mine = zero
    for d in range(ND):
        mine = jnp.where(lane == d, product[8 * d : 8 * d + 8], mine)
    seat = pz * 4 + py
    gathered[seat] = mine

    count = 22
    for dx, dy in steps:
        count = count + exists(dx, dy).astype(jnp.int32)
    pl.semaphore_wait(barrier, count)

    gathers = [
        pltpu.make_async_remote_copy(
            src_ref=gathered.at[seat],
            dst_ref=gathered.at[seat],
            send_sem=gsend_sem.at[k],
            recv_sem=grecv_sem.at[k],
            device_id=in_plane(k),
            device_id_type=MESH,
        )
        for k in range(1, 16)
    ]
    for copy in gathers:
        copy.start()

    def send(n, move, source, target, index):
        copy = pltpu.make_async_remote_copy(
            src_ref=source,
            dst_ref=target,
            send_sem=send_sem.at[n, index],
            recv_sem=recv_sem.at[n, index],
            device_id=(gx + move[0], gy + move[1]),
            device_id_type=MESH,
        )
        return copy, exists(*move), exists(-move[0], -move[1])

    def message(n, index):
        p = n % 2
        if index < 2:
            move = (1, 0) if index == 0 else (-1, 0)
            source = half.at[p, :, pl.ds(C if index == 0 else 2, 2)]
            target = half.at[p, :, pl.ds(0 if index == 0 else C + 2, 2)]
        else:
            move = (1 if index < 4 else -1, 1 if index % 2 == 0 else -1)
            source = half.at[
                p, pl.ds(0, 2), C + 1 if move[0] == 1 else 2, pl.ds(16 if move[1] == 1 else 0, 16)
            ]
            target = side_in.at[p, 0 if move[1] == 1 else 1, 0 if move[0] == 1 else TILES + 1, pl.ds(0, 2)]
        return send(n, move, source, target, index)

    def tiles(n, k):
        return [
            send(
                n,
                (0, 1) if s == 0 else (0, -1),
                side_out.at[n % 2, s, k],
                side_in.at[n % 2, s, k + 1],
                6 + TILES * s + k,
            )
            for s in range(2)
        ]

    def start(messages):
        for copy, there, _ in messages:

            @pl.when(there)
            def _():
                copy.start()

    def arrive(messages):
        for copy, _, here in messages:

            @pl.when(here)
            def _():
                copy.wait_recv()

    def everything(n):
        return [message(n, index) for index in range(6)] + [one for k in range(TILES) for one in tiles(n, k)]

    def sent(n):
        for copy, there, _ in everything(n):

            @pl.when(there)
            def _():
                copy.wait_send()

    def fill(n, k):
        p = n % 2
        place = lax.broadcasted_iota(jnp.int32, (8, NZ), 0)
        for c in range(3):
            for s, y in ((0, C - 2), (1, 0)):
                rows = [jnp.zeros((8, NZ), F32)] * 2
                for x in range(8):
                    tile = field[p, c, pl.ds((8 * k + x) * C + y // 8 * 8, 8)]
                    for j in range(2):
                        line = jnp.broadcast_to(tile[y % 8 + j : y % 8 + j + 1], (8, NZ))
                        rows[j] = jnp.where(place == x, line, rows[j])
                side_out[p, s, k, c] = below(*rows).astype(BF)

    def publish(n, i):
        @pl.when(i == 0)
        def _():
            start([message(n, index) for index in (0, 2, 3)])

        @pl.when(i == 1)
        def _():
            start([message(n, index) for index in (1, 4, 5)])

        for at, k in ((2, 3), (4, 0), (5, 2), (7, 1)):

            @pl.when(i == at)
            def _():
                fill(n, k)
                start(tiles(n, k))

    def receive(n, i):
        @pl.when(i == 0)
        def _():
            arrive([message(n, index) for index in (1, 4, 5)] + tiles(n, 3))

        @pl.when(i == 1)
        def _():
            arrive([message(n, index) for index in (0, 2, 3)] + tiles(n, 0))

        @pl.when(i == 2)
        def _():
            arrive(tiles(n, 2))

        @pl.when(i == 4)
        def _():
            arrive(tiles(n, 1))

    def update(n, g, sources):
        p = n % 2
        x = g * XG
        return advance(
            [half[p, c, pl.ds(x, XG + 4)] for c in range(3)],
            *halo_tiles(side_in.at[p], g),
            [field[p, c, rows_at(g)] for c in range(3)],
            [field[1 - p, c, rows_at(g)] for c in range(3)],
            mod[0, rows_at(g)],
            mod[1, rows_at(g)],
            sources,
            *matrices(table, g),
        )

    def injected(n, g):
        values = dot(hot[g].reshape(3 * ROWS, Q), spread[n])
        return [values[ROWS * c : ROWS * c + ROWS] for c in range(3)]

    def keep(n, g, c, fresh):
        field[n % 2, c, rows_at(g)] = fresh
        half[n % 2, c, pl.ds(g * XG + 2, XG)] = fresh.astype(BF).reshape(XG, C, NZ)

    def to_half(g, carry):
        x = g * XG
        for c in range(3):
            half[0, c, pl.ds(x + 2, XG)] = field[0, c, rows_at(g)].astype(BF).reshape(XG, C, NZ)
        return carry

    loads[0].wait()
    lax.fori_loop(0, GROUPS, to_half, 0)
    start([message(0, index) for index in range(6)])
    for k in range(TILES):
        fill(0, k)
        start(tiles(0, k))

    for load in slot_loads:
        load.wait()
    first_row = py % 2 * 4
    mask = NK * NR // 2 - 1
    across = lax.broadcasted_iota(jnp.int32, (128, 128), 1)
    along = lax.broadcasted_iota(jnp.int32, (128, 128), 0)
    odd_index = 2 * (along + (core * 4 + px) * 128) + 1

    def cosines(t, carry):
        q = slot_tile[0, t // 4, pl.ds(first_row + t % 4, 1)]
        turns = odd_index * q
        turns = ((turns + (mask + 1) // 2) & mask) - (mask + 1) // 2
        s = sine(turns.astype(F32) * (math.pi / (mask + 1)))
        basis[t] = (1.0 - 2.0 * s * s).astype(BF)
        return carry

    lax.fori_loop(0, 16, cosines, 0)
    returns = []
    for k in range(1, 8):
        to = (px + k // 2) % 4 * 2 + (core + k) % 2
        returns.append(
            pltpu.make_async_remote_copy(
                src_ref=part_out.at[to],
                dst_ref=part_in.at[k],
                send_sem=rsend_sem.at[k],
                recv_sem=rrecv_sem.at[k],
                device_id=owner(k),
                device_id_type=MESH,
            )
        )
    def build_hot(g, carry):
        ids = lax.broadcasted_iota(jnp.int32, (ROWS, Q), 0) + g * ROWS
        columns = target_ref[...] // NZ
        for c in range(3):
            same = ids + c * C * C == columns
            hot[g, c] = jnp.where(same, 1.0, 0.0).astype(BF)
        return carry

    lax.fori_loop(0, GROUPS, build_hot, 0)
    for h in range(2):
        depth = lane_spread(target_ref[:, 128 * h : 128 * h + 128] % NZ)
        for b in range(2):
            depth_hot[128 * h : 128 * h + 128, 128 * b : 128 * b + 128] = jnp.where(
                across + 128 * b == depth, 1.0, 0.0
            ).astype(BF)
    def sum_up():
        for copy in gathers:
            copy.wait()
        total = jnp.transpose(gathered[...].reshape(128, 128))
        upper = total.astype(BF)
        lower = (total - upper.astype(F32)).astype(BF)
        both = beside(upper, lower)

        def partial(u, carry):
            cos = beside(basis[2 * u], basis[2 * u + 1])
            sums = dot(both, below(cos, cos))
            row = first_row + u % 2 * 2
            level = beside(*[slot_tile[1, u // 2, pl.ds(row + h, 1)] for h in range(2)])
            depth = lax.broadcasted_iota(jnp.int32, (STEPS * ND, Q), 0) % ND
            sums = jnp.where(depth == level, sums, 0.0).reshape(STEPS, ND, Q)
            sums = jnp.sum(sums, axis=1)
            part_out[u] = below(sums[:, :128], sums[:, 128:])
            return carry

        lax.fori_loop(0, 8, partial, 0)
        for copy in returns:
            copy.start()

    loads[1].wait()
    loads[2].wait()

    def first_step(i, carry):
        receive(0, i)
        pl.when(i == 2)(sum_up)
        g = group_at(i)
        result = update(0, g, None)
        for c in range(3):
            field[1, c, rows_at(g)] = result[c]
        return carry

    lax.fori_loop(0, GROUPS, first_step, 0)
    for copy in returns:
        copy.wait()
    traces = part_out[px * 2 + core]
    for k in range(1, 8):
        traces = traces + part_in[k]
    slot = lax.broadcasted_iota(jnp.int32, (8, 128), 1) + lax.broadcasted_iota(jnp.int32, (8, 128), 0) // 4 * 128
    traces = jnp.where(slot < live_ref[0], traces, 0.0)
    for h in range(2):
        part = slice(128 * h, 128 * h + 128)
        for n in range(STEPS):
            line = jnp.broadcast_to(traces[4 * h + n : 4 * h + n + 1], (128, 128))
            diagonal = jnp.where(along == across, line, 0.0).astype(BF)
            spread[n, part] = dot(diagonal, depth_hot[part]).astype(BF)

    def first_sources(i, carry):
        g = group_at(i)
        sources = injected(0, g)
        for c in range(3):
            keep(1, g, c, field[1, c, rows_at(g)] + sources[c])
        publish(1, i)
        return carry

    lax.fori_loop(0, GROUPS, first_sources, 0)

    spread_store = pltpu.make_async_copy(spread.at[STEPS - 1], spread_hbm, store_sem.at[0])
    spread_store.start()
    prior_store = pltpu.make_async_copy(field.at[0], prior_hbm, store_sem.at[1])

    def last_stores(g):
        x = g * XG
        return (
            pltpu.make_async_copy(
                field.at[1, :, rows_at(g)], last_hbm.at[:, rows_at(g)], group_sem.at[0, g]
            ),
            pltpu.make_async_copy(
                half.at[1, :, pl.ds(x + 2, XG)], half_hbm.at[:, pl.ds(x + 2, XG)], group_sem.at[1, g]
            ),
        )

    for n in range(1, STEPS - 1):
        sent(n - 1)
        if n == STEPS - 2:
            prior_store.start()

        def later_step(i, carry):
            receive(n, i)
            g = group_at(i)
            result = update(n, g, injected(n, g))
            for c in range(3):
                keep(n + 1, g, c, result[c])
            publish(n + 1, i)
            if n == STEPS - 2:
                for store in last_stores(g):
                    store.start()
            return carry

        lax.fori_loop(0, GROUPS, later_step, 0)

    last = STEPS - 1
    arrive([message(last, index) for index in (0, 1)])
    ends = [
        pltpu.make_async_copy(half.at[1, :, pl.ds(x, 2)], half_hbm.at[:, pl.ds(x, 2)], store_sem.at[k])
        for x, k in ((0, 2), (C + 2, 3))
    ]
    for store in ends:
        store.start()
    arrive(everything(last)[2:])
    side_store = pltpu.make_async_copy(side_in.at[1], side_hbm, store_sem.at[5])
    side_store.start()
    sent(last - 1)
    sent(last)
    for store in (spread_store, prior_store, *ends, side_store):
        store.wait()

    def drain(g, carry):
        for store in last_stores(g):
            store.wait()
        return carry

    lax.fori_loop(0, GROUPS, drain, 0)


def last_kernel(
    target_ref,
    table_hbm, half_hbm, side_hbm, spread_hbm, now_hbm, before_hbm, moduli_hbm,
    final_hbm, copy_hbm,
    table, half, side, spread, now, before, mod, final,
    sem, half_sem, load_sem, store_sem,
):
    small = [
        pltpu.make_async_copy(source, target, sem.at[k])
        for k, (source, target) in enumerate(
            (
                (table_hbm.at[pl.ds(0, SHORT)], table),
                (spread_hbm, spread),
                (side_hbm, side),
            )
        )
    ]

    def half_load(k):
        x = k * XG
        return pltpu.make_async_copy(half_hbm.at[:, pl.ds(x, XG)], half.at[:, pl.ds(x, XG)], half_sem.at[k])

    def group_loads(g):
        part = rows_at(g)
        return [
            pltpu.make_async_copy(source.at[:, part], target.at[:, part], load_sem.at[k, g])
            for k, (source, target) in enumerate(
                ((now_hbm, now), (before_hbm, before), (moduli_hbm, mod))
            )
        ]

    def group_stores(g):
        part = rows_at(g)
        return [
            pltpu.make_async_copy(source.at[:, part], target.at[:, part], store_sem.at[k, g])
            for k, (source, target) in enumerate(((final, final_hbm), (now, copy_hbm)))
        ]

    def begin(g):
        half_load(g + 1).start()
        for load in group_loads(g):
            load.start()

    half_load(0).start()
    small[0].start()
    begin(0)
    for load in small[1:]:
        load.start()
    for g in range(1, GROUPS):
        begin(g)
    half_load(0).wait()
    for load in small:
        load.wait()

    def group(g, carry):
        x = g * XG

        half_load(g + 1).wait()
        for load in group_loads(g):
            load.wait()
        stores = group_stores(g)
        stores[1].start()
        ids = lax.broadcasted_iota(jnp.int32, (ROWS, Q), 0) + g * ROWS
        columns = target_ref[...] // NZ
        hot = [jnp.where(ids + c * C * C == columns, 1.0, 0.0).astype(BF) for c in range(3)]
        values = dot(below(*hot), spread[...])
        result = advance(
            [half[c, pl.ds(x, XG + 4)] for c in range(3)],
            *halo_tiles(side, g),
            [now[c, rows_at(g)] for c in range(3)],
            [before[c, rows_at(g)] for c in range(3)],
            mod[0, rows_at(g)],
            mod[1, rows_at(g)],
            [values[ROWS * c : ROWS * c + ROWS] for c in range(3)],
            *matrices(table, g),
        )
        for c in range(3):
            final[c, rows_at(g)] = result[c]
        stores[0].start()
        return carry

    lax.fori_loop(0, GROUPS, group, 0)

    def drain(g, carry):
        for store in group_stores(g):
            store.wait()
        return carry

    lax.fori_loop(0, GROUPS, drain, 0)


def shards(
    layer_slowness, layer_rigidity, layer_damping, layer_of_level,
    slot_offset, slot_level, slot_target, live_count, moduli, field_old, field_now,
):
    fixed = jnp.asarray(constants())
    smem = pl.BlockSpec(memory_space=pltpu.SMEM)
    vmem = pl.BlockSpec(memory_space=pltpu.VMEM)
    any_space = pl.BlockSpec(memory_space=pl.ANY)
    target = slot_target.reshape(1, Q)
    block = jax.ShapeDtypeStruct((3, C * C, NZ), F32)
    whole = (3, C, C, NZ)
    moduli = moduli.reshape(2, C * C, NZ)
    field_old, field_now = field_old.reshape(block.shape), field_now.reshape(block.shape)
    dma = pltpu.SemaphoreType.DMA
    last, prior, half, side, spread = pl.pallas_call(
        main_kernel,
        out_shape=[
            block,
            block,
            jax.ShapeDtypeStruct((3, C + 4, C, NZ), BF),
            jax.ShapeDtypeStruct((2, TILES + 2, 3, 16, NZ), BF),
            jax.ShapeDtypeStruct((Q, NZ), BF),
        ],
        in_specs=[smem] * 5 + [vmem] + [any_space] * 6,
        out_specs=[any_space] * 5,
        scratch_shapes=[
            pltpu.VMEM((2, 3, C * C, NZ), F32),
            pltpu.VMEM((2, C * C, NZ), F32),
            pltpu.VMEM((2, 3, C + 4, C, NZ), BF),
            pltpu.VMEM((2, 2, TILES, 3, 16, NZ), BF),
            pltpu.VMEM((2, 2, TILES + 2, 3, 16, NZ), BF),
            pltpu.VMEM((GROUPS, 3, ROWS, Q), BF),
            pltpu.VMEM((16, 8, 128), F32),
            pltpu.VMEM((16, 128, 128), BF),
            pltpu.VMEM((STEPS, Q, NZ), BF),
            pltpu.VMEM((Q, NZ), BF),
            pltpu.VMEM((8, 8, 128), F32),
            pltpu.VMEM((8, 8, 128), F32),
            pltpu.VMEM((TABLE, NZ), BF),
            pltpu.VMEM((2, 4, 8, 128), jnp.int32),
            pltpu.VMEM((ND + 1, 8, 128), F32),
            pltpu.VMEM((2, ND, 8, 128), F32),
            pltpu.VMEM((2, ND, 8, 128), F32),
            pltpu.VMEM((ND, 8, 2 * F), F32),
            dma((4,)),
            dma((6,)),
            dma((2, GROUPS)),
            dma((STEPS, LINKS)),
            dma((STEPS, LINKS)),
            dma((16,)),
            dma((16,)),
            dma((2, 4)),
            dma((8,)),
            dma((8,)),
        ],
        compiler_params=pltpu.CompilerParams(
            collective_id=0, has_side_effects=True, vmem_limit_bytes=VMEM
        ),
    )(
        layer_slowness, layer_rigidity, layer_damping, layer_of_level, live_count, target,
        fixed,
        slot_offset.reshape(Q, 128), slot_level.reshape(Q, 128), moduli, field_old, field_now,
    )

    final, copied = pl.pallas_call(
        last_kernel,
        out_shape=[block, block],
        in_specs=[vmem] + [any_space] * 7,
        out_specs=[any_space] * 2,
        scratch_shapes=[
            pltpu.VMEM((SHORT, NZ), BF),
            pltpu.VMEM(half.shape, BF),
            pltpu.VMEM(side.shape, BF),
            pltpu.VMEM(spread.shape, BF),
            pltpu.VMEM(block.shape, F32),
            pltpu.VMEM(block.shape, F32),
            pltpu.VMEM(moduli.shape, F32),
            pltpu.VMEM(block.shape, F32),
            dma((3,)),
            dma((GROUPS + 1,)),
            dma((3, GROUPS)),
            dma((2, GROUPS)),
        ],
        compiler_params=pltpu.CompilerParams(vmem_limit_bytes=VMEM),
    )(target, fixed, half, side, spread, last, prior, moduli)
    return final.reshape(whole), copied.reshape(whole)


def solution(mesh):
    in_specs = (
        P(),
        P(),
        P(),
        P(),
        P(),
        P(),
        P(("gx", "gy")),
        P(("gx", "gy")),
        P(None, "gx", "gy", None),
        P(None, "gx", "gy", None),
        P(None, "gx", "gy", None),
    )
    out_specs = (P(None, "gx", "gy", None), P(None, "gx", "gy", None))
    return jax.shard_map(shards, mesh=mesh, in_specs=in_specs, out_specs=out_specs, check_vma=False)
```

```python
import functools
import math

import jax
import jax.numpy as jnp
import ml_dtypes
import numpy as np
from jax import lax
from jax.experimental import pallas as pl
from jax.experimental.pallas import tpu as pltpu
from jax.sharding import PartitionSpec as P

F = 128
NK = 1024
NR = 2048
ND = 32
STEPS = 4
TSTART = 32
GX = 16
GY = 8
C = 32
NZ = 256
Q = 256
GROUPS = 8
XG = 4
ROWS = XG * C
TILES = 4
LINKS = 6 + 2 * TILES
ORDER = (7, 0, 6, 5, 1, 4, 2, 3)
VMEM = 63 * 1024 * 1024
MESH = pl.DeviceIdType.MESH
BF = jnp.bfloat16
F32 = jnp.float32


def constants():
    low, high = ROWS, ROWS + 16

    def place(x, y, half):
        if y < 0:
            return low + 8 * (y + 2) + x + XG * half
        if y >= C:
            return high + 8 * (y - C) + x + XG * half
        return x * C + y

    y2 = np.zeros((2, ROWS, ROWS + 32), np.float32)
    y1 = np.zeros((2, ROWS, ROWS + 32), np.float32)
    for half in range(2):
        for x in range(XG):
            for y in range(C):
                row = x * C + y
                for shift, factor in ((-2, -1.0), (-1, 16.0), (1, 16.0), (2, -1.0)):
                    y2[half, row, place(x, y + shift, half)] += factor
                y1[half, row, place(x, y + 1, half)] += 1.0
                y1[half, row, place(x, y - 1, half)] -= 1.0
    cross = np.zeros((4, ROWS, ROWS + 96), np.float32)
    for kind in range(4):
        half = kind // 2
        cross[kind, :, :ROWS] = 3.0 * y1[half, :, :ROWS]
        cross[kind, :, ROWS + 64 :] = 3.0 * y1[half, :, ROWS:]
        for x in range(XG):
            for y, beyond, sign in ((0, -1, -3.0), (C - 1, C, 3.0)):
                for step in (-1, 1):
                    if (half == 0 and x + step < 0) or (half == 1 and x + step >= XG):
                        spot = ROWS + (32 if beyond < 0 else 48)
                        if kind in (0, 3):
                            spot += 15 if beyond < 0 else 0
                        else:
                            spot += (8 if beyond < 0 else 0) + (7 if half == 0 else 0)
                    else:
                        spot = place(x + step, beyond, half)
                    cross[kind, x * C + y, spot] += sign * step
    z2 = np.zeros((NZ, NZ), np.float32)
    z1 = np.zeros((NZ, NZ), np.float32)
    for z in range(NZ):
        for shift, factor in ((-2, -1.0), (-1, 16.0), (1, 16.0), (2, -1.0)):
            if 0 <= z + shift < NZ:
                z2[z + shift, z] += factor
        if z + 1 < NZ:
            z1[z + 1, z] += 1.0
        if z > 0:
            z1[z - 1, z] -= 1.0
    period = 2 * F
    turns = (np.arange(F)[None, :] + 1) * (TSTART + np.arange(STEPS)[:, None]) % period
    angles = turns * (2.0 * math.pi / period)
    weight = 1.0 / math.sqrt(F)
    waves = np.concatenate([weight * np.cos(angles), -weight * np.sin(angles)], axis=1).T
    waves = np.repeat(waves.astype(np.float32), ND, axis=1)
    upper = waves.astype(ml_dtypes.bfloat16)
    lower = (waves - upper.astype(np.float32)).astype(ml_dtypes.bfloat16)
    half = ml_dtypes.bfloat16
    parts = [*y2, *y1, *cross, z2, z1, 3.0 * z1]
    parts = [np.pad(part, ((0, 0), (0, 256 - part.shape[1]))).astype(half) for part in parts]
    return np.concatenate(parts + [np.concatenate([upper, lower], axis=1)])


AT_Y2, AT_Y1, AT_CROSS, AT_Z2, AT_Z1, AT_Z3 = 0, 256, 512, 1024, 1280, 1536
AT_WAVES, TABLE = 1792, 2048
SHORT = AT_WAVES


def matrices(table, g):
    kind = jnp.where(g == 0, 0, jnp.where(g == GROUPS - 1, 3, 1 + g % 2))

    def part(at, k):
        return table[pl.ds(pl.multiple_of(at + ROWS * k, ROWS), ROWS)]

    return (
        part(AT_Y2, g % 2)[:, : ROWS + 32],
        part(AT_Y1, g % 2)[:, : ROWS + 32],
        part(AT_CROSS, kind),
        table[AT_Z2 : AT_Z2 + NZ],
        table[AT_Z1 : AT_Z1 + NZ],
        table[AT_Z3 : AT_Z3 + NZ],
    )


def halo_tiles(side, g):
    own = g // 2 + 1
    other = own - 1 + 2 * (g % 2)
    return (
        [side[0, own, c] for c in range(3)],
        [side[1, own, c] for c in range(3)],
        [side[0, other, c] for c in range(2)],
        [side[1, other, c] for c in range(2)],
    )


def rows_at(g):
    return pl.ds(pl.multiple_of(g * ROWS, ROWS), ROWS)


def group_at(i):
    g = ORDER[-1]
    for k in range(GROUPS - 1):
        g = jnp.where(i == k, ORDER[k], g)
    return g


def dot(a, b):
    return jnp.dot(a, b, preferred_element_type=F32)


def beside(*parts):
    return jnp.concatenate(parts, axis=1)


def below(*parts):
    return jnp.concatenate(parts, axis=0)


def advance(window, lows, highs, clows, chighs, now, before, lam, mu, sources, y2, y1, cross, z2, z1, z3):
    wide = [w.astype(F32) for w in window]
    inner = [w[2 : 2 + XG].reshape(ROWS, NZ) for w in window]
    second = [(16.0 * (w[1:5] + w[3:7]) - (w[0:4] + w[4:8])).reshape(ROWS, NZ) for w in wide]
    first = [(w[3:7] - w[1:5]).reshape(ROWS, NZ) for w in wide]
    tall = [below(inner[c], lows[c], highs[c]) for c in range(3)]
    skew_z = dot(tall[2], z1)
    skew_y = dot(y1, tall[1])
    lap = [dot(beside(inner[c], y2), below(z2, tall[c])) for c in range(3)]
    mix_0 = dot(
        beside(first[2].astype(BF), cross[:, : ROWS + 64]),
        below(z3, first[1].astype(BF), lows[1], highs[1], clows[1], chighs[1]),
    )
    mix_1 = dot(
        beside(cross, y2),
        below(
            (first[0] + skew_z[:ROWS]).astype(BF), lows[0], highs[0], clows[0], chighs[0],
            skew_z[ROWS:].astype(BF), lows[0], highs[0], tall[1],
        ),
    )
    mix_2 = dot(beside(inner[2], (first[0] + skew_y).astype(BF)), below(z2, z3))
    couple = [second[0] + mix_0, mix_1, mix_2]
    shear = mu * (1.0 / 12.0)
    joint = (lam + mu) * (1.0 / 12.0)
    centre = 2.0 - 90.0 * shear - 30.0 * joint
    result = []
    for c in range(3):
        moved = shear * (second[c] + lap[c]) + joint * couple[c]
        if sources is not None:
            moved = moved + sources[c]
        result.append((centre * now[c] - before[c]) + moved)
    return result


def sine(x):
    y = x * x
    poly = -2.5052108e-08
    for coefficient in (2.7557319e-06, -1.9841270e-04, 8.3333333e-03, -1.6666667e-01, 1.0):
        poly = poly * y + coefficient
    return x * poly


def cosine(x):
    y = x * x
    poly = -2.7557319e-07
    for coefficient in (2.4801587e-05, -1.3888889e-03, 4.1666667e-02, -0.5, 1.0):
        poly = poly * y + coefficient
    return poly


def lane_spread(row):
    return jnp.transpose(jnp.broadcast_to(row.astype(F32), (128, 128))).astype(jnp.int32)


def main_kernel(
    slow_ref, rigid_ref, damp_ref, level_ref, live_ref, target_ref,
    table_hbm, offsets_hbm, levels_hbm, moduli_hbm, old_hbm, now_hbm,
    last_hbm, prior_hbm, half_hbm, side_hbm, spread_hbm,
    field, mod, half, side_out, side_in, hot, gathered, basis, spread,
    depth_hot, part_out, part_in,
    table, slot_tile, zbuf, ebuf, dbuf, kbuf,
    load_sem, store_sem, group_sem, send_sem, recv_sem, gsend_sem, grecv_sem,
    slot_sem, rsend_sem, rrecv_sem,
):
    gx = lax.axis_index("gx")
    gy = lax.axis_index("gy")
    device = gx * GY + gy
    px, pz = gx // 4, gx % 4
    py, core = gy // 2, gy % 2
    block = core * 64 + px * 16 + pz * 4 + py

    loads = [
        pltpu.make_async_copy(now_hbm, field.at[0], load_sem.at[0]),
        pltpu.make_async_copy(old_hbm, field.at[1], load_sem.at[1]),
        pltpu.make_async_copy(moduli_hbm, mod, load_sem.at[2]),
        pltpu.make_async_copy(table_hbm, table, load_sem.at[3]),
    ]
    slot_loads = []
    for x in range(4):
        at = pl.ds(pl.multiple_of(x * 64 + pz * 16 + py // 2 * 8, 8), 8)
        for k, ref in enumerate((offsets_hbm, levels_hbm)):
            slot_loads.append(pltpu.make_async_copy(ref.at[at], slot_tile.at[k, x], slot_sem.at[k, x]))
    for load in loads[:1] + slot_loads + loads[3:] + loads[1:3]:
        load.start()

    for p in range(2):
        half[p, :, 0:2] = jnp.zeros((3, 2, C, NZ), BF)
        half[p, :, C + 2 : C + 4] = jnp.zeros((3, 2, C, NZ), BF)
        for s in range(2):
            side_in[p, s] = jnp.zeros(side_in.shape[2:], BF)

    steps = [(1, 0), (-1, 0), (0, 1), (0, -1), (1, 1), (1, -1), (-1, 1), (-1, -1)]

    def exists(dx, dy):
        ok = None
        for delta, place, size in ((dx, gx, GX), (dy, gy, GY)):
            if delta == 1:
                part = place < size - 1
            elif delta == -1:
                part = place > 0
            else:
                continue
            ok = part if ok is None else jnp.logical_and(ok, part)
        return ok

    barrier = pltpu.get_barrier_semaphore()
    for dx, dy in steps:
        @pl.when(exists(dx, dy))
        def _():
            pl.semaphore_signal(barrier, inc=1, device_id=(gx + dx, gy + dy), device_id_type=MESH)

    def in_plane(k):
        return (px * 4 + (pz + k // 4) % 4, (py + k % 4) % 4 * 2 + core)

    def owner(k):
        return ((px + k // 2) % 4 * 4 + pz, py * 2 + (core + k) % 2)

    for k in range(1, 16):
        pl.semaphore_signal(barrier, inc=1, device_id=in_plane(k), device_id_type=MESH)
    for k in range(1, 8):
        pl.semaphore_signal(barrier, inc=1, device_id=owner(k), device_id_type=MESH)

    rows = lax.broadcasted_iota(jnp.int32, (8, 128), 0) + block * 8
    wavenum = (rows.astype(F32) + 0.5) * (4.0 / NK)
    square_k = wavenum * wavenum
    omega = (lax.broadcasted_iota(jnp.int32, (8, 128), 1) + 1).astype(F32) * (4.0 / F)

    def downward(i, carry):
        down_re, down_im = carry
        layer = level_ref[i]
        part = omega * slow_ref[layer]
        vertical = jnp.sqrt(square_k + part * part)
        fade = jnp.exp(vertical * (-0.25 * damp_ref[layer]))
        angle = 0.125 * vertical
        s, c = sine(angle), cosine(angle)
        leg_re = fade * (1.0 - 2.0 * s * s)
        leg_im = fade * (-2.0 * s * c)
        zbuf[i] = rigid_ref[layer] * vertical
        ebuf[0, i] = leg_re
        ebuf[1, i] = leg_im
        dbuf[0, i] = down_re
        dbuf[1, i] = down_im
        return down_re * leg_re - down_im * leg_im, down_re * leg_im + down_im * leg_re

    one = jnp.ones((8, 128), F32)
    zero = jnp.zeros((8, 128), F32)
    lax.fori_loop(0, ND, downward, (one, zero), unroll=4)
    zbuf[ND] = zbuf[ND - 1]

    def upward(step, carry):
        refl_re, refl_im = carry
        i = ND - 1 - step
        upper, under = zbuf[i], zbuf[i + 1]
        r = (upper - under) / (upper + under)
        leg_re, leg_im = ebuf[0, i], ebuf[1, i]
        trip_re = leg_re * leg_re - leg_im * leg_im
        trip_im = 2.0 * leg_re * leg_im
        upper_re = r + refl_re
        lower_re = 1.0 + r * refl_re
        lower_im = r * refl_im
        scale = 1.0 / (lower_re * lower_re + lower_im * lower_im)
        ratio_re = (upper_re * lower_re + refl_im * lower_im) * scale
        ratio_im = (refl_im * lower_re - upper_re * lower_im) * scale
        fresh_re = trip_re * ratio_re - trip_im * ratio_im
        fresh_im = trip_re * ratio_im + trip_im * ratio_re
        down_re, down_im = dbuf[0, i], dbuf[1, i]
        kbuf[i, :, 0:128] = (down_re * (1.0 + fresh_re) - down_im * fresh_im) * (1.0 / 32.0)
        kbuf[i, :, 128:256] = (down_re * fresh_im + down_im * (1.0 + fresh_re)) * (1.0 / 32.0)
        return fresh_re, fresh_im

    lax.fori_loop(0, ND, upward, (zero, zero), unroll=4)
    loads[3].wait()
    product = dot(kbuf[...].reshape(ND * 8, 2 * F).astype(BF), table[AT_WAVES : AT_WAVES + 2 * F])
    product = product[:, :128] + product[:, 128:]
    lane = lax.broadcasted_iota(jnp.int32, (8, 128), 1) % ND
    mine = zero
    for d in range(ND):
        mine = jnp.where(lane == d, product[8 * d : 8 * d + 8], mine)
    seat = pz * 4 + py
    gathered[seat] = mine

    count = 22
    for dx, dy in steps:
        count = count + exists(dx, dy).astype(jnp.int32)
    pl.semaphore_wait(barrier, count)

    gathers = [
        pltpu.make_async_remote_copy(
            src_ref=gathered.at[seat],
            dst_ref=gathered.at[seat],
            send_sem=gsend_sem.at[k],
            recv_sem=grecv_sem.at[k],
            device_id=in_plane(k),
            device_id_type=MESH,
        )
        for k in range(1, 16)
    ]
    for copy in gathers:
        copy.start()

    def send(n, move, source, target, index):
        copy = pltpu.make_async_remote_copy(
            src_ref=source,
            dst_ref=target,
            send_sem=send_sem.at[n, index],
            recv_sem=recv_sem.at[n, index],
            device_id=(gx + move[0], gy + move[1]),
            device_id_type=MESH,
        )
        return copy, exists(*move), exists(-move[0], -move[1])

    def message(n, index):
        p = n % 2
        if index < 2:
            move = (1, 0) if index == 0 else (-1, 0)
            source = half.at[p, :, pl.ds(C if index == 0 else 2, 2)]
            target = half.at[p, :, pl.ds(0 if index == 0 else C + 2, 2)]
        else:
            move = (1 if index < 4 else -1, 1 if index % 2 == 0 else -1)
            source = half.at[
                p, pl.ds(0, 2), C + 1 if move[0] == 1 else 2, pl.ds(16 if move[1] == 1 else 0, 16)
            ]
            target = side_in.at[p, 0 if move[1] == 1 else 1, 0 if move[0] == 1 else TILES + 1, pl.ds(0, 2)]
        return send(n, move, source, target, index)

    def tiles(n, k):
        return [
            send(
                n,
                (0, 1) if s == 0 else (0, -1),
                side_out.at[n % 2, s, k],
                side_in.at[n % 2, s, k + 1],
                6 + TILES * s + k,
            )
            for s in range(2)
        ]

    def start(messages):
        for copy, there, _ in messages:

            @pl.when(there)
            def _():
                copy.start()

    def arrive(messages):
        for copy, _, here in messages:

            @pl.when(here)
            def _():
                copy.wait_recv()

    def everything(n):
        return [message(n, index) for index in range(6)] + [one for k in range(TILES) for one in tiles(n, k)]

    def sent(n):
        for copy, there, _ in everything(n):

            @pl.when(there)
            def _():
                copy.wait_send()

    def fill(n, k):
        p = n % 2
        place = lax.broadcasted_iota(jnp.int32, (8, NZ), 0)
        for c in range(3):
            for s, y in ((0, C - 2), (1, 0)):
                rows = [jnp.zeros((8, NZ), F32)] * 2
                for x in range(8):
                    tile = field[p, c, pl.ds((8 * k + x) * C + y // 8 * 8, 8)]
                    for j in range(2):
                        line = jnp.broadcast_to(tile[y % 8 + j : y % 8 + j + 1], (8, NZ))
                        rows[j] = jnp.where(place == x, line, rows[j])
                side_out[p, s, k, c] = below(*rows).astype(BF)

    def publish(n, i):
        @pl.when(i == 0)
        def _():
            start([message(n, index) for index in (0, 2, 3)])

        @pl.when(i == 1)
        def _():
            start([message(n, index) for index in (1, 4, 5)])

        for at, k in ((2, 3), (4, 0), (5, 2), (7, 1)):

            @pl.when(i == at)
            def _():
                fill(n, k)
                start(tiles(n, k))

    def receive(n, i):
        @pl.when(i == 0)
        def _():
            arrive([message(n, index) for index in (1, 4, 5)] + tiles(n, 3))

        @pl.when(i == 1)
        def _():
            arrive([message(n, index) for index in (0, 2, 3)] + tiles(n, 0))

        @pl.when(i == 2)
        def _():
            arrive(tiles(n, 2))

        @pl.when(i == 4)
        def _():
            arrive(tiles(n, 1))

    def update(n, g, sources):
        p = n % 2
        x = g * XG
        return advance(
            [half[p, c, pl.ds(x, XG + 4)] for c in range(3)],
            *halo_tiles(side_in.at[p], g),
            [field[p, c, rows_at(g)] for c in range(3)],
            [field[1 - p, c, rows_at(g)] for c in range(3)],
            mod[0, rows_at(g)],
            mod[1, rows_at(g)],
            sources,
            *matrices(table, g),
        )

    def injected(n, g):
        values = dot(hot[g].reshape(3 * ROWS, Q), spread[n])
        return [values[ROWS * c : ROWS * c + ROWS] for c in range(3)]

    def keep(n, g, c, fresh):
        field[n % 2, c, rows_at(g)] = fresh
        half[n % 2, c, pl.ds(g * XG + 2, XG)] = fresh.astype(BF).reshape(XG, C, NZ)

    def to_half(g, carry):
        x = g * XG
        for c in range(3):
            half[0, c, pl.ds(x + 2, XG)] = field[0, c, rows_at(g)].astype(BF).reshape(XG, C, NZ)
        return carry

    loads[0].wait()
    lax.fori_loop(0, GROUPS, to_half, 0)
    start([message(0, index) for index in range(6)])
    for k in range(TILES):
        fill(0, k)
        start(tiles(0, k))

    for load in slot_loads:
        load.wait()
    first_row = py % 2 * 4
    mask = NK * NR // 2 - 1
    across = lax.broadcasted_iota(jnp.int32, (128, 128), 1)
    along = lax.broadcasted_iota(jnp.int32, (128, 128), 0)
    odd_index = 2 * (along + (core * 4 + px) * 128) + 1

    def cosines(t, carry):
        q = slot_tile[0, t // 4, pl.ds(first_row + t % 4, 1)]
        turns = odd_index * q
        turns = ((turns + (mask + 1) // 2) & mask) - (mask + 1) // 2
        s = sine(turns.astype(F32) * (math.pi / (mask + 1)))
        basis[t] = (1.0 - 2.0 * s * s).astype(BF)
        return carry

    lax.fori_loop(0, 16, cosines, 0)
    returns = []
    for k in range(1, 8):
        to = (px + k // 2) % 4 * 2 + (core + k) % 2
        returns.append(
            pltpu.make_async_remote_copy(
                src_ref=part_out.at[to],
                dst_ref=part_in.at[k],
                send_sem=rsend_sem.at[k],
                recv_sem=rrecv_sem.at[k],
                device_id=owner(k),
                device_id_type=MESH,
            )
        )
    def build_hot(g, carry):
        ids = lax.broadcasted_iota(jnp.int32, (ROWS, Q), 0) + g * ROWS
        columns = target_ref[...] // NZ
        for c in range(3):
            same = ids + c * C * C == columns
            hot[g, c] = jnp.where(same, 1.0, 0.0).astype(BF)
        return carry

    lax.fori_loop(0, GROUPS, build_hot, 0)
    for h in range(2):
        depth = lane_spread(target_ref[:, 128 * h : 128 * h + 128] % NZ)
        for b in range(2):
            depth_hot[128 * h : 128 * h + 128, 128 * b : 128 * b + 128] = jnp.where(
                across + 128 * b == depth, 1.0, 0.0
            ).astype(BF)
    def sum_up():
        for copy in gathers:
            copy.wait()
        total = jnp.transpose(gathered[...].reshape(128, 128))
        upper = total.astype(BF)
        lower = (total - upper.astype(F32)).astype(BF)
        both = beside(upper, lower)

        def partial(u, carry):
            cos = beside(basis[2 * u], basis[2 * u + 1])
            sums = dot(both, below(cos, cos))
            row = first_row + u % 2 * 2
            level = beside(*[slot_tile[1, u // 2, pl.ds(row + h, 1)] for h in range(2)])
            depth = lax.broadcasted_iota(jnp.int32, (STEPS * ND, Q), 0) % ND
            sums = jnp.where(depth == level, sums, 0.0).reshape(STEPS, ND, Q)
            sums = jnp.sum(sums, axis=1)
            part_out[u] = below(sums[:, :128], sums[:, 128:])
            return carry

        lax.fori_loop(0, 8, partial, 0)
        for copy in returns:
            copy.start()

    loads[1].wait()
    loads[2].wait()

    def first_step(i, carry):
        receive(0, i)
        pl.when(i == 2)(sum_up)
        g = group_at(i)
        result = update(0, g, None)
        for c in range(3):
            field[1, c, rows_at(g)] = result[c]
        return carry

    lax.fori_loop(0, GROUPS, first_step, 0)
    for copy in returns:
        copy.wait()
    traces = part_out[px * 2 + core]
    for k in range(1, 8):
        traces = traces + part_in[k]
    slot = lax.broadcasted_iota(jnp.int32, (8, 128), 1) + lax.broadcasted_iota(jnp.int32, (8, 128), 0) // 4 * 128
    traces = jnp.where(slot < live_ref[0], traces, 0.0)
    for h in range(2):
        part = slice(128 * h, 128 * h + 128)
        for n in range(STEPS):
            line = jnp.broadcast_to(traces[4 * h + n : 4 * h + n + 1], (128, 128))
            diagonal = jnp.where(along == across, line, 0.0).astype(BF)
            spread[n, part] = dot(diagonal, depth_hot[part]).astype(BF)

    def first_sources(i, carry):
        g = group_at(i)
        sources = injected(0, g)
        for c in range(3):
            keep(1, g, c, field[1, c, rows_at(g)] + sources[c])
        publish(1, i)
        return carry

    lax.fori_loop(0, GROUPS, first_sources, 0)

    spread_store = pltpu.make_async_copy(spread.at[STEPS - 1], spread_hbm, store_sem.at[0])
    spread_store.start()
    prior_store = pltpu.make_async_copy(field.at[0], prior_hbm, store_sem.at[1])

    def last_stores(g):
        return [
            pltpu.make_async_copy(
                field.at[1, :, rows_at(g)], last_hbm.at[:, rows_at(g)], group_sem.at[g]
            )
        ]

    for n in range(1, STEPS - 1):
        sent(n - 1)
        if n == STEPS - 2:
            prior_store.start()

        def later_step(i, carry):
            receive(n, i)
            g = group_at(i)
            result = update(n, g, injected(n, g))
            for c in range(3):
                keep(n + 1, g, c, result[c])
            publish(n + 1, i)
            if n == STEPS - 2:
                for store in last_stores(g):
                    store.start()
            return carry

        lax.fori_loop(0, GROUPS, later_step, 0)

    last = STEPS - 1
    arrive([message(last, index) for index in (0, 1)])
    ends = [
        pltpu.make_async_copy(half.at[1, :, pl.ds(x, 2)], half_hbm.at[:, pl.ds(2 * k - 4, 2)], store_sem.at[k])
        for x, k in ((0, 2), (C + 2, 3))
    ]
    for store in ends:
        store.start()
    arrive(everything(last)[2:])
    side_store = pltpu.make_async_copy(side_in.at[1], side_hbm, store_sem.at[5])
    side_store.start()
    sent(last - 1)
    sent(last)
    for store in (spread_store, prior_store, *ends, side_store):
        store.wait()

    def drain(g, carry):
        for store in last_stores(g):
            store.wait()
        return carry

    lax.fori_loop(0, GROUPS, drain, 0)


def last_kernel(
    target_ref,
    table_hbm, half_hbm, side_hbm, spread_hbm, now_hbm, before_hbm, moduli_hbm,
    final_hbm, copy_hbm,
    table, half, side, spread, now, before, mod, final,
    sem, load_sem, store_sem,
):
    small = [
        pltpu.make_async_copy(source, target, sem.at[k])
        for k, (source, target) in enumerate(
            (
                (table_hbm.at[pl.ds(0, SHORT)], table),
                (spread_hbm, spread),
                (side_hbm, side),
                (half_hbm.at[:, pl.ds(0, 2)], half.at[:, pl.ds(0, 2)]),
                (half_hbm.at[:, pl.ds(2, 2)], half.at[:, pl.ds(C + 2, 2)]),
            )
        )
    ]

    def group_loads(g):
        part = rows_at(g)
        return [
            pltpu.make_async_copy(source.at[:, part], target.at[:, part], load_sem.at[k, g])
            for k, (source, target) in enumerate(
                ((now_hbm, now), (before_hbm, before), (moduli_hbm, mod))
            )
        ]

    def group_stores(g):
        part = rows_at(g)
        return [
            pltpu.make_async_copy(source.at[:, part], target.at[:, part], store_sem.at[k, g])
            for k, (source, target) in enumerate(((final, final_hbm), (now, copy_hbm)))
        ]

    for load in small:
        load.start()

    def begin_one(g, carry):
        for load in group_loads(g):
            load.start()
        return carry

    lax.fori_loop(0, GROUPS, begin_one, 0)
    for load in small:
        load.wait()

    def to_half(g):
        for load in group_loads(g):
            load.wait()
        for c in range(3):
            half[c, pl.ds(g * XG + 2, XG)] = now[c, rows_at(g)].astype(BF).reshape(XG, C, NZ)

    to_half(0)

    def group(g, carry):
        x = g * XG

        stores = group_stores(g)
        stores[1].start()

        @pl.when(g < GROUPS - 1)
        def _():
            to_half(g + 1)

        ids = lax.broadcasted_iota(jnp.int32, (ROWS, Q), 0) + g * ROWS
        columns = target_ref[...] // NZ
        hot = [jnp.where(ids + c * C * C == columns, 1.0, 0.0).astype(BF) for c in range(3)]
        values = dot(below(*hot), spread[...])
        result = advance(
            [half[c, pl.ds(x, XG + 4)] for c in range(3)],
            *halo_tiles(side, g),
            [now[c, rows_at(g)] for c in range(3)],
            [before[c, rows_at(g)] for c in range(3)],
            mod[0, rows_at(g)],
            mod[1, rows_at(g)],
            [values[ROWS * c : ROWS * c + ROWS] for c in range(3)],
            *matrices(table, g),
        )
        for c in range(3):
            final[c, rows_at(g)] = result[c]
        stores[0].start()
        return carry

    lax.fori_loop(0, GROUPS, group, 0)

    def drain(g, carry):
        for store in group_stores(g):
            store.wait()
        return carry

    lax.fori_loop(0, GROUPS, drain, 0)


def shards(
    layer_slowness, layer_rigidity, layer_damping, layer_of_level,
    slot_offset, slot_level, slot_target, live_count, moduli, field_old, field_now,
):
    fixed = jnp.asarray(constants())
    smem = pl.BlockSpec(memory_space=pltpu.SMEM)
    vmem = pl.BlockSpec(memory_space=pltpu.VMEM)
    any_space = pl.BlockSpec(memory_space=pl.ANY)
    target = slot_target.reshape(1, Q)
    block = jax.ShapeDtypeStruct((3, C * C, NZ), F32)
    whole = (3, C, C, NZ)
    moduli = moduli.reshape(2, C * C, NZ)
    field_old, field_now = field_old.reshape(block.shape), field_now.reshape(block.shape)
    dma = pltpu.SemaphoreType.DMA
    last, prior, half, side, spread = pl.pallas_call(
        main_kernel,
        out_shape=[
            block,
            block,
            jax.ShapeDtypeStruct((3, 4, C, NZ), BF),
            jax.ShapeDtypeStruct((2, TILES + 2, 3, 16, NZ), BF),
            jax.ShapeDtypeStruct((Q, NZ), BF),
        ],
        in_specs=[smem] * 5 + [vmem] + [any_space] * 6,
        out_specs=[any_space] * 5,
        scratch_shapes=[
            pltpu.VMEM((2, 3, C * C, NZ), F32),
            pltpu.VMEM((2, C * C, NZ), F32),
            pltpu.VMEM((2, 3, C + 4, C, NZ), BF),
            pltpu.VMEM((2, 2, TILES, 3, 16, NZ), BF),
            pltpu.VMEM((2, 2, TILES + 2, 3, 16, NZ), BF),
            pltpu.VMEM((GROUPS, 3, ROWS, Q), BF),
            pltpu.VMEM((16, 8, 128), F32),
            pltpu.VMEM((16, 128, 128), BF),
            pltpu.VMEM((STEPS, Q, NZ), BF),
            pltpu.VMEM((Q, NZ), BF),
            pltpu.VMEM((8, 8, 128), F32),
            pltpu.VMEM((8, 8, 128), F32),
            pltpu.VMEM((TABLE, NZ), BF),
            pltpu.VMEM((2, 4, 8, 128), jnp.int32),
            pltpu.VMEM((ND + 1, 8, 128), F32),
            pltpu.VMEM((2, ND, 8, 128), F32),
            pltpu.VMEM((2, ND, 8, 128), F32),
            pltpu.VMEM((ND, 8, 2 * F), F32),
            dma((4,)),
            dma((6,)),
            dma((GROUPS,)),
            dma((STEPS, LINKS)),
            dma((STEPS, LINKS)),
            dma((16,)),
            dma((16,)),
            dma((2, 4)),
            dma((8,)),
            dma((8,)),
        ],
        compiler_params=pltpu.CompilerParams(
            collective_id=0, has_side_effects=True, vmem_limit_bytes=VMEM
        ),
    )(
        layer_slowness, layer_rigidity, layer_damping, layer_of_level, live_count, target,
        fixed,
        slot_offset.reshape(Q, 128), slot_level.reshape(Q, 128), moduli, field_old, field_now,
    )

    final, copied = pl.pallas_call(
        last_kernel,
        out_shape=[block, block],
        in_specs=[vmem] + [any_space] * 7,
        out_specs=[any_space] * 2,
        scratch_shapes=[
            pltpu.VMEM((SHORT, NZ), BF),
            pltpu.VMEM((3, C + 4, C, NZ), BF),
            pltpu.VMEM(side.shape, BF),
            pltpu.VMEM(spread.shape, BF),
            pltpu.VMEM(block.shape, F32),
            pltpu.VMEM(block.shape, F32),
            pltpu.VMEM(moduli.shape, F32),
            pltpu.VMEM(block.shape, F32),
            dma((5,)),
            dma((3, GROUPS)),
            dma((2, GROUPS)),
        ],
        compiler_params=pltpu.CompilerParams(vmem_limit_bytes=VMEM),
    )(target, fixed, half, side, spread, last, prior, moduli)
    return final.reshape(whole), copied.reshape(whole)


def solution(mesh):
    in_specs = (
        P(),
        P(),
        P(),
        P(),
        P(),
        P(),
        P(("gx", "gy")),
        P(("gx", "gy")),
        P(None, "gx", "gy", None),
        P(None, "gx", "gy", None),
        P(None, "gx", "gy", None),
    )
    out_specs = (P(None, "gx", "gy", None), P(None, "gx", "gy", None))
    return jax.shard_map(shards, mesh=mesh, in_specs=in_specs, out_specs=out_specs, check_vma=False)
```

```python
import functools
import math

import jax
import jax.numpy as jnp
import ml_dtypes
import numpy as np
from jax import lax
from jax.experimental import pallas as pl
from jax.experimental.pallas import tpu as pltpu
from jax.sharding import PartitionSpec as P

F = 128
NK = 1024
NR = 2048
ND = 32
STEPS = 4
TSTART = 32
GX = 16
GY = 8
C = 32
NZ = 256
Q = 256
GROUPS = 8
XG = 4
ROWS = XG * C
TILES = 4
LINKS = 6 + 2 * TILES
ORDER = (6, 5, 7, 0, 4, 1, 2, 3)
ADDING = (7, 0, 6, 5, 4, 1, 2, 3)
VMEM = 63 * 1024 * 1024
MESH = pl.DeviceIdType.MESH
BF = jnp.bfloat16
F32 = jnp.float32


def constants():
    low, high = ROWS, ROWS + 16

    def place(x, y, half):
        if y < 0:
            return low + 8 * (y + 2) + x + XG * half
        if y >= C:
            return high + 8 * (y - C) + x + XG * half
        return x * C + y

    y2 = np.zeros((2, ROWS, ROWS + 32), np.float32)
    y1 = np.zeros((2, ROWS, ROWS + 32), np.float32)
    for half in range(2):
        for x in range(XG):
            for y in range(C):
                row = x * C + y
                for shift, factor in ((-2, -1.0), (-1, 16.0), (1, 16.0), (2, -1.0)):
                    y2[half, row, place(x, y + shift, half)] += factor
                y1[half, row, place(x, y + 1, half)] += 1.0
                y1[half, row, place(x, y - 1, half)] -= 1.0
    cross = np.zeros((4, ROWS, ROWS + 96), np.float32)
    for kind in range(4):
        half = kind // 2
        cross[kind, :, :ROWS] = 3.0 * y1[half, :, :ROWS]
        cross[kind, :, ROWS + 64 :] = 3.0 * y1[half, :, ROWS:]
        for x in range(XG):
            for y, beyond, sign in ((0, -1, -3.0), (C - 1, C, 3.0)):
                for step in (-1, 1):
                    if (half == 0 and x + step < 0) or (half == 1 and x + step >= XG):
                        spot = ROWS + (32 if beyond < 0 else 48)
                        if kind in (0, 3):
                            spot += 15 if beyond < 0 else 0
                        else:
                            spot += (8 if beyond < 0 else 0) + (7 if half == 0 else 0)
                    else:
                        spot = place(x + step, beyond, half)
                    cross[kind, x * C + y, spot] += sign * step
    z2 = np.zeros((NZ, NZ), np.float32)
    z1 = np.zeros((NZ, NZ), np.float32)
    for z in range(NZ):
        for shift, factor in ((-2, -1.0), (-1, 16.0), (1, 16.0), (2, -1.0)):
            if 0 <= z + shift < NZ:
                z2[z + shift, z] += factor
        if z + 1 < NZ:
            z1[z + 1, z] += 1.0
        if z > 0:
            z1[z - 1, z] -= 1.0
    period = 2 * F
    turns = (np.arange(F)[None, :] + 1) * (TSTART + np.arange(STEPS)[:, None]) % period
    angles = turns * (2.0 * math.pi / period)
    weight = 1.0 / math.sqrt(F)
    waves = np.concatenate([weight * np.cos(angles), -weight * np.sin(angles)], axis=1).T
    waves = np.repeat(waves.astype(np.float32), ND, axis=1)
    upper = waves.astype(ml_dtypes.bfloat16)
    lower = (waves - upper.astype(np.float32)).astype(ml_dtypes.bfloat16)
    half = ml_dtypes.bfloat16
    parts = [*y2, *y1, *cross, z2, z1, 3.0 * z1]
    parts = [np.pad(part, ((0, 0), (0, 256 - part.shape[1]))).astype(half) for part in parts]
    return np.concatenate(parts + [np.concatenate([upper, lower], axis=1)])


AT_Y2, AT_Y1, AT_CROSS, AT_Z2, AT_Z1, AT_Z3 = 0, 256, 512, 1024, 1280, 1536
AT_WAVES, TABLE = 1792, 2048
SHORT = AT_WAVES


def matrices(table, g):
    kind = jnp.where(g == 0, 0, jnp.where(g == GROUPS - 1, 3, 1 + g % 2))

    def part(at, k):
        return table[pl.ds(pl.multiple_of(at + ROWS * k, ROWS), ROWS)]

    return (
        part(AT_Y2, g % 2)[:, : ROWS + 32],
        part(AT_Y1, g % 2)[:, : ROWS + 32],
        part(AT_CROSS, kind),
        table[AT_Z2 : AT_Z2 + NZ],
        table[AT_Z1 : AT_Z1 + NZ],
        table[AT_Z3 : AT_Z3 + NZ],
    )


def halo_tiles(side, g):
    own = g // 2 + 1
    other = own - 1 + 2 * (g % 2)
    return (
        [side[0, own, c] for c in range(3)],
        [side[1, own, c] for c in range(3)],
        [side[0, other, c] for c in range(2)],
        [side[1, other, c] for c in range(2)],
    )


def rows_at(g):
    return pl.ds(pl.multiple_of(g * ROWS, ROWS), ROWS)


def group_at(i, order=ORDER):
    g = order[-1]
    for k in range(GROUPS - 1):
        g = jnp.where(i == k, order[k], g)
    return g


def dot(a, b):
    return jnp.dot(a, b, preferred_element_type=F32)


def beside(*parts):
    return jnp.concatenate(parts, axis=1)


def below(*parts):
    return jnp.concatenate(parts, axis=0)


def advance(window, lows, highs, clows, chighs, now, before, lam, mu, sources, y2, y1, cross, z2, z1, z3):
    wide = [w.astype(F32) for w in window]
    inner = [w[2 : 2 + XG].reshape(ROWS, NZ) for w in window]
    second = [(16.0 * (w[1:5] + w[3:7]) - (w[0:4] + w[4:8])).reshape(ROWS, NZ) for w in wide]
    first = [(w[3:7] - w[1:5]).reshape(ROWS, NZ) for w in wide]
    tall = [below(inner[c], lows[c], highs[c]) for c in range(3)]
    skew_z = dot(tall[2], z1)
    skew_y = dot(y1, tall[1])
    lap = [dot(beside(inner[c], y2), below(z2, tall[c])) for c in range(3)]
    mix_0 = dot(
        beside(first[2].astype(BF), cross[:, : ROWS + 64]),
        below(z3, first[1].astype(BF), lows[1], highs[1], clows[1], chighs[1]),
    )
    mix_1 = dot(
        beside(cross, y2),
        below(
            (first[0] + skew_z[:ROWS]).astype(BF), lows[0], highs[0], clows[0], chighs[0],
            skew_z[ROWS:].astype(BF), lows[0], highs[0], tall[1],
        ),
    )
    mix_2 = dot(beside(inner[2], (first[0] + skew_y).astype(BF)), below(z2, z3))
    couple = [second[0] + mix_0, mix_1, mix_2]
    shear = mu * (1.0 / 12.0)
    joint = (lam + mu) * (1.0 / 12.0)
    centre = 2.0 - 90.0 * shear - 30.0 * joint
    result = []
    for c in range(3):
        moved = shear * (second[c] + lap[c]) + joint * couple[c]
        if sources is not None:
            moved = moved + sources[c]
        result.append((centre * now[c] - before[c]) + moved)
    return result


def sine(x):
    y = x * x
    poly = -2.5052108e-08
    for coefficient in (2.7557319e-06, -1.9841270e-04, 8.3333333e-03, -1.6666667e-01, 1.0):
        poly = poly * y + coefficient
    return x * poly


def cosine(x):
    y = x * x
    poly = -2.7557319e-07
    for coefficient in (2.4801587e-05, -1.3888889e-03, 4.1666667e-02, -0.5, 1.0):
        poly = poly * y + coefficient
    return poly


def lane_spread(row):
    return jnp.transpose(jnp.broadcast_to(row.astype(F32), (128, 128))).astype(jnp.int32)


def main_kernel(
    slow_ref, rigid_ref, damp_ref, level_ref, live_ref, target_ref,
    table_hbm, offsets_hbm, levels_hbm, moduli_hbm, old_hbm, now_hbm,
    last_hbm, prior_hbm, half_hbm, side_hbm, spread_hbm,
    field, mod, half, side_out, side_in, hot, gathered, basis, spread,
    depth_hot, part_out, part_in,
    table, slot_tile, zbuf, ebuf, dbuf, kbuf,
    load_sem, store_sem, group_sem, send_sem, recv_sem, gsend_sem, grecv_sem,
    slot_sem, rsend_sem, rrecv_sem,
):
    gx = lax.axis_index("gx")
    gy = lax.axis_index("gy")
    device = gx * GY + gy
    px, pz = gx // 4, gx % 4
    py, core = gy // 2, gy % 2
    block = core * 64 + px * 16 + pz * 4 + py

    loads = [
        pltpu.make_async_copy(now_hbm, field.at[0], load_sem.at[0]),
        pltpu.make_async_copy(old_hbm, field.at[1], load_sem.at[1]),
        pltpu.make_async_copy(moduli_hbm, mod, load_sem.at[2]),
        pltpu.make_async_copy(table_hbm, table, load_sem.at[3]),
    ]
    slot_loads = []
    for x in range(4):
        at = pl.ds(pl.multiple_of(x * 64 + pz * 16 + py // 2 * 8, 8), 8)
        for k, ref in enumerate((offsets_hbm, levels_hbm)):
            slot_loads.append(pltpu.make_async_copy(ref.at[at], slot_tile.at[k, x], slot_sem.at[k, x]))
    for load in loads[:1] + slot_loads + loads[3:] + loads[1:3]:
        load.start()

    for p in range(2):
        half[p, :, 0:2] = jnp.zeros((3, 2, C, NZ), BF)
        half[p, :, C + 2 : C + 4] = jnp.zeros((3, 2, C, NZ), BF)
        for s in range(2):
            side_in[p, s] = jnp.zeros(side_in.shape[2:], BF)

    steps = [(1, 0), (-1, 0), (0, 1), (0, -1), (1, 1), (1, -1), (-1, 1), (-1, -1)]

    def exists(dx, dy):
        ok = None
        for delta, place, size in ((dx, gx, GX), (dy, gy, GY)):
            if delta == 1:
                part = place < size - 1
            elif delta == -1:
                part = place > 0
            else:
                continue
            ok = part if ok is None else jnp.logical_and(ok, part)
        return ok

    barrier = pltpu.get_barrier_semaphore()
    for dx, dy in steps:
        @pl.when(exists(dx, dy))
        def _():
            pl.semaphore_signal(barrier, inc=1, device_id=(gx + dx, gy + dy), device_id_type=MESH)

    def in_plane(k):
        return (px * 4 + (pz + k // 4) % 4, (py + k % 4) % 4 * 2 + core)

    def owner(k):
        return ((px + k // 2) % 4 * 4 + pz, py * 2 + (core + k) % 2)

    for k in range(1, 16):
        pl.semaphore_signal(barrier, inc=1, device_id=in_plane(k), device_id_type=MESH)
    for k in range(1, 8):
        pl.semaphore_signal(barrier, inc=1, device_id=owner(k), device_id_type=MESH)

    rows = lax.broadcasted_iota(jnp.int32, (8, 128), 0) + block * 8
    wavenum = (rows.astype(F32) + 0.5) * (4.0 / NK)
    square_k = wavenum * wavenum
    omega = (lax.broadcasted_iota(jnp.int32, (8, 128), 1) + 1).astype(F32) * (4.0 / F)

    def downward(i, carry):
        down_re, down_im = carry
        layer = level_ref[i]
        part = omega * slow_ref[layer]
        vertical = jnp.sqrt(square_k + part * part)
        fade = jnp.exp(vertical * (-0.25 * damp_ref[layer]))
        angle = 0.125 * vertical
        s, c = sine(angle), cosine(angle)
        leg_re = fade * (1.0 - 2.0 * s * s)
        leg_im = fade * (-2.0 * s * c)
        zbuf[i] = rigid_ref[layer] * vertical
        ebuf[0, i] = leg_re
        ebuf[1, i] = leg_im
        dbuf[0, i] = down_re
        dbuf[1, i] = down_im
        return down_re * leg_re - down_im * leg_im, down_re * leg_im + down_im * leg_re

    one = jnp.ones((8, 128), F32)
    zero = jnp.zeros((8, 128), F32)
    lax.fori_loop(0, ND, downward, (one, zero), unroll=8)
    zbuf[ND] = zbuf[ND - 1]

    def upward(step, carry):
        refl_re, refl_im = carry
        i = ND - 1 - step
        upper, under = zbuf[i], zbuf[i + 1]
        r = (upper - under) / (upper + under)
        leg_re, leg_im = ebuf[0, i], ebuf[1, i]
        trip_re = leg_re * leg_re - leg_im * leg_im
        trip_im = 2.0 * leg_re * leg_im
        upper_re = r + refl_re
        lower_re = 1.0 + r * refl_re
        lower_im = r * refl_im
        scale = 1.0 / (lower_re * lower_re + lower_im * lower_im)
        ratio_re = (upper_re * lower_re + refl_im * lower_im) * scale
        ratio_im = (refl_im * lower_re - upper_re * lower_im) * scale
        fresh_re = trip_re * ratio_re - trip_im * ratio_im
        fresh_im = trip_re * ratio_im + trip_im * ratio_re
        down_re, down_im = dbuf[0, i], dbuf[1, i]
        kbuf[i, :, 0:128] = (down_re * (1.0 + fresh_re) - down_im * fresh_im) * (1.0 / 32.0)
        kbuf[i, :, 128:256] = (down_re * fresh_im + down_im * (1.0 + fresh_re)) * (1.0 / 32.0)
        return fresh_re, fresh_im

    lax.fori_loop(0, ND, upward, (zero, zero), unroll=4)
    loads[3].wait()
    product = dot(kbuf[...].reshape(ND * 8, 2 * F).astype(BF), table[AT_WAVES : AT_WAVES + 2 * F])
    product = product[:, :128] + product[:, 128:]
    lane = lax.broadcasted_iota(jnp.int32, (8, 128), 1) % ND
    mine = zero
    for d in range(ND):
        mine = jnp.where(lane == d, product[8 * d : 8 * d + 8], mine)
    seat = pz * 4 + py
    gathered[seat] = mine

    count = 22
    for dx, dy in steps:
        count = count + exists(dx, dy).astype(jnp.int32)
    pl.semaphore_wait(barrier, count)

    gathers = [
        pltpu.make_async_remote_copy(
            src_ref=gathered.at[seat],
            dst_ref=gathered.at[seat],
            send_sem=gsend_sem.at[k],
            recv_sem=grecv_sem.at[k],
            device_id=in_plane(k),
            device_id_type=MESH,
        )
        for k in range(1, 16)
    ]
    for copy in gathers:
        copy.start()

    def send(n, move, source, target, index):
        copy = pltpu.make_async_remote_copy(
            src_ref=source,
            dst_ref=target,
            send_sem=send_sem.at[n, index],
            recv_sem=recv_sem.at[n, index],
            device_id=(gx + move[0], gy + move[1]),
            device_id_type=MESH,
        )
        return copy, exists(*move), exists(-move[0], -move[1])

    def message(n, index):
        p = n % 2
        if index < 2:
            move = (1, 0) if index == 0 else (-1, 0)
            source = half.at[p, :, pl.ds(C if index == 0 else 2, 2)]
            target = half.at[p, :, pl.ds(0 if index == 0 else C + 2, 2)]
        else:
            move = (1 if index < 4 else -1, 1 if index % 2 == 0 else -1)
            source = half.at[
                p, pl.ds(0, 2), C + 1 if move[0] == 1 else 2, pl.ds(16 if move[1] == 1 else 0, 16)
            ]
            target = side_in.at[p, 0 if move[1] == 1 else 1, 0 if move[0] == 1 else TILES + 1, pl.ds(0, 2)]
        return send(n, move, source, target, index)

    def tiles(n, k):
        return [
            send(
                n,
                (0, 1) if s == 0 else (0, -1),
                side_out.at[n % 2, s, k],
                side_in.at[n % 2, s, k + 1],
                6 + TILES * s + k,
            )
            for s in range(2)
        ]

    def start(messages):
        for copy, there, _ in messages:

            @pl.when(there)
            def _():
                copy.start()

    def arrive(messages):
        for copy, _, here in messages:

            @pl.when(here)
            def _():
                copy.wait_recv()

    def everything(n):
        return [message(n, index) for index in range(6)] + [one for k in range(TILES) for one in tiles(n, k)]

    def sent(n):
        for copy, there, _ in everything(n):

            @pl.when(there)
            def _():
                copy.wait_send()

    def fill(n, k):
        p = n % 2
        place = lax.broadcasted_iota(jnp.int32, (8, NZ), 0)
        for c in range(3):
            for s, y in ((0, C - 2), (1, 0)):
                rows = [jnp.zeros((8, NZ), F32)] * 2
                for x in range(8):
                    tile = field[p, c, pl.ds((8 * k + x) * C + y // 8 * 8, 8)]
                    for j in range(2):
                        line = jnp.broadcast_to(tile[y % 8 + j : y % 8 + j + 1], (8, NZ))
                        rows[j] = jnp.where(place == x, line, rows[j])
                side_out[p, s, k, c] = below(*rows).astype(BF)

    def publish(n, i, order=ORDER):
        @pl.when(i == order.index(GROUPS - 1))
        def _():
            start([message(n, index) for index in (0, 2, 3)])

        @pl.when(i == order.index(0))
        def _():
            start([message(n, index) for index in (1, 4, 5)])

        for k in range(TILES):

            @pl.when(i == max(order.index(2 * k), order.index(2 * k + 1)))
            def _():
                fill(n, k)
                start(tiles(n, k))

    def receive(n, i):
        @pl.when(i == ORDER.index(GROUPS - 1))
        def _():
            arrive([message(n, index) for index in (1, 4, 5)])

        @pl.when(i == ORDER.index(0))
        def _():
            arrive([message(n, index) for index in (0, 2, 3)])

        for k in range(TILES):
            readers = [g for g in range(2 * k - 1, 2 * k + 3) if 0 <= g < GROUPS]

            @pl.when(i == min(ORDER.index(g) for g in readers))
            def _():
                arrive(tiles(n, k))

    def update(n, g, sources):
        p = n % 2
        x = g * XG
        return advance(
            [half[p, c, pl.ds(x, XG + 4)] for c in range(3)],
            *halo_tiles(side_in.at[p], g),
            [field[p, c, rows_at(g)] for c in range(3)],
            [field[1 - p, c, rows_at(g)] for c in range(3)],
            mod[0, rows_at(g)],
            mod[1, rows_at(g)],
            sources,
            *matrices(table, g),
        )

    def injected(n, g):
        values = dot(hot[g].reshape(3 * ROWS, Q), spread[n])
        return [values[ROWS * c : ROWS * c + ROWS] for c in range(3)]

    def keep(n, g, c, fresh):
        field[n % 2, c, rows_at(g)] = fresh
        half[n % 2, c, pl.ds(g * XG + 2, XG)] = fresh.astype(BF).reshape(XG, C, NZ)

    def to_half(g, carry):
        x = g * XG
        for c in range(3):
            half[0, c, pl.ds(x + 2, XG)] = field[0, c, rows_at(g)].astype(BF).reshape(XG, C, NZ)
        return carry

    loads[0].wait()
    lax.fori_loop(0, GROUPS, to_half, 0)
    start([message(0, index) for index in range(6)])
    for k in range(TILES):
        fill(0, k)
        start(tiles(0, k))

    for load in slot_loads:
        load.wait()
    first_row = py % 2 * 4
    mask = NK * NR // 2 - 1
    across = lax.broadcasted_iota(jnp.int32, (128, 128), 1)
    along = lax.broadcasted_iota(jnp.int32, (128, 128), 0)
    odd_index = 2 * (along + (core * 4 + px) * 128) + 1

    def cosines(t, carry):
        q = slot_tile[0, t // 4, pl.ds(first_row + t % 4, 1)]
        turns = odd_index * q
        turns = ((turns + (mask + 1) // 2) & mask) - (mask + 1) // 2
        s = sine(turns.astype(F32) * (math.pi / (mask + 1)))
        basis[t] = (1.0 - 2.0 * s * s).astype(BF)
        return carry

    lax.fori_loop(0, 16, cosines, 0)
    returns = []
    for k in range(1, 8):
        to = (px + k // 2) % 4 * 2 + (core + k) % 2
        returns.append(
            pltpu.make_async_remote_copy(
                src_ref=part_out.at[to],
                dst_ref=part_in.at[k],
                send_sem=rsend_sem.at[k],
                recv_sem=rrecv_sem.at[k],
                device_id=owner(k),
                device_id_type=MESH,
            )
        )
    def build_hot(g, carry):
        ids = lax.broadcasted_iota(jnp.int32, (ROWS, Q), 0) + g * ROWS
        columns = target_ref[...] // NZ
        for c in range(3):
            same = ids + c * C * C == columns
            hot[g, c] = jnp.where(same, 1.0, 0.0).astype(BF)
        return carry

    lax.fori_loop(0, GROUPS, build_hot, 0)
    for h in range(2):
        depth = lane_spread(target_ref[:, 128 * h : 128 * h + 128] % NZ)
        for b in range(2):
            depth_hot[128 * h : 128 * h + 128, 128 * b : 128 * b + 128] = jnp.where(
                across + 128 * b == depth, 1.0, 0.0
            ).astype(BF)
    def sum_up():
        for copy in gathers:
            copy.wait()
        total = jnp.transpose(gathered[...].reshape(128, 128))
        upper = total.astype(BF)
        lower = (total - upper.astype(F32)).astype(BF)
        both = beside(upper, lower)

        def partial(u, carry):
            cos = beside(basis[2 * u], basis[2 * u + 1])
            sums = dot(both, below(cos, cos))
            row = first_row + u % 2 * 2
            level = beside(*[slot_tile[1, u // 2, pl.ds(row + h, 1)] for h in range(2)])
            depth = lax.broadcasted_iota(jnp.int32, (STEPS * ND, Q), 0) % ND
            sums = jnp.where(depth == level, sums, 0.0).reshape(STEPS, ND, Q)
            sums = jnp.sum(sums, axis=1)
            part_out[u] = below(sums[:, :128], sums[:, 128:])
            return carry

        lax.fori_loop(0, 8, partial, 0)
        for copy in returns:
            copy.start()

    loads[1].wait()
    loads[2].wait()

    def first_step(i, carry):
        receive(0, i)
        pl.when(i == 2)(sum_up)
        g = group_at(i)
        result = update(0, g, None)
        for c in range(3):
            field[1, c, rows_at(g)] = result[c]
        return carry

    lax.fori_loop(0, GROUPS, first_step, 0)
    for copy in returns:
        copy.wait()
    traces = part_out[px * 2 + core]
    for k in range(1, 8):
        traces = traces + part_in[k]
    slot = lax.broadcasted_iota(jnp.int32, (8, 128), 1) + lax.broadcasted_iota(jnp.int32, (8, 128), 0) // 4 * 128
    traces = jnp.where(slot < live_ref[0], traces, 0.0)
    for h in range(2):
        part = slice(128 * h, 128 * h + 128)
        for n in range(STEPS):
            line = jnp.broadcast_to(traces[4 * h + n : 4 * h + n + 1], (128, 128))
            diagonal = jnp.where(along == across, line, 0.0).astype(BF)
            spread[n, part] = dot(diagonal, depth_hot[part]).astype(BF)

    def first_sources(i, carry):
        g = group_at(i, ADDING)
        sources = injected(0, g)
        for c in range(3):
            keep(1, g, c, field[1, c, rows_at(g)] + sources[c])
        publish(1, i, ADDING)
        return carry

    lax.fori_loop(0, GROUPS, first_sources, 0)

    spread_store = pltpu.make_async_copy(spread.at[STEPS - 1], spread_hbm, store_sem.at[0])
    spread_store.start()
    prior_store = pltpu.make_async_copy(field.at[0], prior_hbm, store_sem.at[1])

    def last_stores(g):
        return [
            pltpu.make_async_copy(
                field.at[1, :, rows_at(g)], last_hbm.at[:, rows_at(g)], group_sem.at[g]
            )
        ]

    for n in range(1, STEPS - 1):
        sent(n - 1)
        if n == STEPS - 2:
            prior_store.start()

        def later_step(i, carry):
            receive(n, i)
            g = group_at(i)
            result = update(n, g, injected(n, g))
            for c in range(3):
                keep(n + 1, g, c, result[c])
            publish(n + 1, i)
            if n == STEPS - 2:
                for store in last_stores(g):
                    store.start()
            return carry

        lax.fori_loop(0, GROUPS, later_step, 0)

    last = STEPS - 1
    arrive([message(last, index) for index in (0, 1)])
    ends = [
        pltpu.make_async_copy(half.at[1, :, pl.ds(x, 2)], half_hbm.at[:, pl.ds(2 * k - 4, 2)], store_sem.at[k])
        for x, k in ((0, 2), (C + 2, 3))
    ]
    for store in ends:
        store.start()
    arrive(everything(last)[2:])
    side_store = pltpu.make_async_copy(side_in.at[1], side_hbm, store_sem.at[5])
    side_store.start()
    sent(last - 1)
    sent(last)
    for store in (spread_store, prior_store, *ends, side_store):
        store.wait()

    def drain(g, carry):
        for store in last_stores(g):
            store.wait()
        return carry

    lax.fori_loop(0, GROUPS, drain, 0)


def last_kernel(
    target_ref,
    table_hbm, half_hbm, side_hbm, spread_hbm, now_hbm, before_hbm, moduli_hbm,
    final_hbm, copy_hbm,
    table, half, side, spread, now, before, mod, final,
    sem, load_sem, store_sem,
):
    small = [
        pltpu.make_async_copy(source, target, sem.at[k])
        for k, (source, target) in enumerate(
            (
                (table_hbm.at[pl.ds(0, SHORT)], table),
                (spread_hbm, spread),
                (side_hbm, side),
                (half_hbm.at[:, pl.ds(0, 2)], half.at[:, pl.ds(0, 2)]),
                (half_hbm.at[:, pl.ds(2, 2)], half.at[:, pl.ds(C + 2, 2)]),
            )
        )
    ]

    def group_loads(g):
        part = rows_at(g)
        return [
            pltpu.make_async_copy(source.at[:, part], target.at[:, part], load_sem.at[k, g])
            for k, (source, target) in enumerate(
                ((now_hbm, now), (before_hbm, before), (moduli_hbm, mod))
            )
        ]

    def group_stores(g):
        part = rows_at(g)
        return [
            pltpu.make_async_copy(source.at[:, part], target.at[:, part], store_sem.at[k, g])
            for k, (source, target) in enumerate(((final, final_hbm), (now, copy_hbm)))
        ]

    for load in small:
        load.start()

    def begin_one(g, carry):
        for load in group_loads(g):
            load.start()
        return carry

    lax.fori_loop(0, GROUPS, begin_one, 0)
    for load in small:
        load.wait()

    def to_half(g):
        for load in group_loads(g):
            load.wait()
        for c in range(3):
            half[c, pl.ds(g * XG + 2, XG)] = now[c, rows_at(g)].astype(BF).reshape(XG, C, NZ)

    to_half(0)

    def group(g, carry):
        x = g * XG

        stores = group_stores(g)
        stores[1].start()

        @pl.when(g < GROUPS - 1)
        def _():
            to_half(g + 1)

        ids = lax.broadcasted_iota(jnp.int32, (ROWS, Q), 0) + g * ROWS
        columns = target_ref[...] // NZ
        hot = [jnp.where(ids + c * C * C == columns, 1.0, 0.0).astype(BF) for c in range(3)]
        values = dot(below(*hot), spread[...])
        result = advance(
            [half[c, pl.ds(x, XG + 4)] for c in range(3)],
            *halo_tiles(side, g),
            [now[c, rows_at(g)] for c in range(3)],
            [before[c, rows_at(g)] for c in range(3)],
            mod[0, rows_at(g)],
            mod[1, rows_at(g)],
            [values[ROWS * c : ROWS * c + ROWS] for c in range(3)],
            *matrices(table, g),
        )
        for c in range(3):
            final[c, rows_at(g)] = result[c]
        stores[0].start()
        return carry

    lax.fori_loop(0, GROUPS, group, 0)

    def drain(g, carry):
        for store in group_stores(g):
            store.wait()
        return carry

    lax.fori_loop(0, GROUPS, drain, 0)


def shards(
    layer_slowness, layer_rigidity, layer_damping, layer_of_level,
    slot_offset, slot_level, slot_target, live_count, moduli, field_old, field_now,
):
    fixed = jnp.asarray(constants())
    smem = pl.BlockSpec(memory_space=pltpu.SMEM)
    vmem = pl.BlockSpec(memory_space=pltpu.VMEM)
    any_space = pl.BlockSpec(memory_space=pl.ANY)
    target = slot_target.reshape(1, Q)
    block = jax.ShapeDtypeStruct((3, C * C, NZ), F32)
    whole = (3, C, C, NZ)
    moduli = moduli.reshape(2, C * C, NZ)
    field_old, field_now = field_old.reshape(block.shape), field_now.reshape(block.shape)
    dma = pltpu.SemaphoreType.DMA
    last, prior, half, side, spread = pl.pallas_call(
        main_kernel,
        out_shape=[
            block,
            block,
            jax.ShapeDtypeStruct((3, 4, C, NZ), BF),
            jax.ShapeDtypeStruct((2, TILES + 2, 3, 16, NZ), BF),
            jax.ShapeDtypeStruct((Q, NZ), BF),
        ],
        in_specs=[smem] * 5 + [vmem] + [any_space] * 6,
        out_specs=[any_space] * 5,
        scratch_shapes=[
            pltpu.VMEM((2, 3, C * C, NZ), F32),
            pltpu.VMEM((2, C * C, NZ), F32),
            pltpu.VMEM((2, 3, C + 4, C, NZ), BF),
            pltpu.VMEM((2, 2, TILES, 3, 16, NZ), BF),
            pltpu.VMEM((2, 2, TILES + 2, 3, 16, NZ), BF),
            pltpu.VMEM((GROUPS, 3, ROWS, Q), BF),
            pltpu.VMEM((16, 8, 128), F32),
            pltpu.VMEM((16, 128, 128), BF),
            pltpu.VMEM((STEPS, Q, NZ), BF),
            pltpu.VMEM((Q, NZ), BF),
            pltpu.VMEM((8, 8, 128), F32),
            pltpu.VMEM((8, 8, 128), F32),
            pltpu.VMEM((TABLE, NZ), BF),
            pltpu.VMEM((2, 4, 8, 128), jnp.int32),
            pltpu.VMEM((ND + 1, 8, 128), F32),
            pltpu.VMEM((2, ND, 8, 128), F32),
            pltpu.VMEM((2, ND, 8, 128), F32),
            pltpu.VMEM((ND, 8, 2 * F), F32),
            dma((4,)),
            dma((6,)),
            dma((GROUPS,)),
            dma((STEPS, LINKS)),
            dma((STEPS, LINKS)),
            dma((16,)),
            dma((16,)),
            dma((2, 4)),
            dma((8,)),
            dma((8,)),
        ],
        compiler_params=pltpu.CompilerParams(
            collective_id=0, has_side_effects=True, vmem_limit_bytes=VMEM
        ),
    )(
        layer_slowness, layer_rigidity, layer_damping, layer_of_level, live_count, target,
        fixed,
        slot_offset.reshape(Q, 128), slot_level.reshape(Q, 128), moduli, field_old, field_now,
    )

    final, copied = pl.pallas_call(
        last_kernel,
        out_shape=[block, block],
        in_specs=[vmem] + [any_space] * 7,
        out_specs=[any_space] * 2,
        scratch_shapes=[
            pltpu.VMEM((SHORT, NZ), BF),
            pltpu.VMEM((3, C + 4, C, NZ), BF),
            pltpu.VMEM(side.shape, BF),
            pltpu.VMEM(spread.shape, BF),
            pltpu.VMEM(block.shape, F32),
            pltpu.VMEM(block.shape, F32),
            pltpu.VMEM(moduli.shape, F32),
            pltpu.VMEM(block.shape, F32),
            dma((5,)),
            dma((3, GROUPS)),
            dma((2, GROUPS)),
        ],
        compiler_params=pltpu.CompilerParams(vmem_limit_bytes=VMEM),
    )(target, fixed, half, side, spread, last, prior, moduli)
    return final.reshape(whole), copied.reshape(whole)


def solution(mesh):
    in_specs = (
        P(),
        P(),
        P(),
        P(),
        P(),
        P(),
        P(("gx", "gy")),
        P(("gx", "gy")),
        P(None, "gx", "gy", None),
        P(None, "gx", "gy", None),
        P(None, "gx", "gy", None),
    )
    out_specs = (P(None, "gx", "gy", None), P(None, "gx", "gy", None))
    return jax.shard_map(shards, mesh=mesh, in_specs=in_specs, out_specs=out_specs, check_vma=False)
```

```python
import functools
import math

import jax
import jax.numpy as jnp
import ml_dtypes
import numpy as np
from jax import lax
from jax.experimental import pallas as pl
from jax.experimental.pallas import tpu as pltpu
from jax.sharding import PartitionSpec as P

F = 128
NK = 1024
NR = 2048
ND = 32
STEPS = 4
TSTART = 32
GX = 16
GY = 8
C = 32
NZ = 256
Q = 256
GROUPS = 8
XG = 4
ROWS = XG * C
TILES = 4
LINKS = 6 + 2 * TILES
ORDER = (6, 5, 7, 0, 4, 1, 2, 3)
ADDING = (7, 0, 6, 5, 4, 1, 2, 3)
VMEM = 63 * 1024 * 1024
MESH = pl.DeviceIdType.MESH
BF = jnp.bfloat16
F32 = jnp.float32


def constants():
    low, high = ROWS, ROWS + 16

    def place(x, y, half):
        if y < 0:
            return low + 8 * (y + 2) + x + XG * half
        if y >= C:
            return high + 8 * (y - C) + x + XG * half
        return x * C + y

    y2 = np.zeros((2, ROWS, ROWS + 32), np.float32)
    y1 = np.zeros((2, ROWS, ROWS + 32), np.float32)
    for half in range(2):
        for x in range(XG):
            for y in range(C):
                row = x * C + y
                for shift, factor in ((-2, -1.0), (-1, 16.0), (1, 16.0), (2, -1.0)):
                    y2[half, row, place(x, y + shift, half)] += factor
                y1[half, row, place(x, y + 1, half)] += 1.0
                y1[half, row, place(x, y - 1, half)] -= 1.0
    cross = np.zeros((4, ROWS, ROWS + 96), np.float32)
    for kind in range(4):
        half = kind // 2
        cross[kind, :, :ROWS] = 3.0 * y1[half, :, :ROWS]
        cross[kind, :, ROWS + 64 :] = 3.0 * y1[half, :, ROWS:]
        for x in range(XG):
            for y, beyond, sign in ((0, -1, -3.0), (C - 1, C, 3.0)):
                for step in (-1, 1):
                    if (half == 0 and x + step < 0) or (half == 1 and x + step >= XG):
                        spot = ROWS + (32 if beyond < 0 else 48)
                        if kind in (0, 3):
                            spot += 15 if beyond < 0 else 0
                        else:
                            spot += (8 if beyond < 0 else 0) + (7 if half == 0 else 0)
                    else:
                        spot = place(x + step, beyond, half)
                    cross[kind, x * C + y, spot] += sign * step
    z2 = np.zeros((NZ, NZ), np.float32)
    z1 = np.zeros((NZ, NZ), np.float32)
    for z in range(NZ):
        for shift, factor in ((-2, -1.0), (-1, 16.0), (1, 16.0), (2, -1.0)):
            if 0 <= z + shift < NZ:
                z2[z + shift, z] += factor
        if z + 1 < NZ:
            z1[z + 1, z] += 1.0
        if z > 0:
            z1[z - 1, z] -= 1.0
    period = 2 * F
    turns = (np.arange(F)[None, :] + 1) * (TSTART + np.arange(STEPS)[:, None]) % period
    angles = turns * (2.0 * math.pi / period)
    weight = 1.0 / math.sqrt(F)
    waves = np.concatenate([weight * np.cos(angles), -weight * np.sin(angles)], axis=1).T
    waves = np.repeat(waves.astype(np.float32), ND, axis=1)
    upper = waves.astype(ml_dtypes.bfloat16)
    lower = (waves - upper.astype(np.float32)).astype(ml_dtypes.bfloat16)
    half = ml_dtypes.bfloat16
    parts = [*y2, *y1, *cross, z2, z1, 3.0 * z1]
    parts = [np.pad(part, ((0, 0), (0, 256 - part.shape[1]))).astype(half) for part in parts]
    return np.concatenate(parts + [np.concatenate([upper, lower], axis=1)])


AT_Y2, AT_Y1, AT_CROSS, AT_Z2, AT_Z1, AT_Z3 = 0, 256, 512, 1024, 1280, 1536
AT_WAVES, TABLE = 1792, 2048
SHORT = AT_WAVES


def matrices(table, g):
    kind = jnp.where(g == 0, 0, jnp.where(g == GROUPS - 1, 3, 1 + g % 2))

    def part(at, k):
        return table[pl.ds(pl.multiple_of(at + ROWS * k, ROWS), ROWS)]

    return (
        part(AT_Y2, g % 2)[:, : ROWS + 32],
        part(AT_Y1, g % 2)[:, : ROWS + 32],
        part(AT_CROSS, kind),
        table[AT_Z2 : AT_Z2 + NZ],
        table[AT_Z1 : AT_Z1 + NZ],
        table[AT_Z3 : AT_Z3 + NZ],
    )


def halo_tiles(side, g):
    own = g // 2 + 1
    other = own - 1 + 2 * (g % 2)
    return (
        [side[0, own, c] for c in range(3)],
        [side[1, own, c] for c in range(3)],
        [side[0, other, c] for c in range(2)],
        [side[1, other, c] for c in range(2)],
    )


def rows_at(g):
    return pl.ds(pl.multiple_of(g * ROWS, ROWS), ROWS)


def group_at(i, order=ORDER):
    g = order[-1]
    for k in range(GROUPS - 1):
        g = jnp.where(i == k, order[k], g)
    return g


def dot(a, b):
    return jnp.dot(a, b, preferred_element_type=F32)


def beside(*parts):
    return jnp.concatenate(parts, axis=1)


def below(*parts):
    return jnp.concatenate(parts, axis=0)


def advance(window, lows, highs, clows, chighs, now, before, lam, mu, sources, y2, y1, cross, z2, z1, z3):
    wide = [w.astype(F32) for w in window]
    inner = [w[2 : 2 + XG].reshape(ROWS, NZ) for w in window]
    second = [(16.0 * (w[1:5] + w[3:7]) - (w[0:4] + w[4:8])).reshape(ROWS, NZ) for w in wide]
    first = [(w[3:7] - w[1:5]).reshape(ROWS, NZ) for w in wide]
    tall = [below(inner[c], lows[c], highs[c]) for c in range(3)]
    skew_z = dot(tall[2], z1)
    skew_y = dot(y1, tall[1])
    lap = [dot(beside(inner[c], y2), below(z2, tall[c])) for c in range(3)]
    mix_0 = dot(
        beside(first[2].astype(BF), cross[:, : ROWS + 64]),
        below(z3, first[1].astype(BF), lows[1], highs[1], clows[1], chighs[1]),
    )
    mix_1 = dot(
        beside(cross, y2),
        below(
            (first[0] + skew_z[:ROWS]).astype(BF), lows[0], highs[0], clows[0], chighs[0],
            skew_z[ROWS:].astype(BF), lows[0], highs[0], tall[1],
        ),
    )
    mix_2 = dot(beside(inner[2], (first[0] + skew_y).astype(BF)), below(z2, z3))
    couple = [second[0] + mix_0, mix_1, mix_2]
    shear = mu * (1.0 / 12.0)
    joint = (lam + mu) * (1.0 / 12.0)
    centre = 2.0 - 90.0 * shear - 30.0 * joint
    result = []
    for c in range(3):
        moved = shear * (second[c] + lap[c]) + joint * couple[c]
        if sources is not None:
            moved = moved + sources[c]
        result.append((centre * now[c] - before[c]) + moved)
    return result


def sine(x):
    y = x * x
    poly = -2.5052108e-08
    for coefficient in (2.7557319e-06, -1.9841270e-04, 8.3333333e-03, -1.6666667e-01, 1.0):
        poly = poly * y + coefficient
    return x * poly


def cosine(x):
    y = x * x
    poly = -2.7557319e-07
    for coefficient in (2.4801587e-05, -1.3888889e-03, 4.1666667e-02, -0.5, 1.0):
        poly = poly * y + coefficient
    return poly


def lane_spread(row):
    return jnp.transpose(jnp.broadcast_to(row.astype(F32), (128, 128))).astype(jnp.int32)


def main_kernel(
    slow_ref, rigid_ref, damp_ref, level_ref, live_ref, target_ref,
    table_hbm, offsets_hbm, levels_hbm, moduli_hbm, old_hbm, now_hbm,
    last_hbm, prior_hbm, half_hbm, side_hbm, spread_hbm,
    field, mod, half, side_out, side_in, hot, gathered, basis, spread,
    depth_hot, part_out, part_in,
    table, slot_tile, zbuf, ebuf, dbuf, kbuf,
    load_sem, store_sem, group_sem, send_sem, recv_sem, gsend_sem, grecv_sem,
    slot_sem, rsend_sem, rrecv_sem,
):
    gx = lax.axis_index("gx")
    gy = lax.axis_index("gy")
    device = gx * GY + gy
    px, pz = gx // 4, gx % 4
    py, core = gy // 2, gy % 2
    block = core * 64 + px * 16 + pz * 4 + py

    loads = [
        pltpu.make_async_copy(now_hbm, field.at[0], load_sem.at[0]),
        pltpu.make_async_copy(old_hbm, field.at[1], load_sem.at[1]),
        pltpu.make_async_copy(moduli_hbm, mod, load_sem.at[2]),
        pltpu.make_async_copy(table_hbm, table, load_sem.at[3]),
    ]
    slot_loads = []
    for x in range(4):
        at = pl.ds(pl.multiple_of(x * 64 + pz * 16 + py // 2 * 8, 8), 8)
        for k, ref in enumerate((offsets_hbm, levels_hbm)):
            slot_loads.append(pltpu.make_async_copy(ref.at[at], slot_tile.at[k, x], slot_sem.at[k, x]))
    for load in loads[:1] + slot_loads + loads[3:] + loads[1:3]:
        load.start()

    def outside(edge, *parts):
        @pl.when(edge)
        def _():
            for part in parts:
                part[...] = jnp.zeros(part.shape, BF)

    for p in range(2):
        outside(gx == 0, half.at[p, :, 0:2], side_in.at[p, 0, 0], side_in.at[p, 1, 0])
        outside(
            gx == GX - 1,
            half.at[p, :, C + 2 : C + 4], side_in.at[p, 0, TILES + 1], side_in.at[p, 1, TILES + 1],
        )
        outside(gy == 0, side_in.at[p, 0])
        outside(gy == GY - 1, side_in.at[p, 1])

    steps = [(1, 0), (-1, 0), (0, 1), (0, -1), (1, 1), (1, -1), (-1, 1), (-1, -1)]

    def exists(dx, dy):
        ok = None
        for delta, place, size in ((dx, gx, GX), (dy, gy, GY)):
            if delta == 1:
                part = place < size - 1
            elif delta == -1:
                part = place > 0
            else:
                continue
            ok = part if ok is None else jnp.logical_and(ok, part)
        return ok

    barrier = pltpu.get_barrier_semaphore()
    for dx, dy in steps:
        @pl.when(exists(dx, dy))
        def _():
            pl.semaphore_signal(barrier, inc=1, device_id=(gx + dx, gy + dy), device_id_type=MESH)

    def in_plane(k):
        return (px * 4 + (pz + k // 4) % 4, (py + k % 4) % 4 * 2 + core)

    def owner(k):
        return ((px + k // 2) % 4 * 4 + pz, py * 2 + (core + k) % 2)

    for k in range(1, 16):
        pl.semaphore_signal(barrier, inc=1, device_id=in_plane(k), device_id_type=MESH)
    for k in range(1, 8):
        pl.semaphore_signal(barrier, inc=1, device_id=owner(k), device_id_type=MESH)

    rows = lax.broadcasted_iota(jnp.int32, (8, 128), 0) + block * 8
    wavenum = (rows.astype(F32) + 0.5) * (4.0 / NK)
    square_k = wavenum * wavenum
    omega = (lax.broadcasted_iota(jnp.int32, (8, 128), 1) + 1).astype(F32) * (4.0 / F)

    def downward(i, carry):
        down_re, down_im = carry
        layer = level_ref[i]
        part = omega * slow_ref[layer]
        vertical = jnp.sqrt(square_k + part * part)
        fade = jnp.exp(vertical * (-0.25 * damp_ref[layer]))
        angle = 0.125 * vertical
        s, c = sine(angle), cosine(angle)
        leg_re = fade * (1.0 - 2.0 * s * s)
        leg_im = fade * (-2.0 * s * c)
        zbuf[i] = rigid_ref[layer] * vertical
        ebuf[0, i] = leg_re
        ebuf[1, i] = leg_im
        dbuf[0, i] = down_re
        dbuf[1, i] = down_im
        return down_re * leg_re - down_im * leg_im, down_re * leg_im + down_im * leg_re

    one = jnp.ones((8, 128), F32)
    zero = jnp.zeros((8, 128), F32)
    lax.fori_loop(0, ND, downward, (one, zero), unroll=8)
    zbuf[ND] = zbuf[ND - 1]

    def upward(block_id, carry):
        top_re, top_im = carry
        base_re, base_im = one, zero
        for k in range(8):
            i = ND - 1 - (8 * block_id + k)
            upper, under = zbuf[i], zbuf[i + 1]
            r = (upper - under) / (upper + under)
            leg_re, leg_im = ebuf[0, i], ebuf[1, i]
            trip_re = leg_re * leg_re - leg_im * leg_im
            trip_im = 2.0 * leg_re * leg_im
            num_re, num_im = r * base_re + top_re, r * base_im + top_im
            base_re, base_im = base_re + r * top_re, base_im + r * top_im
            top_re = trip_re * num_re - trip_im * num_im
            top_im = trip_re * num_im + trip_im * num_re
            scale = 1.0 / (base_re * base_re + base_im * base_im)
            fresh_re = (top_re * base_re + top_im * base_im) * scale
            fresh_im = (top_im * base_re - top_re * base_im) * scale
            down_re, down_im = dbuf[0, i], dbuf[1, i]
            kbuf[i, :, 0:128] = (down_re * (1.0 + fresh_re) - down_im * fresh_im) * (1.0 / 32.0)
            kbuf[i, :, 128:256] = (down_re * fresh_im + down_im * (1.0 + fresh_re)) * (1.0 / 32.0)
        return fresh_re, fresh_im

    lax.fori_loop(0, ND // 8, upward, (zero, zero))
    loads[3].wait()
    product = dot(kbuf[...].reshape(ND * 8, 2 * F).astype(BF), table[AT_WAVES : AT_WAVES + 2 * F])
    product = product[:, :128] + product[:, 128:]
    lane = lax.broadcasted_iota(jnp.int32, (8, 128), 1) % ND
    mine = zero
    for d in range(ND):
        mine = jnp.where(lane == d, product[8 * d : 8 * d + 8], mine)
    seat = pz * 4 + py
    gathered[seat] = mine

    count = 22
    for dx, dy in steps:
        count = count + exists(dx, dy).astype(jnp.int32)
    pl.semaphore_wait(barrier, count)

    gathers = [
        pltpu.make_async_remote_copy(
            src_ref=gathered.at[seat],
            dst_ref=gathered.at[seat],
            send_sem=gsend_sem.at[k],
            recv_sem=grecv_sem.at[k],
            device_id=in_plane(k),
            device_id_type=MESH,
        )
        for k in range(1, 16)
    ]
    for copy in gathers:
        copy.start()

    def send(n, move, source, target, index):
        copy = pltpu.make_async_remote_copy(
            src_ref=source,
            dst_ref=target,
            send_sem=send_sem.at[n, index],
            recv_sem=recv_sem.at[n, index],
            device_id=(gx + move[0], gy + move[1]),
            device_id_type=MESH,
        )
        return copy, exists(*move), exists(-move[0], -move[1])

    def message(n, index):
        p = n % 2
        if index < 2:
            move = (1, 0) if index == 0 else (-1, 0)
            source = half.at[p, :, pl.ds(C if index == 0 else 2, 2)]
            target = half.at[p, :, pl.ds(0 if index == 0 else C + 2, 2)]
        else:
            move = (1 if index < 4 else -1, 1 if index % 2 == 0 else -1)
            source = half.at[
                p, pl.ds(0, 2), C + 1 if move[0] == 1 else 2, pl.ds(16 if move[1] == 1 else 0, 16)
            ]
            target = side_in.at[p, 0 if move[1] == 1 else 1, 0 if move[0] == 1 else TILES + 1, pl.ds(0, 2)]
        return send(n, move, source, target, index)

    def tiles(n, k):
        return [
            send(
                n,
                (0, 1) if s == 0 else (0, -1),
                side_out.at[n % 2, s, k],
                side_in.at[n % 2, s, k + 1],
                6 + TILES * s + k,
            )
            for s in range(2)
        ]

    def start(messages):
        for copy, there, _ in messages:

            @pl.when(there)
            def _():
                copy.start()

    def arrive(messages):
        for copy, _, here in messages:

            @pl.when(here)
            def _():
                copy.wait_recv()

    def everything(n):
        return [message(n, index) for index in range(6)] + [one for k in range(TILES) for one in tiles(n, k)]

    def sent(n):
        for copy, there, _ in everything(n):

            @pl.when(there)
            def _():
                copy.wait_send()

    def fill(n, k):
        p = n % 2
        place = lax.broadcasted_iota(jnp.int32, (8, NZ), 0)
        for c in range(3):
            for s, y in ((0, C - 2), (1, 0)):
                rows = [jnp.zeros((8, NZ), F32)] * 2
                for x in range(8):
                    tile = field[p, c, pl.ds((8 * k + x) * C + y // 8 * 8, 8)]
                    for j in range(2):
                        line = jnp.broadcast_to(tile[y % 8 + j : y % 8 + j + 1], (8, NZ))
                        rows[j] = jnp.where(place == x, line, rows[j])
                side_out[p, s, k, c] = below(*rows).astype(BF)

    def publish(n, i, order=ORDER):
        @pl.when(i == order.index(GROUPS - 1))
        def _():
            start([message(n, index) for index in (0, 2, 3)])

        @pl.when(i == order.index(0))
        def _():
            start([message(n, index) for index in (1, 4, 5)])

        for k in range(TILES):

            @pl.when(i == max(order.index(2 * k), order.index(2 * k + 1)))
            def _():
                fill(n, k)
                start(tiles(n, k))

    def receive(n, i):
        @pl.when(i == ORDER.index(GROUPS - 1))
        def _():
            arrive([message(n, index) for index in (1, 4, 5)])

        @pl.when(i == ORDER.index(0))
        def _():
            arrive([message(n, index) for index in (0, 2, 3)])

        for k in range(TILES):
            readers = [g for g in range(2 * k - 1, 2 * k + 3) if 0 <= g < GROUPS]

            @pl.when(i == min(ORDER.index(g) for g in readers))
            def _():
                arrive(tiles(n, k))

    def update(n, g, sources):
        p = n % 2
        x = g * XG
        return advance(
            [half[p, c, pl.ds(x, XG + 4)] for c in range(3)],
            *halo_tiles(side_in.at[p], g),
            [field[p, c, rows_at(g)] for c in range(3)],
            [field[1 - p, c, rows_at(g)] for c in range(3)],
            mod[0, rows_at(g)],
            mod[1, rows_at(g)],
            sources,
            *matrices(table, g),
        )

    def injected(n, g):
        values = dot(hot[g].reshape(3 * ROWS, Q), spread[n])
        return [values[ROWS * c : ROWS * c + ROWS] for c in range(3)]

    def keep(n, g, c, fresh):
        field[n % 2, c, rows_at(g)] = fresh
        half[n % 2, c, pl.ds(g * XG + 2, XG)] = fresh.astype(BF).reshape(XG, C, NZ)

    def to_half(g, carry):
        x = g * XG
        for c in range(3):
            half[0, c, pl.ds(x + 2, XG)] = field[0, c, rows_at(g)].astype(BF).reshape(XG, C, NZ)
        return carry

    loads[0].wait()
    lax.fori_loop(0, GROUPS, to_half, 0)
    start([message(0, index) for index in range(6)])
    for k in range(TILES):
        fill(0, k)
        start(tiles(0, k))

    for load in slot_loads:
        load.wait()
    first_row = py % 2 * 4
    mask = NK * NR // 2 - 1
    across = lax.broadcasted_iota(jnp.int32, (128, 128), 1)
    along = lax.broadcasted_iota(jnp.int32, (128, 128), 0)
    odd_index = 2 * (along + (core * 4 + px) * 128) + 1

    def cosines(t, carry):
        q = slot_tile[0, t // 4, pl.ds(first_row + t % 4, 1)]
        turns = odd_index * q
        turns = ((turns + (mask + 1) // 2) & mask) - (mask + 1) // 2
        s = sine(turns.astype(F32) * (math.pi / (mask + 1)))
        basis[t] = (1.0 - 2.0 * s * s).astype(BF)
        return carry

    lax.fori_loop(0, 16, cosines, 0)
    returns = []
    for k in range(1, 8):
        to = (px + k // 2) % 4 * 2 + (core + k) % 2
        returns.append(
            pltpu.make_async_remote_copy(
                src_ref=part_out.at[to],
                dst_ref=part_in.at[k],
                send_sem=rsend_sem.at[k],
                recv_sem=rrecv_sem.at[k],
                device_id=owner(k),
                device_id_type=MESH,
            )
        )
    def build_hot(g, carry):
        ids = lax.broadcasted_iota(jnp.int32, (ROWS, Q), 0) + g * ROWS
        columns = target_ref[...] // NZ
        for c in range(3):
            same = ids + c * C * C == columns
            hot[g, c] = jnp.where(same, 1.0, 0.0).astype(BF)
        return carry

    lax.fori_loop(0, GROUPS, build_hot, 0)
    for h in range(2):
        depth = lane_spread(target_ref[:, 128 * h : 128 * h + 128] % NZ)
        for b in range(2):
            depth_hot[128 * h : 128 * h + 128, 128 * b : 128 * b + 128] = jnp.where(
                across + 128 * b == depth, 1.0, 0.0
            ).astype(BF)
    def sum_up():
        for copy in gathers:
            copy.wait()
        total = jnp.transpose(gathered[...].reshape(128, 128))
        upper = total.astype(BF)
        lower = (total - upper.astype(F32)).astype(BF)
        both = beside(upper, lower)

        def partial(u, carry):
            cos = beside(basis[2 * u], basis[2 * u + 1])
            sums = dot(both, below(cos, cos))
            row = first_row + u % 2 * 2
            level = beside(*[slot_tile[1, u // 2, pl.ds(row + h, 1)] for h in range(2)])
            depth = lax.broadcasted_iota(jnp.int32, (STEPS * ND, Q), 0) % ND
            sums = jnp.where(depth == level, sums, 0.0).reshape(STEPS, ND, Q)
            sums = jnp.sum(sums, axis=1)
            part_out[u] = below(sums[:, :128], sums[:, 128:])
            return carry

        lax.fori_loop(0, 8, partial, 0)
        for copy in returns:
            copy.start()

    loads[1].wait()
    loads[2].wait()

    def first_step(i, carry):
        receive(0, i)
        pl.when(i == 2)(sum_up)
        g = group_at(i)
        result = update(0, g, None)
        for c in range(3):
            field[1, c, rows_at(g)] = result[c]
        return carry

    lax.fori_loop(0, GROUPS, first_step, 0)
    for copy in returns:
        copy.wait()
    traces = part_out[px * 2 + core]
    for k in range(1, 8):
        traces = traces + part_in[k]
    slot = lax.broadcasted_iota(jnp.int32, (8, 128), 1) + lax.broadcasted_iota(jnp.int32, (8, 128), 0) // 4 * 128
    traces = jnp.where(slot < live_ref[0], traces, 0.0)
    for h in range(2):
        part = slice(128 * h, 128 * h + 128)
        for n in range(STEPS):
            line = jnp.broadcast_to(traces[4 * h + n : 4 * h + n + 1], (128, 128))
            diagonal = jnp.where(along == across, line, 0.0).astype(BF)
            spread[n, part] = dot(diagonal, depth_hot[part]).astype(BF)

    def first_sources(i, carry):
        g = group_at(i, ADDING)
        sources = injected(0, g)
        for c in range(3):
            keep(1, g, c, field[1, c, rows_at(g)] + sources[c])
        publish(1, i, ADDING)
        return carry

    lax.fori_loop(0, GROUPS, first_sources, 0)

    spread_store = pltpu.make_async_copy(spread.at[STEPS - 1], spread_hbm, store_sem.at[0])
    spread_store.start()
    prior_store = pltpu.make_async_copy(field.at[0], prior_hbm, store_sem.at[1])

    def last_stores(g):
        return [
            pltpu.make_async_copy(
                field.at[1, :, rows_at(g)], last_hbm.at[:, rows_at(g)], group_sem.at[g]
            )
        ]

    for n in range(1, STEPS - 1):
        sent(n - 1)
        if n == STEPS - 2:
            prior_store.start()

        def later_step(i, carry):
            receive(n, i)
            g = group_at(i)
            result = update(n, g, injected(n, g))
            for c in range(3):
                keep(n + 1, g, c, result[c])
            publish(n + 1, i)
            if n == STEPS - 2:
                for store in last_stores(g):
                    store.start()
            return carry

        lax.fori_loop(0, GROUPS, later_step, 0)

    last = STEPS - 1
    arrive([message(last, index) for index in (0, 1)])
    ends = [
        pltpu.make_async_copy(half.at[1, :, pl.ds(x, 2)], half_hbm.at[:, pl.ds(2 * k - 4, 2)], store_sem.at[k])
        for x, k in ((0, 2), (C + 2, 3))
    ]
    for store in ends:
        store.start()
    arrive(everything(last)[2:])
    side_store = pltpu.make_async_copy(side_in.at[1], side_hbm, store_sem.at[5])
    side_store.start()
    sent(last - 1)
    sent(last)
    for store in (spread_store, prior_store, *ends, side_store):
        store.wait()

    def drain(g, carry):
        for store in last_stores(g):
            store.wait()
        return carry

    lax.fori_loop(0, GROUPS, drain, 0)


def last_kernel(
    target_ref,
    table_hbm, half_hbm, side_hbm, spread_hbm, now_hbm, before_hbm, moduli_hbm,
    final_hbm, copy_hbm,
    table, half, side, spread, now, before, mod, final,
    sem, load_sem, store_sem,
):
    small = [
        pltpu.make_async_copy(source, target, sem.at[k])
        for k, (source, target) in enumerate(
            (
                (table_hbm.at[pl.ds(0, SHORT)], table),
                (spread_hbm, spread),
                (side_hbm, side),
                (half_hbm.at[:, pl.ds(0, 2)], half.at[:, pl.ds(0, 2)]),
                (half_hbm.at[:, pl.ds(2, 2)], half.at[:, pl.ds(C + 2, 2)]),
            )
        )
    ]

    def group_loads(g):
        part = rows_at(g)
        return [
            pltpu.make_async_copy(source.at[:, part], target.at[:, part], load_sem.at[k, g])
            for k, (source, target) in enumerate(
                ((now_hbm, now), (before_hbm, before), (moduli_hbm, mod))
            )
        ]

    def group_stores(g):
        part = rows_at(g)
        return [
            pltpu.make_async_copy(source.at[:, part], target.at[:, part], store_sem.at[k, g])
            for k, (source, target) in enumerate(((final, final_hbm), (now, copy_hbm)))
        ]

    for load in small:
        load.start()

    def begin_one(g, carry):
        for load in group_loads(g):
            load.start()
        return carry

    lax.fori_loop(0, GROUPS, begin_one, 0)
    for load in small:
        load.wait()

    def to_half(g):
        for load in group_loads(g):
            load.wait()
        for c in range(3):
            half[c, pl.ds(g * XG + 2, XG)] = now[c, rows_at(g)].astype(BF).reshape(XG, C, NZ)

    to_half(0)

    def group(g, carry):
        x = g * XG

        stores = group_stores(g)
        stores[1].start()

        @pl.when(g < GROUPS - 1)
        def _():
            to_half(g + 1)

        ids = lax.broadcasted_iota(jnp.int32, (ROWS, Q), 0) + g * ROWS
        columns = target_ref[...] // NZ
        hot = [jnp.where(ids + c * C * C == columns, 1.0, 0.0).astype(BF) for c in range(3)]
        values = dot(below(*hot), spread[...])
        result = advance(
            [half[c, pl.ds(x, XG + 4)] for c in range(3)],
            *halo_tiles(side, g),
            [now[c, rows_at(g)] for c in range(3)],
            [before[c, rows_at(g)] for c in range(3)],
            mod[0, rows_at(g)],
            mod[1, rows_at(g)],
            [values[ROWS * c : ROWS * c + ROWS] for c in range(3)],
            *matrices(table, g),
        )
        for c in range(3):
            final[c, rows_at(g)] = result[c]
        stores[0].start()
        return carry

    lax.fori_loop(0, GROUPS, group, 0)

    def drain(g, carry):
        for store in group_stores(g):
            store.wait()
        return carry

    lax.fori_loop(0, GROUPS, drain, 0)


def shards(
    layer_slowness, layer_rigidity, layer_damping, layer_of_level,
    slot_offset, slot_level, slot_target, live_count, moduli, field_old, field_now,
):
    fixed = jnp.asarray(constants())
    smem = pl.BlockSpec(memory_space=pltpu.SMEM)
    vmem = pl.BlockSpec(memory_space=pltpu.VMEM)
    any_space = pl.BlockSpec(memory_space=pl.ANY)
    target = slot_target.reshape(1, Q)
    block = jax.ShapeDtypeStruct((3, C * C, NZ), F32)
    whole = (3, C, C, NZ)
    moduli = moduli.reshape(2, C * C, NZ)
    field_old, field_now = field_old.reshape(block.shape), field_now.reshape(block.shape)
    dma = pltpu.SemaphoreType.DMA
    last, prior, half, side, spread = pl.pallas_call(
        main_kernel,
        out_shape=[
            block,
            block,
            jax.ShapeDtypeStruct((3, 4, C, NZ), BF),
            jax.ShapeDtypeStruct((2, TILES + 2, 3, 16, NZ), BF),
            jax.ShapeDtypeStruct((Q, NZ), BF),
        ],
        in_specs=[smem] * 5 + [vmem] + [any_space] * 6,
        out_specs=[any_space] * 5,
        scratch_shapes=[
            pltpu.VMEM((2, 3, C * C, NZ), F32),
            pltpu.VMEM((2, C * C, NZ), F32),
            pltpu.VMEM((2, 3, C + 4, C, NZ), BF),
            pltpu.VMEM((2, 2, TILES, 3, 16, NZ), BF),
            pltpu.VMEM((2, 2, TILES + 2, 3, 16, NZ), BF),
            pltpu.VMEM((GROUPS, 3, ROWS, Q), BF),
            pltpu.VMEM((16, 8, 128), F32),
            pltpu.VMEM((16, 128, 128), BF),
            pltpu.VMEM((STEPS, Q, NZ), BF),
            pltpu.VMEM((Q, NZ), BF),
            pltpu.VMEM((8, 8, 128), F32),
            pltpu.VMEM((8, 8, 128), F32),
            pltpu.VMEM((TABLE, NZ), BF),
            pltpu.VMEM((2, 4, 8, 128), jnp.int32),
            pltpu.VMEM((ND + 1, 8, 128), F32),
            pltpu.VMEM((2, ND, 8, 128), F32),
            pltpu.VMEM((2, ND, 8, 128), F32),
            pltpu.VMEM((ND, 8, 2 * F), F32),
            dma((4,)),
            dma((6,)),
            dma((GROUPS,)),
            dma((STEPS, LINKS)),
            dma((STEPS, LINKS)),
            dma((16,)),
            dma((16,)),
            dma((2, 4)),
            dma((8,)),
            dma((8,)),
        ],
        compiler_params=pltpu.CompilerParams(
            collective_id=0, has_side_effects=True, vmem_limit_bytes=VMEM
        ),
    )(
        layer_slowness, layer_rigidity, layer_damping, layer_of_level, live_count, target,
        fixed,
        slot_offset.reshape(Q, 128), slot_level.reshape(Q, 128), moduli, field_old, field_now,
    )

    final, copied = pl.pallas_call(
        last_kernel,
        out_shape=[block, block],
        in_specs=[vmem] + [any_space] * 7,
        out_specs=[any_space] * 2,
        scratch_shapes=[
            pltpu.VMEM((SHORT, NZ), BF),
            pltpu.VMEM((3, C + 4, C, NZ), BF),
            pltpu.VMEM(side.shape, BF),
            pltpu.VMEM(spread.shape, BF),
            pltpu.VMEM(block.shape, F32),
            pltpu.VMEM(block.shape, F32),
            pltpu.VMEM(moduli.shape, F32),
            pltpu.VMEM(block.shape, F32),
            dma((5,)),
            dma((3, GROUPS)),
            dma((2, GROUPS)),
        ],
        compiler_params=pltpu.CompilerParams(vmem_limit_bytes=VMEM),
    )(target, fixed, half, side, spread, last, prior, moduli)
    return final.reshape(whole), copied.reshape(whole)


def solution(mesh):
    in_specs = (
        P(),
        P(),
        P(),
        P(),
        P(),
        P(),
        P(("gx", "gy")),
        P(("gx", "gy")),
        P(None, "gx", "gy", None),
        P(None, "gx", "gy", None),
        P(None, "gx", "gy", None),
    )
    out_specs = (P(None, "gx", "gy", None), P(None, "gx", "gy", None))
    return jax.shard_map(shards, mesh=mesh, in_specs=in_specs, out_specs=out_specs, check_vma=False)
```
